32 devices in a mesh: seq: 4 (over y, x), fsdp: 8 (over z, core).
Axes of the slice: x: 2, y: 2, z: 4, core: 2. Of those that a mesh axis runs over, the one named last changes fastest.
Arguments:
- tokens: bfloat16 [8192, 2048], P(('fsdp', 'seq')), may hold values from -6 to 6
- seq_lengths: int32 [8, 3], P('fsdp'), may hold values from 1 to 1022, as said below
- pic_starts: int32 [8, 2], P('fsdp'), may hold values from 0 to 768, as said below
- pic_lengths: int32 [8, 2], P('fsdp'), may hold values from 64 to 256, as said below
- norm1_gain: bfloat16 [2048], P(('seq', 'fsdp')), may hold values from 0.5 to 1.5
- w_query: bfloat16 [2048, 2048], P(('seq', 'fsdp')), may hold values from -0.125 to 0.125
- w_key: bfloat16 [2048, 1024], P(('seq', 'fsdp')), may hold values from -0.125 to 0.125
- w_value: bfloat16 [2048, 1024], P(('seq', 'fsdp')), may hold values from -0.125 to 0.125
- q_gain: bfloat16 [128], P(('seq', 'fsdp')), may hold values from 0.099609375 to 1.8984375
- k_gain: bfloat16 [128], P(('seq', 'fsdp')), may hold values from 0.099609375 to 1.8984375
- w_out: bfloat16 [2048, 2048], P(('seq', 'fsdp')), may hold values from -2 to 2
- norm2_gain: bfloat16 [2048], P(('seq', 'fsdp')), may hold values from 0.5 to 1.5
- w_gate: bfloat16 [2048, 6144], P(('seq', 'fsdp')), may hold values from -0.125 to 0.125
- w_up: bfloat16 [2048, 6144], P(('seq', 'fsdp')), may hold values from -0.125 to 0.125
- w_down: bfloat16 [6144, 2048], P(None, ('seq', 'fsdp')), may hold values from -0.625 to 0.625
- cotangent: bfloat16 [8192, 2048], P(('fsdp', 'seq')), may hold values from -6 to 6
Outputs:
- output: bfloat16 [8192, 2048], P(('fsdp', 'seq'))
- input_grad: bfloat16 [8192, 2048], P(('fsdp', 'seq'))
- norm1_gain_grad: float32 [2048], P(('seq', 'fsdp'))
- w_query_grad: float32 [2048, 2048], P(('seq', 'fsdp'))
- w_key_grad: float32 [2048, 1024], P(('seq', 'fsdp'))
- w_value_grad: float32 [2048, 1024], P(('seq', 'fsdp'))
- q_gain_grad: float32 [128], P(('seq', 'fsdp'))
- k_gain_grad: float32 [128], P(('seq', 'fsdp'))
- w_out_grad: float32 [2048, 2048], P(('seq', 'fsdp'))
- norm2_gain_grad: float32 [2048], P(('seq', 'fsdp'))
- w_gate_grad: float32 [2048, 6144], P(('seq', 'fsdp'))
- w_up_grad: float32 [2048, 6144], P(('seq', 'fsdp'))
- w_down_grad: float32 [6144, 2048], P(None, ('seq', 'fsdp'))
The draws below stay inside these ranges and needn't reach their ends.
Inputs may be any that keep to these rules, and one draw needn't show every extreme that they name: `seq_lengths`: each group's three lengths sum to 1024; the first and the last have 1 to 32 tokens; in some group both of these have 1. `pic_starts`: picture i of a group starts at a place from 2 i * 256 to 2 i * 256 + 256; pictures don't intersect; in some group the first picture starts at 0 and the last at 768. `pic_lengths`: in every group one picture has exactly 256 tokens.
All inputs are finite; a program needn't handle non-finite values.
Results may differ from the reference program's by a relative error of at most 0.025.
Values may be sent and summed in bfloat16 or wider, within the bound.
A program may use at most 640 MiB of HBM per device.

```python
import jax
import jax.numpy as jnp
from jax import lax

D = 2048
HQ = 16
KV = 8
HD = 128
FF = 6144
TOK_DEV = 256
PIECE = 256
TOKENS = 8192
N_SEQ = 4
N_FSDP = 8


def picture_layout(key):
    slot_count = TOK_DEV * N_SEQ // (2 * PIECE)
    offset_key, size_key, chosen_key, edge_key = jax.random.split(key, 4)
    offsets = jax.random.randint(offset_key, (N_FSDP, slot_count), 0, PIECE + 1)
    sizes = jax.random.randint(size_key, (N_FSDP, slot_count), PIECE // 4, PIECE + 1)
    chosen = jax.random.randint(chosen_key, (N_FSDP, 1), 0, slot_count)
    sizes = jnp.where(jnp.arange(slot_count)[None, :] == chosen, PIECE, sizes)
    edge_group = jax.random.randint(edge_key, (), 0, N_FSDP)
    rows = jnp.arange(N_FSDP)[:, None]
    cols = jnp.arange(slot_count)[None, :]
    offsets = jnp.where((rows == edge_group) & (cols == 0), 0, offsets)
    offsets = jnp.where((rows == edge_group) & (cols == slot_count - 1), PIECE, offsets)
    begins = cols * (2 * PIECE) + offsets
    return (begins.astype(jnp.int32), sizes.astype(jnp.int32))


def draw_seq_lengths(key, part):
    key = jax.random.fold_in(key, 11)
    edge_key, group_key = jax.random.split(key)
    edges = jax.random.randint(edge_key, (N_FSDP, 2), 1, TOK_DEV // 8 + 1)
    short_group = jax.random.randint(group_key, (), 0, N_FSDP)
    edges = jnp.where(jnp.arange(N_FSDP)[:, None] == short_group, 1, edges)
    middle = TOK_DEV * N_SEQ - edges[:, 0] - edges[:, 1]
    return jnp.stack([edges[:, 0], middle, edges[:, 1]], axis=1).astype(jnp.int32)


def draw_pic_starts(key, part):
    begins, sizes = picture_layout(key)
    return begins


def draw_pic_lengths(key, part):
    begins, sizes = picture_layout(key)
    return sizes


def with_spikes(array, own_key, source, target, shards_of, factor):
    owner, partner = [(jnp.arange(array.shape[axis_at]) // (array.shape[axis_at] // shards_of)).reshape([-1 if axis == axis_at else 1 for axis in range(array.ndim)]) for axis_at in (source, target)]
    chosen = jax.random.permutation(own_key, shards_of)[partner]
    strong = (owner == chosen) | (owner == (partner + shards_of // 2) % shards_of)
    return jnp.where(strong, factor * array, array)


def shard_levels(stream_key, dims, pieces, low, high):
    def one(dim, parts):
        heights = jax.random.uniform(jax.random.fold_in(jax.random.fold_in(stream_key, 6), dim), (parts,), jnp.float32, low / len(pieces), high / len(pieces))
        return jnp.repeat(jnp.exp(heights), dims[dim] // parts).reshape((-1,) + (1,) * (len(dims) - dim - 1))

    loudness = one(*pieces[0])
    for cut in pieces[1:]:
        loudness = loudness * one(*cut)
    return loudness


def scatter_about(rng, dims, deviation, limit, pieces=(), kind=jnp.bfloat16):
    level = shard_levels(rng, dims, pieces, -0.22, 0.18) if pieces else 1.0
    values = jax.random.normal(rng, dims, jnp.float32) * deviation * level
    return jnp.minimum(jnp.maximum(values, -limit), limit).astype(kind)


def noise_with(stream_key, dims, scale, most, cuts, heavy, held_as=jnp.bfloat16):
    entries = scale * jax.random.normal(stream_key, dims, jnp.float32)
    if cuts:
        entries = entries * shard_levels(stream_key, dims, cuts, -0.22, 0.18)
    return jnp.clip(with_spikes(entries, jax.random.fold_in(stream_key, 3), *heavy), -most, most).astype(held_as)


def setup_inputs(seed: int = 0) -> dict:
    splits = jax.random.split(jax.random.key(seed), 17)
    return {
        "tokens": scatter_about(splits[0], (TOKENS, D), 1.0, 6.0, ((0, 32),)),
        "seq_lengths": draw_seq_lengths(jax.random.fold_in(splits[16], 71), 0),
        "pic_starts": draw_pic_starts(jax.random.fold_in(splits[16], 71), 0),
        "pic_lengths": draw_pic_lengths(jax.random.fold_in(splits[16], 71), 0),
        "norm1_gain": jnp.clip(1.0 + 0.1 * jax.random.normal(splits[4], (D,), jnp.float32), 0.5, 1.5).astype(jnp.bfloat16),
        "w_query": scatter_about(splits[5], (D, HQ * HD), D ** -0.5, 0.125, ((0, 32),)),
        "w_key": scatter_about(splits[6], (D, KV * HD), D ** -0.5, 0.125, ((0, 32),)),
        "w_value": scatter_about(splits[7], (D, KV * HD), D ** -0.5, 0.125, ((0, 32),)),
        "q_gain": jnp.clip(1.0 + 0.18 * jax.random.normal(splits[8], (HD,), jnp.float32), 0.099609375, 1.8984375).astype(jnp.bfloat16),
        "k_gain": jnp.clip(1.0 + 0.18 * jax.random.normal(splits[9], (HD,), jnp.float32), 0.099609375, 1.8984375).astype(jnp.bfloat16),
        "w_out": scatter_about(splits[10], (HQ * HD, D), (max(HQ * HD // 256, 1)) ** -0.5, 2.0, ((0, 32),)),
        "norm2_gain": jnp.clip(1.0 + 0.1 * jax.random.normal(splits[11], (D,), jnp.float32), 0.5, 1.5).astype(jnp.bfloat16),
        "w_gate": scatter_about(splits[12], (D, FF), D ** -0.5, 0.125, ((0, 32),)),
        "w_up": scatter_about(splits[13], (D, FF), D ** -0.5, 0.125, ((0, 32),)),
        "w_down": noise_with(splits[14], (FF, D), (max(FF // 16, 1)) ** -0.5, 0.625, ((1, 32),), (0, 1, 32, 2.75)),
        "cotangent": scatter_about(splits[15], (TOKENS, D), 1.0, 6.0, ((0, 32),)),
    }


epsilon = 1e-06
theta = 1000000.0
masked_score = -1e+30

@jax.custom_vjp
def low(v):
    return lax.optimization_barrier(v.astype(jnp.bfloat16)).astype(jnp.float32)

@jax.custom_vjp
def low_back(v):
    return v

def low_keep(v):
    return (low(v), None)

def low_pass(kept, grad):
    return (grad,)

def back_keep(v):
    return (v, None)

def back_low(kept, grad):
    return (low(grad),)
low.defvjp(low_keep, low_pass)
low_back.defvjp(back_keep, back_low)

def product(left_rows, right_rows):
    return jnp.dot(left_rows, right_rows, precision=lax.Precision.HIGHEST, preferred_element_type=jnp.float32)

def normalize(values):
    return values * lax.rsqrt(lax.optimization_barrier(jnp.mean(values * values, axis=-1, keepdims=True)) + epsilon)

def rotate(values, position):
    half_size = values.shape[-1] // 2
    frequency = jnp.float32(theta) ** (-(jnp.arange(half_size, dtype=jnp.float32) * 2.0 / values.shape[-1]))
    angles = position.astype(jnp.float32)[:, None] * frequency[None, :]
    cosine = jnp.cos(angles)[:, None, :]
    sine_part = jnp.sin(angles)[:, None, :]
    leading = values[..., :half_size]
    trailing = values[..., half_size:]
    return jnp.concatenate([leading * cosine - trailing * sine_part, trailing * cosine + leading * sine_part], axis=-1)

def head_prep(values, gain, position):
    row_count = values.shape[0]
    shaped = values.reshape(row_count, -1, gain.shape[0])
    return rotate(normalize(shaped) * gain, position).reshape(row_count, -1)

def layout(lengths, starts, sizes, places):
    border_one = lengths[0]
    border_two = border_one + lengths[1]
    member = (places >= border_one).astype(jnp.int32) + (places >= border_two).astype(jnp.int32)
    begins = jnp.where(member == 0, 0, jnp.where(member == 1, border_one, border_two)).astype(jnp.int32)
    inside = (places[:, None] >= starts[None, :]) & (places[:, None] < starts[None, :] + sizes[None, :])
    numbers = jnp.arange(1, starts.shape[0] + 1, dtype=jnp.int32)
    label = lax.optimization_barrier(jnp.sum(jnp.where(inside, numbers[None, :], 0), axis=1)).astype(jnp.int32) - 1
    return (member, (places - begins).astype(jnp.int32), label)

def visible(query_member, query_place, query_label, key_member, key_place, key_label):
    same_sequence = query_member[:, None] == key_member[None, :]
    causal = query_place[:, None] >= key_place[None, :]
    picture = (query_label[:, None] == key_label[None, :]) & (query_label[:, None] >= 0)
    return same_sequence & (causal | picture)

def attend(query_r, key_r, valued, allowed):
    row_count = query_r.shape[0]
    group_ratio = HQ // KV
    query_heads = query_r.reshape(row_count, KV, group_ratio, HD).transpose(1, 0, 2, 3)
    key_heads = key_r.reshape(row_count, KV, HD).transpose(1, 0, 2)
    value_heads = valued.reshape(row_count, KV, HD).transpose(1, 0, 2)

    def one_head(items):
        query_head, key_head, value_head = items
        scores = low_back(HD ** (-0.5) * jnp.einsum('trd,kd->trk', query_head, key_head, precision=lax.Precision.HIGHEST))
        scores = jnp.where(allowed[:, None, :], scores, masked_score)
        highest = lax.optimization_barrier(jnp.max(scores, axis=-1, keepdims=True))
        log_total = highest + jnp.log(lax.optimization_barrier(jnp.sum(jnp.exp(scores - highest), axis=-1, keepdims=True)))
        softmax_weights = jnp.exp(scores - log_total)
        return jnp.einsum('trk,kd->trd', low(softmax_weights), value_head, precision=lax.Precision.HIGHEST)
    mixed = lax.map(jax.checkpoint(one_head), (query_heads, key_heads, value_heads))
    return mixed.transpose(1, 0, 2, 3).reshape(row_count, HQ * HD)

def forward_group(inputs, params, member, position, label):
    gain_one, query_weight, key_weight, value_weight, query_gain, key_gain, out_weight, gain_two, gate_weight, up_weight, down_weight = params
    normed_one = low(normalize(inputs) * gain_one)
    query_raw = low_back(product(normed_one, query_weight))
    key_raw = low_back(product(normed_one, key_weight))
    valued = low(low_back(product(normed_one, value_weight)))
    query_r = low(head_prep(query_raw, query_gain, position))
    key_r = low(head_prep(key_raw, key_gain, position))
    places = jnp.arange(inputs.shape[0], dtype=jnp.int32)
    allowed = visible(member, places, label, member, places, label)
    mixed = low(low_back(attend(query_r, key_r, valued, allowed)))
    middle = inputs + low_back(product(mixed, out_weight))
    normed_two = low(normalize(middle) * gain_two)
    gate = low_back(product(normed_two, gate_weight))
    up_part = low_back(product(normed_two, up_weight))
    hidden = low(jax.nn.silu(gate) * up_part)
    return middle + low_back(product(hidden, down_weight))

def reference(tokens, seq_lengths, pic_starts, pic_lengths, norm1_gain, w_query, w_key, w_value, q_gain, k_gain, w_out, norm2_gain, w_gate, w_up, w_down, cotangent):
    group_rows = TOK_DEV * N_SEQ
    params = tuple((matrix.astype(jnp.float32) for matrix in (norm1_gain, w_query, w_key, w_value, q_gain, k_gain, w_out, norm2_gain, w_gate, w_up, w_down)))
    places = jnp.arange(group_rows, dtype=jnp.int32)
    member, position, label = jax.vmap(lambda lengths_row, starts_row, sizes_row: layout(lengths_row, starts_row, sizes_row, places))(seq_lengths, pic_starts, pic_lengths)
    inputs = tokens.astype(jnp.float32).reshape(N_FSDP, group_rows, D)
    grads_in = cotangent.astype(jnp.float32).reshape(N_FSDP, group_rows, D)

    def step(carry, items):
        block_in, block_grad, block_member, block_position, block_label = items

        def forward(values, *weights_in):
            return forward_group(values, weights_in, block_member, block_position, block_label)
        result, pull = jax.vjp(forward, block_in, *params)
        pulled = pull(block_grad)
        carry = tuple((earlier + later for earlier, later in zip(carry, pulled[1:])))
        return (carry, (result, pulled[0]))
    zeros_init = tuple((jnp.zeros_like(matrix) for matrix in params))
    sums, (results, input_grads) = lax.scan(step, zeros_init, (inputs, grads_in, member, position, label))
    return (results.reshape(TOKENS, D).astype(jnp.bfloat16), input_grads.reshape(TOKENS, D).astype(jnp.bfloat16), sums[0], sums[1], sums[2], sums[3], sums[4], sums[5], sums[6], sums[7], sums[8], sums[9], sums[10])
```

```python
import functools

import jax
import jax.numpy as jnp
from jax import lax
from jax.experimental import pallas as pl
from jax.experimental.pallas import tpu as pltpu
from jax.sharding import PartitionSpec as P

epsilon = 1e-06
theta = 1000000.0
masked_score = -1e30
log2e = 1.4426950408889634

MESH = pl.DeviceIdType.MESH
ANY = pl.BlockSpec(memory_space=pl.ANY)
VMEM = pl.BlockSpec(memory_space=pltpu.VMEM)
BF = jnp.bfloat16
F32 = jnp.float32
LIMIT = 60 * 1024 * 1024


def dot(a, b):
    return jnp.dot(a, b, preferred_element_type=F32)


def dot_nt(a, b):
    return lax.dot_general(a, b, (((1,), (1,)), ((), ())), preferred_element_type=F32)


def dot_tn(a, b):
    return lax.dot_general(a, b, (((0,), (0,)), ((), ())), preferred_element_type=F32)


def shape(dims, dtype):
    return jax.ShapeDtypeStruct(dims, dtype)


def comm_params(number):
    return pltpu.CompilerParams(
        collective_id=number, has_side_effects=True, vmem_limit_bytes=LIMIT
    )


def plain_params():
    return pltpu.CompilerParams(vmem_limit_bytes=LIMIT)


def remote(src, dst, send, recv, axis, index):
    return pltpu.make_async_remote_copy(
        src_ref=src,
        dst_ref=dst,
        send_sem=send,
        recv_sem=recv,
        device_id={axis: index},
        device_id_type=MESH,
    )


def greet(places):
    barrier = pltpu.get_barrier_semaphore()
    for axis, index in places:
        pl.semaphore_signal(barrier, inc=1, device_id={axis: index}, device_id_type=MESH)
    pl.semaphore_wait(barrier, len(places))


def others(axis, n):
    me = lax.axis_index(axis)
    return [(axis, lax.rem(me + j, n)) for j in range(1, n)]


def square(me):
    return me + 1 - 2 * lax.rem(me, 2), lax.rem(me + 2, 4), 3 - me


def ring_places(n):
    me = lax.axis_index("seq")
    if n == 4:
        across, along, _ = square(me)
        return [("seq", across), ("seq", along)]
    return others("seq", n)


def gather_copies(n):
    return 6 if n == 4 else n - 1


def gather(n, own, out, send, recv, local):
    me = lax.axis_index("seq")
    keep = pltpu.make_async_copy(own, out.at[me], local)
    keep.start()
    if n == 4:
        across, along, _ = square(me)
        half = own.shape[0] // 2
        low, high = pl.ds(0, half), pl.ds(half, half)

        def piece(number, rows, to):
            return remote(
                own.at[rows], out.at[me, rows], send.at[number], recv.at[number], "seq", to
            )

        first = [
            piece(0, low, across),
            piece(1, high, along),
            piece(2, high, across),
            piece(3, low, along),
        ]
        for copy in first:
            copy.start()
        first[0].wait_recv()
        on_a = remote(
            out.at[across, low], out.at[across, low], send.at[4], recv.at[4], "seq", along
        )
        on_a.start()
        first[1].wait_recv()
        on_b = remote(
            out.at[along, high], out.at[along, high], send.at[5], recv.at[5], "seq", across
        )
        on_b.start()
        first[2].wait_recv()
        first[3].wait_recv()
        on_a.wait_recv()
        on_b.wait_recv()
        for copy in first + [on_a, on_b]:
            copy.wait_send()
    else:
        copies = []
        for j in range(1, n):
            to = lax.rem(me + j, n)
            copies.append(
                remote(own, out.at[me], send.at[j - 1], recv.at[j - 1], "seq", to)
            )
        for copy in copies:
            copy.start()
        for copy in copies:
            copy.wait()
    keep.wait()


def scatter_slots(n):
    return 4 if n == 4 else n - 1


def scatter_sum(n, part, slots, stage, send, recv, finish):
    me = lax.axis_index("seq")
    rows = part.shape[1]
    if n == 4:
        across, along, corner = square(me)
        half = rows // 2
        low, high = pl.ds(0, half), pl.ds(half, half)
        c0 = remote(part.at[corner, low], slots.at[2, low], send.at[0], recv.at[0], "seq", along)
        c1 = remote(part.at[corner, high], slots.at[2, high], send.at[1], recv.at[1], "seq", across)
        c2 = remote(part.at[across, high], slots.at[0, high], send.at[2], recv.at[2], "seq", across)
        c3 = remote(part.at[along, low], slots.at[1, low], send.at[3], recv.at[3], "seq", along)
        c4 = remote(stage.at[low], slots.at[0, low], send.at[4], recv.at[4], "seq", across)
        c5 = remote(stage.at[high], slots.at[1, high], send.at[5], recv.at[5], "seq", along)
        for copy in (c0, c1, c2, c3):
            copy.start()
        c0.wait_recv()
        stage[low] = (
            part[across, low].astype(F32) + slots[2, low].astype(F32)
        ).astype(BF)
        c4.start()
        c1.wait_recv()
        stage[high] = (
            part[along, high].astype(F32) + slots[2, high].astype(F32)
        ).astype(BF)
        c5.start()
        for copy in (c2, c3, c4, c5):
            copy.wait_recv()
        copies = (c0, c1, c2, c3, c4, c5)
        count = 2
    else:
        copies = []
        for j in range(1, n):
            to = lax.rem(me + j, n)
            copies.append(
                remote(part.at[to], slots.at[j - 1], send.at[j - 1], recv.at[j - 1], "seq", to)
            )
        for copy in copies:
            copy.start()
        for copy in copies:
            copy.wait_recv()
        count = n - 1
    step = 32

    def chunk(number, carry):
        at = pl.ds(pl.multiple_of(number * step, step), step)
        total = part[me, at].astype(F32)
        for slot in range(count):
            total += slots[slot, at].astype(F32)
        finish(at, total)
        return carry

    lax.fori_loop(0, rows // step, chunk, 0)
    for copy in copies:
        copy.wait_send()


def inverse_rms(values):
    return lax.rsqrt(jnp.mean(values * values, axis=-1, keepdims=True) + epsilon)


def norm_back(values, gain, grad):
    inverse = inverse_rms(values)
    scaled = grad * gain
    back = inverse * scaled - values * (
        inverse * inverse * inverse * jnp.mean(scaled * values, axis=-1, keepdims=True)
    )
    return back, jnp.sum(grad * values * inverse, axis=0, keepdims=True)


def attention_weights_out(n, nf, wq, wk, wv, gains, out, all_gains, seen, send, recv, gsend, grecv, local):
    me, spot = lax.axis_index("seq"), lax.axis_index("fsdp")
    greet(others("seq", n) + others("fsdp", nf))
    widths = [wq.shape[1] // n, wk.shape[1] // n, wv.shape[1] // n]
    begins = [0, widths[0], widths[0] + widths[1]]
    copies = []
    small = []
    for j in range(1, n):
        to = lax.rem(me + j, n)
        copy = remote(gains, seen.at[me], gsend.at[j - 1], grecv.at[j - 1], "seq", to)
        copy.start()
        small.append(copy)
        for i, ref in enumerate((wq, wk, wv)):
            columns = pl.ds(pl.multiple_of(to * widths[i], 128), widths[i])
            copies.append(
                remote(
                    ref.at[:, columns],
                    out.at[me, :, pl.ds(begins[i], widths[i])],
                    send.at[3 * j - 3 + i],
                    recv.at[3 * j - 3 + i],
                    "seq",
                    to,
                )
            )
    for copy in copies:
        copy.start()
    keeps = []
    for i, ref in enumerate((wq, wk, wv)):
        columns = pl.ds(pl.multiple_of(me * widths[i], 128), widths[i])
        keeps.append(
            pltpu.make_async_copy(
                ref.at[:, columns], out.at[me, :, pl.ds(begins[i], widths[i])], local.at[i]
            )
        )
    keeps.append(pltpu.make_async_copy(gains, seen.at[me], local.at[3]))
    for keep in keeps:
        keep.start()
    keeps[3].wait()
    for copy in small:
        copy.wait()
    last = pltpu.make_async_copy(seen, all_gains.at[spot], local.at[4])
    last.start()
    wide = []
    for j in range(1, nf):
        to = lax.rem(spot + j, nf)
        copy = remote(
            seen, all_gains.at[spot], gsend.at[n + j - 2], grecv.at[n + j - 2], "fsdp", to
        )
        copy.start()
        wide.append(copy)
    for copy in copies + wide:
        copy.wait()
    for keep in keeps[:3] + [last]:
        keep.wait()


def hidden_weights_out(n, x, wg, wu, wd, xg, gu, dn, send, recv, asend, arecv, local):
    me = lax.axis_index("seq")
    greet(others("seq", n))
    width = wg.shape[1] // n
    copies, keeps = [], []
    views = [(wg, gu, 0), (wu, gu, 1), (wd, dn, 0)]
    for i, (ref, out, place) in enumerate(views):
        for j in range(1, n):
            to = lax.rem(me + j, n)
            columns = pl.ds(pl.multiple_of(to * width, 128), width)
            k = i * (n - 1) + j - 1
            copies.append(
                remote(
                    ref.at[:, columns],
                    out.at[me, :, pl.ds(place * width, width)],
                    send.at[k],
                    recv.at[k],
                    "seq",
                    to,
                )
            )
        columns = pl.ds(pl.multiple_of(me * width, 128), width)
        keeps.append(
            pltpu.make_async_copy(
                ref.at[:, columns], out.at[me, :, pl.ds(place * width, width)], local.at[i]
            )
        )
    for copy in copies:
        copy.start()
    for keep in keeps:
        keep.start()
    gather(n, x, xg, asend, arecv, local.at[3])
    for copy in copies:
        copy.wait()
    for keep in keeps:
        keep.wait()


def gather_alone(n, x, out, send, recv, local):
    greet(ring_places(n))
    gather(n, x, out, send, recv, local)


def project(x_ref, gain_ref, w_ref, gq_ref, gk_ref, cos_ref, sin_ref, n1_ref, qraw_ref, kraw_ref, q_ref, k_ref, v_ref, kt_ref, vt_ref):
    x = x_ref[...].astype(F32)
    normed = (x * inverse_rms(x) * gain_ref[...]).astype(BF)
    n1_ref[...] = normed
    full = dot(normed, w_ref[...])
    qw, kw = q_ref.shape[1], k_ref.shape[1]
    cos, sin = cos_ref[...], sin_ref[...]

    def prep(head, gain):
        u = head * inverse_rms(head) * gain
        return u * cos + pltpu.roll(u, 64, 1) * sin

    qraw_ref[...] = full[:, :qw]
    kraw_ref[...] = full[:, qw : qw + kw]
    v = full[:, qw + kw :]
    v_ref[...] = v.astype(BF)
    vt_ref[...] = v.T.astype(BF)
    for h in range(qw // 128):
        q_ref[:, h * 128 : h * 128 + 128] = prep(
            full[:, h * 128 : h * 128 + 128], gq_ref[...]
        ).astype(BF)
    for h in range(kw // 128):
        turned = prep(full[:, qw + h * 128 : qw + h * 128 + 128], gk_ref[...])
        k_ref[:, h * 128 : h * 128 + 128] = turned.astype(BF)
        kt_ref[h * 128 : h * 128 + 128, :] = turned.T.astype(BF)


def bias_of(low_ref, high_ref, keys):
    key = lax.broadcasted_iota(jnp.int32, (keys, low_ref.shape[1]), 0)
    fine = (key >= low_ref[0:1, :]) & (key <= high_ref[0:1, :])
    return jnp.where(fine, 0.0, masked_score)


def attend(q_ref, k_ref, vt_ref, wo_ref, low_ref, high_ref, attn_ref, lse_ref, part_ref, bias):
    keys = k_ref.shape[0]
    bias[...] = bias_of(low_ref, high_ref, keys)
    heads = q_ref.shape[1] // 128
    ratio = heads // (k_ref.shape[1] // 128)
    factor = 128 ** (-0.5) * log2e
    for h in range(heads):
        kv = h // ratio
        scores = dot_nt(
            k_ref[:, kv * 128 : kv * 128 + 128], q_ref[:, h * 128 : h * 128 + 128]
        )
        scores = scores * factor + bias[...]
        top = jnp.max(scores, axis=0, keepdims=True)
        probs = jnp.exp2(scores - top)
        total = jnp.sum(probs, axis=0, keepdims=True)
        mixed = dot(vt_ref[kv * 128 : kv * 128 + 128, :], probs.astype(BF))
        lse_ref[h : h + 1, :] = top + jnp.log2(total)
        attn_ref[:, h * 128 : h * 128 + 128] = (mixed / total).T.astype(BF)
    part_ref[...] = dot(attn_ref[...], wo_ref[...]).astype(BF)


def middle_stage(n, part, x, gain, x2, n2, slots, stage, own, send, recv, asend, arecv, local):
    greet(ring_places(n))

    def finish(at, total):
        value = x[at].astype(F32) + total
        x2[at] = value
        own[at] = (value * inverse_rms(value) * gain[...]).astype(BF)

    scatter_sum(n, part, slots, stage, send, recv, finish)
    gather(n, own, n2, asend, arecv, local)


def ffn_forward(n2_ref, wg_ref, wu_ref, gate_ref, up_ref, hidden_ref):
    gate = dot(n2_ref[...], wg_ref[...])
    up = dot(n2_ref[...], wu_ref[...])
    gate_ref[...] = gate
    up_ref[...] = up
    hidden_ref[...] = (gate * jax.nn.sigmoid(gate) * up).astype(BF)


def ffn_back(cot_ref, wd_ref, gate_ref, up_ref, dgate_ref, dup_ref):
    dh = dot(cot_ref[...], wd_ref[...])
    gate = gate_ref[...]
    s = jax.nn.sigmoid(gate)
    dgate_ref[...] = (dh * up_ref[...] * (s * (1.0 + gate * (1.0 - s)))).astype(BF)
    dup_ref[...] = (dh * (gate * s)).astype(BF)


def two_nt(a_ref, b_ref, wa_ref, wb_ref, out_ref):
    out_ref[...] = (dot_nt(a_ref[...], wa_ref[...]) + dot_nt(b_ref[...], wb_ref[...])).astype(BF)


def one_nt(a_ref, w_ref, out_ref):
    out_ref[...] = dot_nt(a_ref[...], w_ref[...]).astype(BF)


def back_stage(n, part, x2, cot, gain, dx2, dz, dgain, slots, stage, own, send, recv, asend, arecv, local):
    greet(ring_places(n))
    dgain[...] = jnp.zeros_like(dgain)

    def finish(at, total):
        back, dg = norm_back(x2[at], gain[...], total)
        value = cot[at].astype(F32) + back
        dx2[at] = value
        own[at] = value.astype(BF)
        dgain[0:1] += dg

    scatter_sum(n, part, slots, stage, send, recv, finish)
    gather(n, own, dz, asend, arecv, local)


def out_stage(n, part, x2, out, slots, stage, send, recv):
    greet(ring_places(n))

    def finish(at, total):
        out[at] = (x2[at] + total).astype(BF)

    scatter_sum(n, part, slots, stage, send, recv, finish)


def input_stage(n, part, x, dx2, gain, out, dgain, slots, stage, send, recv):
    greet(ring_places(n))
    dgain[...] = jnp.zeros_like(dgain)

    def finish(at, total):
        back, dg = norm_back(x[at].astype(F32), gain[...], total)
        out[at] = (dx2[at] + back).astype(BF)
        dgain[0:1] += dg

    scatter_sum(n, part, slots, stage, send, recv, finish)


def attend_back(q_ref, qraw_ref, k_ref, kt_ref, v_ref, kraw_ref, dz_ref, wo_ref, lse_ref, low_ref, high_ref, cq_ref, sq_ref, ck_ref, sk_ref, gq_ref, gk_ref, dq_ref, dk_ref, dv_ref, dgq_ref, dgk_ref, dk_sum, dv_sum):
    kv, block = pl.program_id(0), pl.program_id(1)
    keys = k_ref.shape[0]
    ratio = q_ref.shape[1] // 128
    scale = 128 ** (-0.5)

    @pl.when((kv == 0) & (block == 0))
    def _():
        dgq_ref[...] = jnp.zeros_like(dgq_ref)
        dgk_ref[...] = jnp.zeros_like(dgk_ref)

    @pl.when(block == 0)
    def _():
        dk_sum[...] = jnp.zeros_like(dk_sum)
        dv_sum[...] = jnp.zeros_like(dv_sum)

    bias = bias_of(low_ref, high_ref, keys)
    dattn = dot_nt(dz_ref[...], wo_ref[...]).astype(BF)

    def prep_back(grad, raw, gain, cos, sin):
        du = grad * cos - pltpu.roll(grad, 64, 1) * sin
        return norm_back(raw, gain, du)

    for r in range(ratio):
        span = slice(r * 128, r * 128 + 128)
        qh, dah = q_ref[:, span], dattn[:, span]
        lse = lse_ref[pl.ds(kv * ratio + r, 1), :]
        scores = dot_nt(k_ref[...], qh) * (scale * log2e) + bias
        probs = jnp.exp2(scores - lse)
        dprobs = dot_nt(v_ref[...], dah)
        delta = jnp.sum(probs * dprobs, axis=0, keepdims=True)
        ds = (probs * (dprobs - delta)).astype(BF)
        dv_sum[...] += dot(probs.astype(BF), dah)
        dk_sum[...] += dot(ds, qh)
        dqr = dot(kt_ref[...], ds).T * scale
        back, dg = prep_back(dqr, qraw_ref[:, span], gq_ref[...], cq_ref[...], sq_ref[...])
        dq_ref[:, span] = back.astype(BF)
        dgq_ref[0:1] += dg

    @pl.when(block == pl.num_programs(1) - 1)
    def _():
        dv_ref[...] = dv_sum[...].astype(BF)
        back, dg = prep_back(
            dk_sum[...] * scale, kraw_ref[...], gk_ref[...], ck_ref[...], sk_ref[...]
        )
        dk_ref[...] = back.astype(BF)
        dgk_ref[0:1] += dg


def qkv_back(dq_ref, dk_ref, dv_ref, w_ref, out_ref):
    qw, kw = dq_ref.shape[1], dk_ref.shape[1]
    out_ref[...] = (
        dot_nt(dq_ref[...], w_ref[:, :qw])
        + dot_nt(dk_ref[...], w_ref[:, qw : qw + kw])
        + dot_nt(dv_ref[...], w_ref[:, qw + kw :])
    ).astype(BF)


def exchange(n, count, *refs):
    ins, outs = refs[:count], refs[count : 2 * count]
    send, recv, local = refs[2 * count :]
    me = lax.axis_index("seq")
    greet(others("seq", n))
    copies, keeps = [], []
    for i in range(count):
        for j in range(1, n):
            to = lax.rem(me + j, n)
            k = i * (n - 1) + j - 1
            copies.append(
                remote(ins[i].at[to], outs[i].at[me], send.at[k], recv.at[k], "seq", to)
            )
        keeps.append(pltpu.make_async_copy(ins[i].at[me], outs[i].at[me], local.at[i]))
    for copy in copies + keeps:
        copy.start()
    for copy in copies + keeps:
        copy.wait()


def gains_back(n, nf, part, out, wide, mid, seen, send, recv, local):
    me, spot = lax.axis_index("seq"), lax.axis_index("fsdp")
    greet(others("seq", n) + others("fsdp", nf))
    copies = []
    for j in range(1, nf):
        to = lax.rem(spot + j, nf)
        copies.append(
            remote(part.at[to], wide.at[j - 1], send.at[j - 1], recv.at[j - 1], "fsdp", to)
        )
    for copy in copies:
        copy.start()
    for copy in copies:
        copy.wait_recv()
    total = part[spot]
    for j in range(nf - 1):
        total += wide[j]
    mid[...] = total
    near = []
    for j in range(1, n):
        to = lax.rem(me + j, n)
        k = nf + j - 2
        near.append(remote(mid.at[to], seen.at[j - 1], send.at[k], recv.at[k], "seq", to))
    for copy in near:
        copy.start()
    for copy in near:
        copy.wait_recv()
    result = mid[me]
    for j in range(n - 1):
        result += seen[j]
    out[...] = result
    for copy in copies + near:
        copy.wait_send()


def dma(count):
    return pltpu.SemaphoreType.DMA((count,))


def shards(
    n,
    nf,
    tokens,
    seq_lengths,
    pic_starts,
    pic_lengths,
    norm1_gain,
    w_query,
    w_key,
    w_value,
    q_gain,
    k_gain,
    w_out,
    norm2_gain,
    w_gate,
    w_up,
    w_down,
    cotangent,
):
    rows, width = tokens.shape
    group = rows * n
    depth = w_query.shape[0]
    head = q_gain.shape[0] * n * nf
    qw, kw = w_query.shape[1] // n, w_key.shape[1] // n
    cw = qw + 2 * kw
    fw = w_gate.shape[1] // n
    qheads, kheads = qw // head, kw // head
    ratio = qheads // kheads
    own_gain = norm1_gain.shape[0]
    own_head = q_gain.shape[0]

    packed = jnp.zeros((8, 128), F32)
    packed = packed.at[0, :own_gain].set(norm1_gain.astype(F32))
    packed = packed.at[1, :own_gain].set(norm2_gain.astype(F32))
    packed = packed.at[2, :own_head].set(q_gain.astype(F32))
    packed = packed.at[3, :own_head].set(k_gain.astype(F32))
    wo = lax.all_gather(w_out, "fsdp", axis=0, tiled=True)
    w_att, all_gains = pl.pallas_call(
        functools.partial(attention_weights_out, n, nf),
        out_shape=(shape((n, depth, cw), BF), shape((nf, n, 8, 128), F32)),
        in_specs=[ANY] * 4,
        out_specs=(ANY, ANY),
        scratch_shapes=[
            pltpu.VMEM((n, 8, 128), F32),
            dma(3 * (n - 1)),
            dma(3 * (n - 1)),
            dma(n + nf - 2),
            dma(n + nf - 2),
            dma(5),
        ],
        compiler_params=comm_params(0),
    )(w_query, w_key, w_value, packed)
    w_att = lax.all_gather(w_att, "fsdp", axis=1, tiled=True).reshape(width, cw)
    ordered = all_gains.transpose(1, 0, 2, 3)
    gain_one = ordered[:, :, 0, :own_gain].reshape(1, width)
    gain_two = ordered[:, :, 1, :own_gain].reshape(1, width)
    gain_q = ordered[:, :, 2, :own_head].reshape(1, head)
    gain_k = ordered[:, :, 3, :own_head].reshape(1, head)

    wdt = w_down.T
    xg, gu, dn = pl.pallas_call(
        functools.partial(hidden_weights_out, n),
        out_shape=(
            shape((n, rows, width), BF),
            shape((n, depth, 2 * fw), BF),
            shape((n, depth, fw), BF),
        ),
        in_specs=[ANY] * 4,
        out_specs=(ANY,) * 3,
        scratch_shapes=[
            dma(3 * (n - 1)),
            dma(3 * (n - 1)),
            dma(gather_copies(n)),
            dma(gather_copies(n)),
            dma(4),
        ],
        compiler_params=comm_params(1),
    )(tokens, w_gate, w_up, wdt)
    gu = lax.all_gather(gu, "fsdp", axis=1, tiled=True).reshape(width, 2 * fw)
    dn = lax.all_gather(dn, "fsdp", axis=1, tiled=True).reshape(width, fw)

    places = jnp.arange(group, dtype=jnp.int32)
    lengths = seq_lengths[0]
    border_one = lengths[0]
    border_two = border_one + lengths[1]
    begins = jnp.where(places >= border_two, border_two, jnp.where(places >= border_one, border_one, 0))
    ends = jnp.where(places >= border_two, group, jnp.where(places >= border_one, border_two, border_one))
    starts, sizes = pic_starts[0], pic_lengths[0]
    inside = (places[:, None] >= starts[None, :]) & (places[:, None] < (starts + sizes)[None, :])
    pic_end = jnp.max(jnp.where(inside, (starts + sizes)[None, :], 0), axis=1)
    last = jnp.maximum(places, jnp.minimum(pic_end, ends) - 1)
    low = jnp.broadcast_to(begins[None, :], (8, group))
    high = jnp.broadcast_to(last[None, :], (8, group))
    half = head // 2
    frequency = F32(theta) ** (-(jnp.arange(half, dtype=F32) * 2.0 / head))
    angles = (places - begins).astype(F32)[:, None] * frequency[None, :]
    cosine, sine = jnp.cos(angles), jnp.sin(angles)
    cos = jnp.concatenate([cosine, cosine], axis=1)
    sin = jnp.concatenate([-sine, sine], axis=1)

    def whole(dims):
        return pl.BlockSpec(dims, lambda *ids: (0,) * len(dims))

    def by_rows(count, columns):
        return pl.BlockSpec((count, columns), lambda i: (i, 0))

    def by_cols(count, columns):
        return pl.BlockSpec((count, columns), lambda i: (0, i))

    blocks = group // 256
    n1, qraw, kraw, q, k, v, kt, vt = pl.pallas_call(
        project,
        grid=(blocks,),
        out_shape=(
            shape((group, width), BF),
            shape((group, qw), F32),
            shape((group, kw), F32),
            shape((group, qw), BF),
            shape((group, kw), BF),
            shape((group, kw), BF),
            shape((kw, group), BF),
            shape((kw, group), BF),
        ),
        in_specs=[
            by_rows(256, width),
            whole((1, width)),
            whole((width, cw)),
            whole((1, head)),
            whole((1, head)),
            by_rows(256, head),
            by_rows(256, head),
        ],
        out_specs=(
            by_rows(256, width),
            by_rows(256, qw),
            by_rows(256, kw),
            by_rows(256, qw),
            by_rows(256, kw),
            by_rows(256, kw),
            by_cols(kw, 256),
            by_cols(kw, 256),
        ),
        compiler_params=plain_params(),
    )(xg.reshape(group, width), gain_one, w_att, gain_q, gain_k, cos, sin)

    attn, lse, part_out = pl.pallas_call(
        attend,
        grid=(blocks,),
        out_shape=(
            shape((group, qw), BF),
            shape((8, group), F32),
            shape((group, width), BF),
        ),
        in_specs=[
            by_rows(256, qw),
            whole((group, kw)),
            whole((kw, group)),
            whole((qw, width)),
            by_cols(8, 256),
            by_cols(8, 256),
        ],
        out_specs=(by_rows(256, qw), by_cols(8, 256), by_rows(256, width)),
        scratch_shapes=[pltpu.VMEM((group, 256), F32)],
        compiler_params=plain_params(),
    )(q, k, vt, wo, low, high)

    slots = [
        pltpu.VMEM((scatter_slots(n), rows, width), BF),
        pltpu.VMEM((rows, width), BF),
    ]
    sems = [dma(max(6, n - 1)), dma(max(6, n - 1))]
    gather_sems = [dma(gather_copies(n)), dma(gather_copies(n)), pltpu.SemaphoreType.DMA]

    x2, n2 = pl.pallas_call(
        functools.partial(middle_stage, n),
        out_shape=(shape((rows, width), F32), shape((n, rows, width), BF)),
        in_specs=[VMEM] * 3,
        out_specs=(VMEM, ANY),
        scratch_shapes=slots + [pltpu.VMEM((rows, width), BF)] + sems + gather_sems,
        compiler_params=comm_params(2),
    )(part_out.reshape(n, rows, width), tokens, gain_two)
    n2 = n2.reshape(group, width)

    (cotangent_late,) = lax.optimization_barrier((cotangent, n2))[:1]
    cg = pl.pallas_call(
        functools.partial(gather_alone, n),
        out_shape=shape((n, rows, width), BF),
        in_specs=[ANY],
        out_specs=ANY,
        scratch_shapes=gather_sems,
        compiler_params=comm_params(3),
    )(cotangent_late).reshape(group, width)

    tile = 256
    tiles = fw // tile
    gate, up, hidden = pl.pallas_call(
        ffn_forward,
        grid=(tiles,),
        out_shape=(
            shape((group, fw), F32),
            shape((group, fw), F32),
            shape((group, fw), BF),
        ),
        in_specs=[
            whole((group, width)),
            by_cols(width, tile),
            pl.BlockSpec((width, tile), lambda i: (0, i + tiles)),
        ],
        out_specs=(by_cols(group, tile),) * 3,
        compiler_params=plain_params(),
    )(n2, gu, gu)

    def reduce_rows(grad, columns):
        return lax.psum_scatter(
            grad.reshape(n, width // n, columns), "fsdp", scatter_dimension=1, tiled=True
        )

    dn_share = reduce_rows(dot_tn(cg, hidden).astype(BF), fw)

    dgate, dup = pl.pallas_call(
        ffn_back,
        grid=(tiles,),
        out_shape=(shape((group, fw), BF), shape((group, fw), BF)),
        in_specs=[
            whole((group, width)),
            by_cols(width, tile),
            by_cols(group, tile),
            by_cols(group, tile),
        ],
        out_specs=(by_cols(group, tile),) * 2,
        compiler_params=plain_params(),
    )(cg, dn, gate, up)

    dgu = jnp.concatenate([dot_tn(n2, dgate).astype(BF), dot_tn(n2, dup).astype(BF)], axis=1)
    gu_share = reduce_rows(dgu, 2 * fw)

    part_n2 = pl.pallas_call(
        two_nt,
        grid=(blocks,),
        out_shape=shape((group, width), BF),
        in_specs=[
            by_rows(256, fw),
            by_rows(256, fw),
            pl.BlockSpec((width, fw), lambda i: (0, 0)),
            pl.BlockSpec((width, fw), lambda i: (0, 1)),
        ],
        out_specs=by_rows(256, width),
        compiler_params=plain_params(),
    )(dgate, dup, gu, gu)

    dx2, dz, dgain_two = pl.pallas_call(
        functools.partial(back_stage, n),
        out_shape=(
            shape((rows, width), F32),
            shape((n, rows, width), BF),
            shape((8, width), F32),
        ),
        in_specs=[VMEM] * 4,
        out_specs=(VMEM, ANY, VMEM),
        scratch_shapes=slots + [pltpu.VMEM((rows, width), BF)] + sems + gather_sems,
        compiler_params=comm_params(4),
    )(part_n2.reshape(n, rows, width), x2, cotangent, gain_two)
    dz = dz.reshape(group, width)

    part_y = pl.pallas_call(
        one_nt,
        grid=(blocks,),
        out_shape=shape((group, width), BF),
        in_specs=[by_rows(256, fw), whole((width, fw))],
        out_specs=by_rows(256, width),
        compiler_params=plain_params(),
    )(hidden, dn)
    output = pl.pallas_call(
        functools.partial(out_stage, n),
        out_shape=shape((rows, width), BF),
        in_specs=[VMEM] * 2,
        out_specs=VMEM,
        scratch_shapes=slots + sems,
        compiler_params=comm_params(5),
    )(part_y.reshape(n, rows, width), x2)

    wide = ratio * head
    dq, dk, dv, dgain_q, dgain_k = pl.pallas_call(
        attend_back,
        grid=(kheads, blocks),
        out_shape=(
            shape((group, qw), BF),
            shape((group, kw), BF),
            shape((group, kw), BF),
            shape((8, head), F32),
            shape((8, head), F32),
        ),
        in_specs=[
            pl.BlockSpec((256, wide), lambda h, b: (b, h)),
            pl.BlockSpec((256, wide), lambda h, b: (b, h)),
            pl.BlockSpec((group, head), lambda h, b: (0, h)),
            pl.BlockSpec((head, group), lambda h, b: (h, 0)),
            pl.BlockSpec((group, head), lambda h, b: (0, h)),
            pl.BlockSpec((group, head), lambda h, b: (0, h)),
            pl.BlockSpec((256, width), lambda h, b: (b, 0)),
            pl.BlockSpec((wide, width), lambda h, b: (h, 0)),
            pl.BlockSpec((8, 256), lambda h, b: (0, b)),
            pl.BlockSpec((8, 256), lambda h, b: (0, b)),
            pl.BlockSpec((8, 256), lambda h, b: (0, b)),
            pl.BlockSpec((256, head), lambda h, b: (b, 0)),
            pl.BlockSpec((256, head), lambda h, b: (b, 0)),
            whole((group, head)),
            whole((group, head)),
            whole((1, head)),
            whole((1, head)),
        ],
        out_specs=(
            pl.BlockSpec((256, wide), lambda h, b: (b, h)),
            pl.BlockSpec((group, head), lambda h, b: (0, h)),
            pl.BlockSpec((group, head), lambda h, b: (0, h)),
            whole((8, head)),
            whole((8, head)),
        ),
        scratch_shapes=[pltpu.VMEM((group, head), F32), pltpu.VMEM((group, head), F32)],
        compiler_params=plain_params(),
    )(q, qraw, k, kt, v, kraw, dz, wo, lse, low, high, cos, sin, cos, sin, gain_q, gain_k)

    wo_share = lax.psum_scatter(
        dot_tn(attn, dz).astype(BF), "fsdp", scatter_dimension=0, tiled=True
    )
    dqkv = jnp.concatenate([dq, dk, dv], axis=1)
    att_share = reduce_rows(dot_tn(n1, dqkv).astype(BF), cw)

    part_n1 = pl.pallas_call(
        qkv_back,
        grid=(blocks,),
        out_shape=shape((group, width), BF),
        in_specs=[
            by_rows(256, qw),
            by_rows(256, kw),
            by_rows(256, kw),
            whole((width, cw)),
        ],
        out_specs=by_rows(256, width),
        compiler_params=plain_params(),
    )(dq, dk, dv, w_att)
    input_grad, dgain_one = pl.pallas_call(
        functools.partial(input_stage, n),
        out_shape=(shape((rows, width), BF), shape((8, width), F32)),
        in_specs=[VMEM] * 4,
        out_specs=(VMEM, VMEM),
        scratch_shapes=slots + sems,
        compiler_params=comm_params(6),
    )(part_n1.reshape(n, rows, width), tokens, dx2, gain_one)

    def owned(row, count):
        cut = row.reshape(n, nf, 1, count)
        return jnp.pad(cut, ((0, 0), (0, 0), (0, 0), (0, 128 - count)))

    blocks_of = jnp.concatenate(
        [
            owned(dgain_one[0], own_gain),
            owned(dgain_two[0], own_gain),
            owned(dgain_q[0], own_head),
            owned(dgain_k[0], own_head),
            jnp.zeros((n, nf, 4, 128), F32),
        ],
        axis=2,
    ).transpose(1, 0, 2, 3)
    gains = pl.pallas_call(
        functools.partial(gains_back, n, nf),
        out_shape=shape((8, 128), F32),
        in_specs=[VMEM],
        out_specs=VMEM,
        scratch_shapes=[
            pltpu.VMEM((nf - 1, n, 8, 128), F32),
            pltpu.VMEM((n, 8, 128), F32),
            pltpu.VMEM((n - 1, 8, 128), F32),
            dma(n + nf - 2),
            dma(n + nf - 2),
            pltpu.SemaphoreType.DMA,
        ],
        compiler_params=comm_params(7),
    )(blocks_of)

    def swap(number, *arrays):
        count = len(arrays)
        return pl.pallas_call(
            functools.partial(exchange, n, count),
            out_shape=tuple(shape(a.shape, a.dtype) for a in arrays),
            in_specs=[ANY] * count,
            out_specs=(ANY,) * count,
            scratch_shapes=[dma(count * (n - 1)), dma(count * (n - 1)), dma(count)],
            compiler_params=comm_params(number),
        )(*arrays)

    gu_mine, dn_mine = swap(8, gu_share, dn_share)
    (att_mine,) = swap(9, att_share)

    def assemble(array, begin, count):
        return array[:, :, begin : begin + count].transpose(1, 0, 2).reshape(depth, -1).astype(F32)

    return (
        output,
        input_grad,
        gains[0, :own_gain],
        assemble(att_mine, 0, qw),
        assemble(att_mine, qw, kw),
        assemble(att_mine, qw + kw, kw),
        gains[2, :own_head],
        gains[3, :own_head],
        wo_share.astype(F32),
        gains[1, :own_gain],
        assemble(gu_mine, 0, fw),
        assemble(gu_mine, fw, fw),
        assemble(dn_mine, 0, fw).T,
    )


def solution(mesh):
    return jax.shard_map(
        functools.partial(shards, mesh.shape["seq"], mesh.shape["fsdp"]),
        mesh=mesh,
        in_specs=(
            P(("fsdp", "seq"), None),
            P("fsdp", None),
            P("fsdp", None),
            P("fsdp", None),
            P(("seq", "fsdp")),
            P(("seq", "fsdp"), None),
            P(("seq", "fsdp"), None),
            P(("seq", "fsdp"), None),
            P(("seq", "fsdp")),
            P(("seq", "fsdp")),
            P(("seq", "fsdp"), None),
            P(("seq", "fsdp")),
            P(("seq", "fsdp"), None),
            P(("seq", "fsdp"), None),
            P(None, ("seq", "fsdp")),
            P(("fsdp", "seq"), None),
        ),
        out_specs=(
            P(("fsdp", "seq"), None),
            P(("fsdp", "seq"), None),
            P(("seq", "fsdp")),
            P(("seq", "fsdp"), None),
            P(("seq", "fsdp"), None),
            P(("seq", "fsdp"), None),
            P(("seq", "fsdp")),
            P(("seq", "fsdp")),
            P(("seq", "fsdp"), None),
            P(("seq", "fsdp")),
            P(("seq", "fsdp"), None),
            P(("seq", "fsdp"), None),
            P(None, ("seq", "fsdp")),
        ),
        check_vma=False,
    )
```

```python
import functools

import jax
import jax.numpy as jnp
from jax import lax
from jax.experimental import pallas as pl
from jax.experimental.pallas import tpu as pltpu
from jax.sharding import PartitionSpec as P

epsilon = 1e-06
theta = 1000000.0
masked_score = -1e30
log2e = 1.4426950408889634

MESH = pl.DeviceIdType.MESH
ANY = pl.BlockSpec(memory_space=pl.ANY)
VMEM = pl.BlockSpec(memory_space=pltpu.VMEM)
BF = jnp.bfloat16
F32 = jnp.float32
LIMIT = 60 * 1024 * 1024


def dot(a, b):
    return jnp.dot(a, b, preferred_element_type=F32)


def dot_nt(a, b):
    return lax.dot_general(a, b, (((1,), (1,)), ((), ())), preferred_element_type=F32)


def dot_tn(a, b):
    return lax.dot_general(a, b, (((0,), (0,)), ((), ())), preferred_element_type=F32)


def shape(dims, dtype):
    return jax.ShapeDtypeStruct(dims, dtype)


def comm_params(number):
    return pltpu.CompilerParams(
        collective_id=number, has_side_effects=True, vmem_limit_bytes=LIMIT
    )


def plain_params():
    return pltpu.CompilerParams(vmem_limit_bytes=LIMIT)


def remote(src, dst, send, recv, axis, index):
    return pltpu.make_async_remote_copy(
        src_ref=src,
        dst_ref=dst,
        send_sem=send,
        recv_sem=recv,
        device_id={axis: index},
        device_id_type=MESH,
    )


def greet(places):
    barrier = pltpu.get_barrier_semaphore()
    for axis, index in places:
        pl.semaphore_signal(barrier, inc=1, device_id={axis: index}, device_id_type=MESH)
    pl.semaphore_wait(barrier, len(places))


def others(axis, n):
    me = lax.axis_index(axis)
    return [(axis, lax.rem(me + j, n)) for j in range(1, n)]


def square(me):
    return me + 1 - 2 * lax.rem(me, 2), lax.rem(me + 2, 4), 3 - me


def ring_places(n):
    me = lax.axis_index("seq")
    if n == 4:
        across, along, _ = square(me)
        return [("seq", across), ("seq", along)]
    return others("seq", n)


def gather_copies(n):
    return 6 if n == 4 else n - 1


def gather_parts(n, own, out, send, recv, local):
    me = lax.axis_index("seq")
    keep = pltpu.make_async_copy(own, out.at[me], local)
    half = own.shape[0] // 2
    low, high = pl.ds(0, half), pl.ds(half, half)
    if n == 4:
        across, along, _ = square(me)
        moves = [
            (own.at[low], out.at[me, low], across),
            (own.at[high], out.at[me, high], along),
            (own.at[high], out.at[me, high], across),
            (own.at[low], out.at[me, low], along),
            (out.at[across, low], out.at[across, low], along),
            (out.at[along, high], out.at[along, high], across),
        ]
    else:
        moves = [(own, out.at[me], lax.rem(me + j, n)) for j in range(1, n)]
    copies = [
        remote(src, dst, send.at[i], recv.at[i], "seq", to)
        for i, (src, dst, to) in enumerate(moves)
    ]

    def start():
        for copy in copies[:4]:
            copy.start()
        if n != 4:
            for copy in copies[4:]:
                copy.start()
        keep.start()

    def relay():
        if n == 4:
            copies[0].wait_recv()
            copies[4].start()
            copies[1].wait_recv()
            copies[5].start()

    def finish():
        for copy in copies[2:] if n == 4 else copies:
            copy.wait_recv()
        for copy in copies:
            copy.wait_send()
        keep.wait()

    return start, relay, finish


def gather(n, own, out, send, recv, local):
    for part in gather_parts(n, own, out, send, recv, local):
        part()


def scatter_slots(n):
    return 4 if n == 4 else n - 1


def scatter_sum(n, part, slots, stage, send, recv, finish):
    start, relay, total = scatter_parts(n, part, slots, stage, send, recv, finish)
    start()
    relay()
    total()


def scatter_parts(n, part, slots, stage, send, recv, finish):
    me = lax.axis_index("seq")
    rows = part.shape[1]
    half = rows // 2
    low, high = pl.ds(0, half), pl.ds(half, half)
    if n == 4:
        across, along, corner = square(me)
        moves = [
            (part.at[corner, low], slots.at[2, low], along),
            (part.at[corner, high], slots.at[2, high], across),
            (part.at[across, high], slots.at[0, high], across),
            (part.at[along, low], slots.at[1, low], along),
            (stage.at[low], slots.at[0, low], across),
            (stage.at[high], slots.at[1, high], along),
        ]
        count = 2
    else:
        moves = []
        for j in range(1, n):
            to = lax.rem(me + j, n)
            moves.append((part.at[to], slots.at[j - 1], to))
        count = n - 1
    copies = [
        remote(src, dst, send.at[i], recv.at[i], "seq", to)
        for i, (src, dst, to) in enumerate(moves)
    ]

    def start(begin=0, end=4):
        for copy in copies[begin:end] if n == 4 else copies:
            copy.start()

    def relay():
        if n == 4:
            copies[0].wait_recv()
            stage[low] = (part[across, low].astype(F32) + slots[2, low].astype(F32)).astype(BF)
            copies[4].start()
            copies[1].wait_recv()
            stage[high] = (part[along, high].astype(F32) + slots[2, high].astype(F32)).astype(BF)
            copies[5].start()

    def total():
        for copy in copies[2:] if n == 4 else copies:
            copy.wait_recv()
        step = 32

        def chunk(number, carry):
            at = pl.ds(pl.multiple_of(number * step, step), step)
            value = part[me, at].astype(F32)
            for slot in range(count):
                value += slots[slot, at].astype(F32)
            finish(at, value)
            return carry

        lax.fori_loop(0, rows // step, chunk, 0)
        for copy in copies:
            copy.wait_send()

    return start, relay, total


def inverse_rms(values):
    return lax.rsqrt(jnp.mean(values * values, axis=-1, keepdims=True) + epsilon)


def norm_back(values, gain, grad):
    inverse = inverse_rms(values)
    scaled = grad * gain
    back = inverse * scaled - values * (
        inverse * inverse * inverse * jnp.mean(scaled * values, axis=-1, keepdims=True)
    )
    return back, jnp.sum(grad * values * inverse, axis=0, keepdims=True)


def attention_weights_out(n, wq, wk, wv, out, send, recv, local):
    me = lax.axis_index("seq")
    greet(others("seq", n))
    widths = [wq.shape[1] // n, wk.shape[1] // n, wv.shape[1] // n]
    begins = [0, widths[0], widths[0] + widths[1]]
    copies = []
    for j in range(1, n):
        to = lax.rem(me + j, n)
        for i, ref in enumerate((wq, wk, wv)):
            columns = pl.ds(pl.multiple_of(to * widths[i], 128), widths[i])
            copies.append(
                remote(
                    ref.at[:, columns],
                    out.at[me, :, pl.ds(begins[i], widths[i])],
                    send.at[3 * j - 3 + i],
                    recv.at[3 * j - 3 + i],
                    "seq",
                    to,
                )
            )
    for i, ref in enumerate((wq, wk, wv)):
        columns = pl.ds(pl.multiple_of(me * widths[i], 128), widths[i])
        copies.append(
            pltpu.make_async_copy(
                ref.at[:, columns], out.at[me, :, pl.ds(begins[i], widths[i])], local.at[i]
            )
        )
    for copy in copies:
        copy.start()
    for copy in copies:
        copy.wait()


def start_columns(n, views, send, recv, local):
    me = lax.axis_index("seq")
    width = views[0][0].shape[1] // n
    copies, keeps = [], []
    for i, (ref, out, place) in enumerate(views):
        for j in range(1, n):
            to = lax.rem(me + j, n)
            columns = pl.ds(pl.multiple_of(to * width, 128), width)
            k = i * (n - 1) + j - 1
            copies.append(
                remote(
                    ref.at[:, columns],
                    out.at[me, :, pl.ds(place * width, width)],
                    send.at[k],
                    recv.at[k],
                    "seq",
                    to,
                )
            )
        columns = pl.ds(pl.multiple_of(me * width, 128), width)
        keeps.append(
            pltpu.make_async_copy(
                ref.at[:, columns], out.at[me, :, pl.ds(place * width, width)], local.at[i]
            )
        )
    for copy in copies + keeps:
        copy.start()
    return copies + keeps


def gate_up_out(n, nf, wg, wu, gains, gu, all_gains, seen, send, recv, local, gsend, grecv, glocal):
    me, spot = lax.axis_index("seq"), lax.axis_index("fsdp")
    greet(others("seq", n) + others("fsdp", nf))
    small = []
    for j in range(1, n):
        to = lax.rem(me + j, n)
        small.append(
            remote(gains, seen.at[me], gsend.at[j - 1], grecv.at[j - 1], "seq", to)
        )
    keep = pltpu.make_async_copy(gains, seen.at[me], glocal.at[0])
    for copy in small + [keep]:
        copy.start()
    copies = start_columns(n, [(wg, gu, 0), (wu, gu, 1)], send, recv, local)
    for copy in small + [keep]:
        copy.wait()
    wide = [pltpu.make_async_copy(seen, all_gains.at[spot], glocal.at[1])]
    for j in range(1, nf):
        to = lax.rem(spot + j, nf)
        k = n + j - 2
        wide.append(
            remote(seen, all_gains.at[spot], gsend.at[k], grecv.at[k], "fsdp", to)
        )
    for copy in wide:
        copy.start()
    for copy in copies + wide:
        copy.wait()


def line_gather(own, out, send, recv, local):
    spot = lax.axis_index("fsdp")
    z = lax.div(spot, 2)
    twin = spot + 1 - 2 * lax.rem(spot, 2)
    keep = pltpu.make_async_copy(own, out.at[spot], local)
    keep.start()

    def up(k):
        block = spot - 2 * k
        return remote(
            own if k == 0 else out.at[block], out.at[block], send.at[k], recv.at[k], "fsdp", spot + 2
        )

    def down(k):
        block = spot + 2 * k
        return remote(
            own if k == 0 else out.at[block],
            out.at[block],
            send.at[3 + k],
            recv.at[3 + k],
            "fsdp",
            spot - 2,
        )

    def over(offset):
        block = spot + 2 * offset
        return remote(
            own if offset == 0 else out.at[block],
            out.at[block],
            send.at[6 + lax.div(block, 2)],
            recv.at[6 + lax.div(block, 2)],
            "fsdp",
            twin,
        )

    def from_twin(offset):
        block = twin + 2 * offset
        return remote(
            own, out.at[block], send.at[6 + lax.div(block, 2)], recv.at[6 + lax.div(block, 2)], "fsdp", twin
        )

    @pl.when(z < 3)
    def _():
        up(0).start()

    @pl.when(z > 0)
    def _():
        down(0).start()

    over(0).start()
    for k in range(1, 4):

        @pl.when(z >= k)
        def _():
            up(k - 1).wait_recv()
            if k < 3:

                @pl.when(z < 3)
                def _():
                    up(k).start()

            over(-k).start()

        @pl.when(z + k <= 3)
        def _():
            down(k - 1).wait_recv()
            if k < 3:

                @pl.when(z > 0)
                def _():
                    down(k).start()

            over(k).start()

    from_twin(0).wait_recv()
    over(0).wait_send()
    for k in range(1, 4):

        @pl.when(z >= k)
        def _():
            from_twin(-k).wait_recv()
            over(-k).wait_send()

        @pl.when(z + k <= 3)
        def _():
            from_twin(k).wait_recv()
            over(k).wait_send()

    for k in range(3):

        @pl.when((z >= k) & (z < 3))
        def _():
            up(k).wait_send()

        @pl.when((z + k <= 3) & (z > 0))
        def _():
            down(k).wait_send()

    keep.wait()


def greet_line(places):
    spot = lax.axis_index("fsdp")
    z = lax.div(spot, 2)
    twin = spot + 1 - 2 * lax.rem(spot, 2)
    barrier = pltpu.get_barrier_semaphore()
    for axis, index in places + [("fsdp", twin)]:
        pl.semaphore_signal(barrier, inc=1, device_id={axis: index}, device_id_type=MESH)

    @pl.when(z < 3)
    def _():
        pl.semaphore_signal(barrier, inc=1, device_id={"fsdp": spot + 2}, device_id_type=MESH)

    @pl.when(z > 0)
    def _():
        pl.semaphore_signal(barrier, inc=1, device_id={"fsdp": spot - 2}, device_id_type=MESH)

    inner = (z < 3).astype(jnp.int32) + (z > 0).astype(jnp.int32)
    pl.semaphore_wait(barrier, len(places) + 1 + inner)


def entry_stage(n, nf, line, x, wd, w_out, xg, dn, wo, send, recv, local, wsend, wrecv, wlocal, lsend, lrecv, llocal):
    if line:
        greet_line(others("seq", n))
    else:
        greet(others("seq", n))
    start, relay, finish = gather_parts(n, x, xg, send, recv, local)
    start()
    copies = start_columns(n, [(wd, dn, 0)], wsend, wrecv, wlocal)
    if line:
        line_gather(w_out, wo, lsend, lrecv, llocal)
    else:
        keep = pltpu.make_async_copy(w_out, wo.at[0], llocal)
        keep.start()
        keep.wait()
    relay()
    finish()
    for copy in copies:
        copy.wait()


def half_gather(n, begin, cot, cg, send, recv, local):
    at = pl.ds(begin, cot.shape[0] // 2)
    start, relay, finish = gather_parts(n, cot.at[at], cg.at[:, at], send, recv, local)
    step, steps = pl.program_id(0), pl.num_programs(0)

    @pl.when(step == 0)
    def _():
        greet(ring_places(n))
        start()

    @pl.when(step == steps - 1)
    def _():
        relay()

    return finish


def project(n, x_ref, gain_ref, w_ref, gq_ref, gk_ref, cos_ref, sin_ref, cot, n1_ref, qraw_ref, kraw_ref, q_ref, k_ref, v_ref, kt_ref, vt_ref, cg, send, recv, local):
    finish_half = half_gather(n, 0, cot, cg, send, recv, local)
    x = x_ref[...].astype(F32)
    normed = (x * inverse_rms(x) * gain_ref[...]).astype(BF)
    n1_ref[...] = normed
    full = dot(normed, w_ref[...])
    qw, kw = q_ref.shape[1], k_ref.shape[1]
    cos, sin = cos_ref[...], sin_ref[...]

    def prep(head, gain):
        u = head * inverse_rms(head) * gain
        return u * cos + pltpu.roll(u, 64, 1) * sin

    qraw_ref[...] = full[:, :qw]
    kraw_ref[...] = full[:, qw : qw + kw]
    v = full[:, qw + kw :]
    v_ref[...] = v.astype(BF)
    vt_ref[...] = v.T.astype(BF)
    for h in range(qw // 128):
        q_ref[:, h * 128 : h * 128 + 128] = prep(
            full[:, h * 128 : h * 128 + 128], gq_ref[...]
        ).astype(BF)
    for h in range(kw // 128):
        turned = prep(full[:, qw + h * 128 : qw + h * 128 + 128], gk_ref[...])
        k_ref[:, h * 128 : h * 128 + 128] = turned.astype(BF)
        kt_ref[h * 128 : h * 128 + 128, :] = turned.T.astype(BF)

    @pl.when(pl.program_id(0) == pl.num_programs(0) - 1)
    def _():
        finish_half()


def bias_of(low_ref, high_ref, keys):
    key = lax.broadcasted_iota(jnp.int32, (keys, low_ref.shape[1]), 0)
    fine = (key >= low_ref[0:1, :]) & (key <= high_ref[0:1, :])
    return jnp.where(fine, 0.0, masked_score)


def attend(n, q_ref, k_ref, vt_ref, wo_ref, low_ref, high_ref, cot, cg_half, attn_ref, lse_ref, part_ref, cg, bias, send, recv, local):
    finish_half = half_gather(n, cot.shape[0] // 2, cot, cg, send, recv, local)
    keys = k_ref.shape[0]
    bias[...] = bias_of(low_ref, high_ref, keys)
    heads = q_ref.shape[1] // 128
    ratio = heads // (k_ref.shape[1] // 128)
    factor = 128 ** (-0.5) * log2e
    for h in range(heads):
        kv = h // ratio
        scores = dot_nt(
            k_ref[:, kv * 128 : kv * 128 + 128], q_ref[:, h * 128 : h * 128 + 128]
        )
        scores = scores * factor + bias[...]
        top = jnp.max(scores, axis=0, keepdims=True)
        probs = jnp.exp2(scores - top)
        total = jnp.sum(probs, axis=0, keepdims=True)
        mixed = dot(vt_ref[kv * 128 : kv * 128 + 128, :], probs.astype(BF))
        lse_ref[h : h + 1, :] = top + jnp.log2(total)
        attn_ref[:, h * 128 : h * 128 + 128] = (mixed / total).T.astype(BF)
    part_ref[...] = dot(attn_ref[...], wo_ref[...]).astype(BF)

    @pl.when(pl.program_id(0) == pl.num_programs(0) - 1)
    def _():
        finish_half()


def middle_stage(n, part, x, gain, x2, n2, slots, stage, own, send, recv, asend, arecv, local):
    greet(ring_places(n))

    def finish(at, total):
        value = x[at].astype(F32) + total
        x2[at] = value
        own[at] = (value * inverse_rms(value) * gain[...]).astype(BF)

    scatter_sum(n, part, slots, stage, send, recv, finish)
    gather(n, own, n2, asend, arecv, local)


def ffn_forward(n2_ref, wg_ref, wu_ref, gate_ref, up_ref, hidden_ref):
    gate = dot(n2_ref[...], wg_ref[...])
    up = dot(n2_ref[...], wu_ref[...])
    gate_ref[...] = gate
    up_ref[...] = up
    hidden_ref[...] = (gate * jax.nn.sigmoid(gate) * up).astype(BF)


def ffn_back(cot_ref, wd_ref, gate_ref, up_ref, dgate_ref, dup_ref):
    dh = dot(cot_ref[...], wd_ref[...])
    gate = gate_ref[...]
    s = jax.nn.sigmoid(gate)
    dgate_ref[...] = (dh * up_ref[...] * (s * (1.0 + gate * (1.0 - s)))).astype(BF)
    dup_ref[...] = (dh * (gate * s)).astype(BF)


def two_nt(a_ref, b_ref, wa_ref, wb_ref, out_ref):
    out_ref[...] = (dot_nt(a_ref[...], wa_ref[...]) + dot_nt(b_ref[...], wb_ref[...])).astype(BF)


def one_nt(a_ref, w_ref, out_ref):
    out_ref[...] = dot_nt(a_ref[...], w_ref[...]).astype(BF)


def back_stage(n, part, x2, cot, gain, dx2, dz, dgain, slots, stage, own, send, recv, asend, arecv, local):
    greet(ring_places(n))
    dgain[...] = jnp.zeros_like(dgain)

    def finish(at, total):
        back, dg = norm_back(x2[at], gain[...], total)
        value = cot[at].astype(F32) + back
        dx2[at] = value
        own[at] = value.astype(BF)
        dgain[0:1] += dg

    scatter_sum(n, part, slots, stage, send, recv, finish)
    gather(n, own, dz, asend, arecv, local)


def input_stage(n, part, x, gain, out, dgain, slots, stage, send, recv):
    greet(ring_places(n))
    dgain[...] = jnp.zeros_like(dgain)

    def finish(at, total):
        back, dg = norm_back(x[at].astype(F32), gain[...], total)
        out[at] = back
        dgain[0:1] += dg

    scatter_sum(n, part, slots, stage, send, recv, finish)


def attend_back(n, q_ref, qraw_ref, k_ref, kt_ref, v_ref, kraw_ref, dz_ref, wo_ref, lse_ref, low_ref, high_ref, cq_ref, sq_ref, ck_ref, sk_ref, gq_ref, gk_ref, part, dq_ref, dk_ref, dv_ref, dgq_ref, dgk_ref, out, dk_sum, dv_sum, slots, stage, send, recv):
    kv, block = pl.program_id(0), pl.program_id(1)
    keys = k_ref.shape[0]
    ratio = q_ref.shape[1] // 128
    scale = 128 ** (-0.5)

    def finish(at, total):
        out[at] = total

    start, relay, total = scatter_parts(n, part, slots, stage, send, recv, finish)
    steps = pl.num_programs(0) * pl.num_programs(1)
    step = kv * pl.num_programs(1) + block

    @pl.when(step == 0)
    def _():
        greet(ring_places(n))
        start()
        dgq_ref[...] = jnp.zeros_like(dgq_ref)
        dgk_ref[...] = jnp.zeros_like(dgk_ref)

    @pl.when(step == steps // 2)
    def _():
        relay()

    @pl.when(block == 0)
    def _():
        dk_sum[...] = jnp.zeros_like(dk_sum)
        dv_sum[...] = jnp.zeros_like(dv_sum)

    bias = bias_of(low_ref, high_ref, keys)
    dattn = dot_nt(dz_ref[...], wo_ref[...]).astype(BF)

    def prep_back(grad, raw, gain, cos, sin):
        du = grad * cos - pltpu.roll(grad, 64, 1) * sin
        return norm_back(raw, gain, du)

    for r in range(ratio):
        span = slice(r * 128, r * 128 + 128)
        qh, dah = q_ref[:, span], dattn[:, span]
        lse = lse_ref[pl.ds(kv * ratio + r, 1), :]
        scores = dot_nt(k_ref[...], qh) * (scale * log2e) + bias
        probs = jnp.exp2(scores - lse)
        dprobs = dot_nt(v_ref[...], dah)
        delta = jnp.sum(probs * dprobs, axis=0, keepdims=True)
        ds = (probs * (dprobs - delta)).astype(BF)
        dv_sum[...] += dot(probs.astype(BF), dah)
        dk_sum[...] += dot(ds, qh)
        dqr = dot(kt_ref[...], ds).T * scale
        back, dg = prep_back(dqr, qraw_ref[:, span], gq_ref[...], cq_ref[...], sq_ref[...])
        dq_ref[:, span] = back.astype(BF)
        dgq_ref[0:1] += dg

    @pl.when(block == pl.num_programs(1) - 1)
    def _():
        dv_ref[...] = dv_sum[...].astype(BF)
        back, dg = prep_back(
            dk_sum[...] * scale, kraw_ref[...], gk_ref[...], ck_ref[...], sk_ref[...]
        )
        dk_ref[...] = back.astype(BF)
        dgk_ref[0:1] += dg

    @pl.when(step == steps - 1)
    def _():
        total()


def gradient(counts, kept, *refs):
    a_ref, bs, out_ref, turned = refs[0], refs[1 : 1 + len(counts)], refs[-2], refs[-1]
    spot = pl.program_id(0)

    @pl.when(spot == 0)
    def _():
        turned[...] = a_ref[...].T

    depth = out_ref.shape[1]
    step = min(512, depth)
    begin = 0
    for b_ref, count in zip(bs, counts):

        @pl.when((spot >= begin) & (spot < begin + count))
        def _(b_ref=b_ref):
            for at in range(0, turned.shape[0], step):
                inner = at % depth
                out_ref[at // depth, inner : inner + step, :] = dot(
                    turned[at : at + step, :], b_ref[...]
                ).astype(BF)

        begin += count


def qkv_back(dq_ref, dk_ref, dv_ref, w_ref, out_ref):
    qw, kw = dq_ref.shape[1], dk_ref.shape[1]
    out_ref[...] = (
        dot_nt(dq_ref[...], w_ref[:, :qw])
        + dot_nt(dk_ref[...], w_ref[:, qw : qw + kw])
        + dot_nt(dv_ref[...], w_ref[:, qw + kw :])
    ).astype(BF)


def exchange(n, count, *refs):
    ins, outs = refs[:count], refs[count : 2 * count]
    send, recv, local = refs[2 * count :]
    me = lax.axis_index("seq")
    greet(others("seq", n))
    copies, keeps = [], []
    for i in range(count):
        for j in range(1, n):
            to = lax.rem(me + j, n)
            k = i * (n - 1) + j - 1
            copies.append(
                remote(ins[i].at[to], outs[i].at[me], send.at[k], recv.at[k], "seq", to)
            )
        keeps.append(pltpu.make_async_copy(ins[i].at[me], outs[i].at[me], local.at[i]))
    for copy in copies + keeps:
        copy.start()
    for copy in copies + keeps:
        copy.wait()


def widen(pieces, *refs):
    ins, outs = refs[: -len(pieces)], refs[-len(pieces) :]
    for out, (i, begin, count) in zip(outs, pieces):
        out[...] = ins[i][0, :, begin : begin + count].astype(F32)


def gains_back(n, nf, part, out, wide, mid, seen, send, recv, local):
    me, spot = lax.axis_index("seq"), lax.axis_index("fsdp")
    greet(others("seq", n) + others("fsdp", nf))
    copies = []
    for j in range(1, nf):
        to = lax.rem(spot + j, nf)
        copies.append(
            remote(part.at[to], wide.at[j - 1], send.at[j - 1], recv.at[j - 1], "fsdp", to)
        )
    for copy in copies:
        copy.start()
    for copy in copies:
        copy.wait_recv()
    total = part[spot]
    for j in range(nf - 1):
        total += wide[j]
    mid[...] = total
    near = []
    for j in range(1, n):
        to = lax.rem(me + j, n)
        k = nf + j - 2
        near.append(remote(mid.at[to], seen.at[j - 1], send.at[k], recv.at[k], "seq", to))
    for copy in near:
        copy.start()
    for copy in near:
        copy.wait_recv()
    result = mid[me]
    for j in range(n - 1):
        result += seen[j]
    out[...] = result
    for copy in copies + near:
        copy.wait_send()


def after(value, done):
    return lax.optimization_barrier((value, done))[0]


def dma(count):
    return pltpu.SemaphoreType.DMA((count,))


def shards(
    n,
    nf,
    tokens,
    seq_lengths,
    pic_starts,
    pic_lengths,
    norm1_gain,
    w_query,
    w_key,
    w_value,
    q_gain,
    k_gain,
    w_out,
    norm2_gain,
    w_gate,
    w_up,
    w_down,
    cotangent,
):
    rows, width = tokens.shape
    group = rows * n
    depth = w_query.shape[0]
    head = q_gain.shape[0] * n * nf
    qw, kw = w_query.shape[1] // n, w_key.shape[1] // n
    cw = qw + 2 * kw
    fw = w_gate.shape[1] // n
    qheads, kheads = qw // head, kw // head
    ratio = qheads // kheads
    own_gain = norm1_gain.shape[0]
    own_head = q_gain.shape[0]

    packed = jnp.zeros((8, 128), F32)
    packed = packed.at[0, :own_gain].set(norm1_gain.astype(F32))
    packed = packed.at[1, :own_gain].set(norm2_gain.astype(F32))
    packed = packed.at[2, :own_head].set(q_gain.astype(F32))
    packed = packed.at[3, :own_head].set(k_gain.astype(F32))
    w_att = pl.pallas_call(
        functools.partial(attention_weights_out, n),
        out_shape=shape((n, depth, cw), BF),
        in_specs=[ANY] * 3,
        out_specs=ANY,
        scratch_shapes=[dma(3 * (n - 1)), dma(3 * (n - 1)), dma(3)],
        compiler_params=comm_params(0),
    )(w_query, w_key, w_value)
    gu, all_gains = pl.pallas_call(
        functools.partial(gate_up_out, n, nf),
        out_shape=(shape((n, depth, 2 * fw), BF), shape((nf, n, 8, 128), F32)),
        in_specs=[ANY] * 3,
        out_specs=(ANY, ANY),
        scratch_shapes=[
            pltpu.VMEM((n, 8, 128), F32),
            dma(2 * (n - 1)),
            dma(2 * (n - 1)),
            dma(2),
            dma(n + nf - 2),
            dma(n + nf - 2),
            dma(2),
        ],
        compiler_params=comm_params(8),
    )(after(w_gate, w_att), w_up, packed)
    ordered = all_gains.transpose(1, 0, 2, 3)
    gain_one = ordered[:, :, 0, :own_gain].reshape(1, width)
    gain_two = ordered[:, :, 1, :own_gain].reshape(1, width)
    gain_q = ordered[:, :, 2, :own_head].reshape(1, head)
    gain_k = ordered[:, :, 3, :own_head].reshape(1, head)

    wdt = w_down.T
    gather_sems = [dma(gather_copies(n)), dma(gather_copies(n)), pltpu.SemaphoreType.DMA]
    line = nf == 8
    w_att = lax.all_gather(w_att, "fsdp", axis=1, tiled=True).reshape(width, cw)
    xg, dn, wo = pl.pallas_call(
        functools.partial(entry_stage, n, nf, line),
        out_shape=(
            shape((n, rows, width), BF),
            shape((n, depth, fw), BF),
            shape((nf if line else 1, depth, width), BF),
        ),
        in_specs=[ANY] * 3,
        out_specs=(ANY,) * 3,
        scratch_shapes=gather_sems
        + [dma(n - 1), dma(n - 1), dma(1), dma(10), dma(10), pltpu.SemaphoreType.DMA],
        compiler_params=comm_params(1),
    )(after(tokens, gu), wdt, w_out)
    wo = wo.reshape(-1, width)
    if not line:
        wo = lax.all_gather(wo, "fsdp", axis=0, tiled=True)
    gu = lax.all_gather(gu, "fsdp", axis=1, tiled=True).reshape(width, 2 * fw)
    dn = lax.all_gather(dn, "fsdp", axis=1, tiled=True).reshape(width, fw)

    places = jnp.arange(group, dtype=jnp.int32)
    lengths = seq_lengths[0]
    border_one = lengths[0]
    border_two = border_one + lengths[1]
    begins = jnp.where(places >= border_two, border_two, jnp.where(places >= border_one, border_one, 0))
    ends = jnp.where(places >= border_two, group, jnp.where(places >= border_one, border_two, border_one))
    starts, sizes = pic_starts[0], pic_lengths[0]
    inside = (places[:, None] >= starts[None, :]) & (places[:, None] < (starts + sizes)[None, :])
    pic_end = jnp.max(jnp.where(inside, (starts + sizes)[None, :], 0), axis=1)
    last = jnp.maximum(places, jnp.minimum(pic_end, ends) - 1)
    low = jnp.broadcast_to(begins[None, :], (8, group))
    high = jnp.broadcast_to(last[None, :], (8, group))
    half = head // 2
    frequency = F32(theta) ** (-(jnp.arange(half, dtype=F32) * 2.0 / head))
    angles = (places - begins).astype(F32)[:, None] * frequency[None, :]
    cosine, sine = jnp.cos(angles), jnp.sin(angles)
    cos = jnp.concatenate([cosine, cosine], axis=1)
    sin = jnp.concatenate([-sine, sine], axis=1)

    def whole(dims):
        return pl.BlockSpec(dims, lambda *ids: (0,) * len(dims))

    def by_rows(count, columns):
        return pl.BlockSpec((count, columns), lambda i: (i, 0))

    def by_cols(count, columns):
        return pl.BlockSpec((count, columns), lambda i: (0, i))

    blocks = group // 256
    n1, qraw, kraw, q, k, v, kt, vt, cg = pl.pallas_call(
        functools.partial(project, n),
        grid=(blocks,),
        out_shape=(
            shape((group, width), BF),
            shape((group, qw), F32),
            shape((group, kw), F32),
            shape((group, qw), BF),
            shape((group, kw), BF),
            shape((group, kw), BF),
            shape((kw, group), BF),
            shape((kw, group), BF),
            shape((n, rows, width), BF),
        ),
        in_specs=[
            by_rows(256, width),
            whole((1, width)),
            whole((width, cw)),
            whole((1, head)),
            whole((1, head)),
            by_rows(256, head),
            by_rows(256, head),
            ANY,
        ],
        out_specs=(
            by_rows(256, width),
            by_rows(256, qw),
            by_rows(256, kw),
            by_rows(256, qw),
            by_rows(256, kw),
            by_rows(256, kw),
            by_cols(kw, 256),
            by_cols(kw, 256),
            ANY,
        ),
        scratch_shapes=gather_sems,
        compiler_params=comm_params(11),
    )(xg.reshape(group, width), gain_one, w_att, gain_q, gain_k, cos, sin, cotangent)

    attn, lse, part_out, cg = pl.pallas_call(
        functools.partial(attend, n),
        grid=(blocks,),
        out_shape=(
            shape((group, qw), BF),
            shape((8, group), F32),
            shape((group, width), BF),
            shape((n, rows, width), BF),
        ),
        in_specs=[
            by_rows(256, qw),
            whole((group, kw)),
            whole((kw, group)),
            whole((qw, width)),
            by_cols(8, 256),
            by_cols(8, 256),
            ANY,
            ANY,
        ],
        out_specs=(by_rows(256, qw), by_cols(8, 256), by_rows(256, width), ANY),
        scratch_shapes=[pltpu.VMEM((group, 256), F32)] + gather_sems,
        input_output_aliases={7: 3},
        compiler_params=comm_params(3),
    )(q, k, vt, wo, low, high, cotangent, cg)
    cg = cg.reshape(group, width)

    slots = [
        pltpu.VMEM((scatter_slots(n), rows, width), BF),
        pltpu.VMEM((rows, width), BF),
    ]
    sems = [dma(max(6, n - 1)), dma(max(6, n - 1))]

    x2, n2 = pl.pallas_call(
        functools.partial(middle_stage, n),
        out_shape=(shape((rows, width), F32), shape((n, rows, width), BF)),
        in_specs=[VMEM] * 3,
        out_specs=(VMEM, ANY),
        scratch_shapes=slots + [pltpu.VMEM((rows, width), BF)] + sems + gather_sems,
        compiler_params=comm_params(2),
    )(part_out.reshape(n, rows, width), tokens, gain_two)
    n2 = n2.reshape(group, width)

    tile = 256
    tiles = fw // tile
    gate, up, hidden = pl.pallas_call(
        ffn_forward,
        grid=(tiles,),
        out_shape=(
            shape((group, fw), F32),
            shape((group, fw), F32),
            shape((group, fw), BF),
        ),
        in_specs=[
            whole((group, width)),
            by_cols(width, tile),
            pl.BlockSpec((width, tile), lambda i: (0, i + tiles)),
        ],
        out_specs=(by_cols(group, tile),) * 3,
        compiler_params=plain_params(),
    )(n2, gu, gu)

    def product(a, *bs, into=None, dims=None, spot=None):
        tile = 512
        while any(b.shape[1] % tile for b in bs):
            tile //= 2
        counts = [b.shape[1] // tile for b in bs]
        begins = [sum(counts[:i]) for i in range(len(bs))]

        def spec(begin, count):
            return pl.BlockSpec(
                (group, tile), lambda i: (0, jnp.clip(i - begin, 0, count - 1))
            )

        if dims is None:
            dims = (1, a.shape[1], sum(counts) * tile)
        lead = a.shape[1] // dims[1]
        across = dims[2] // tile
        first = 0 if spot is None else spot
        kept = [] if into is None else [into]
        return pl.pallas_call(
            functools.partial(gradient, counts, len(kept)),
            grid=(sum(counts),),
            out_shape=shape(dims, BF),
            in_specs=[whole(a.shape)]
            + [spec(b, c) for b, c in zip(begins, counts)]
            + [ANY] * len(kept),
            out_specs=pl.BlockSpec(
                (lead, dims[1], tile),
                lambda i: (first + lax.div(i, across), 0, lax.rem(i, across)),
            ),
            scratch_shapes=[pltpu.VMEM((a.shape[1], group), BF)],
            input_output_aliases={} if into is None else {1 + len(bs): 0},
            compiler_params=plain_params(),
        )(a, *bs, *kept)

    def reduce_rows(grad, columns):
        return lax.psum_scatter(
            grad.reshape(n, width // n, columns), "fsdp", scatter_dimension=1, tiled=True
        )

    dn_grad = product(cg, hidden)
    dn_share = reduce_rows(dn_grad, fw)

    dgate, dup = pl.pallas_call(
        ffn_back,
        grid=(tiles,),
        out_shape=(shape((group, fw), BF), shape((group, fw), BF)),
        in_specs=[
            whole((group, width)),
            by_cols(width, tile),
            by_cols(group, tile),
            by_cols(group, tile),
        ],
        out_specs=(by_cols(group, tile),) * 2,
        compiler_params=plain_params(),
    )(cg, after(dn, dn_grad), gate, up)

    gu_grad = product(n2, dgate, dup)
    part_n2 = pl.pallas_call(
        two_nt,
        grid=(blocks,),
        out_shape=shape((group, width), BF),
        in_specs=[
            by_rows(256, fw),
            by_rows(256, fw),
            pl.BlockSpec((width, fw), lambda i: (0, 0)),
            pl.BlockSpec((width, fw), lambda i: (0, 1)),
        ],
        out_specs=by_rows(256, width),
        compiler_params=plain_params(),
    )(after(dgate, gu_grad), dup, gu, gu)
    part_y = pl.pallas_call(
        one_nt,
        grid=(blocks,),
        out_shape=shape((group, width), BF),
        in_specs=[by_rows(256, fw), whole((width, fw))],
        out_specs=by_rows(256, width),
        compiler_params=plain_params(),
    )(after(hidden, part_n2), dn)
    gu_share = reduce_rows(after(gu_grad, (dn_share, part_y)), 2 * fw)

    dx2, dz, dgain_two = pl.pallas_call(
        functools.partial(back_stage, n),
        out_shape=(
            shape((rows, width), F32),
            shape((n, rows, width), BF),
            shape((8, width), F32),
        ),
        in_specs=[VMEM] * 4,
        out_specs=(VMEM, ANY, VMEM),
        scratch_shapes=slots + [pltpu.VMEM((rows, width), BF)] + sems + gather_sems,
        compiler_params=comm_params(4),
    )(
        after(part_n2, (part_y, dn_share)).reshape(n, rows, width), x2, cotangent, gain_two,
    )
    dz = dz.reshape(group, width)

    wo_grad = product(attn, dz, dims=(n + width // cw, qw, cw), spot=n)

    wide = ratio * head
    dq, dk, dv, dgain_q, dgain_k, branch = pl.pallas_call(
        functools.partial(attend_back, n),
        grid=(kheads, blocks),
        out_shape=(
            shape((group, qw), BF),
            shape((group, kw), BF),
            shape((group, kw), BF),
            shape((8, head), F32),
            shape((8, head), F32),
            shape((rows, width), F32),
        ),
        in_specs=[
            pl.BlockSpec((256, wide), lambda h, b: (b, h)),
            pl.BlockSpec((256, wide), lambda h, b: (b, h)),
            pl.BlockSpec((group, head), lambda h, b: (0, h)),
            pl.BlockSpec((head, group), lambda h, b: (h, 0)),
            pl.BlockSpec((group, head), lambda h, b: (0, h)),
            pl.BlockSpec((group, head), lambda h, b: (0, h)),
            pl.BlockSpec((256, width), lambda h, b: (b, 0)),
            pl.BlockSpec((wide, width), lambda h, b: (h, 0)),
            pl.BlockSpec((8, 256), lambda h, b: (0, b)),
            pl.BlockSpec((8, 256), lambda h, b: (0, b)),
            pl.BlockSpec((8, 256), lambda h, b: (0, b)),
            pl.BlockSpec((256, head), lambda h, b: (b, 0)),
            pl.BlockSpec((256, head), lambda h, b: (b, 0)),
            whole((group, head)),
            whole((group, head)),
            whole((1, head)),
            whole((1, head)),
            VMEM,
        ],
        out_specs=(
            pl.BlockSpec((256, wide), lambda h, b: (b, h)),
            pl.BlockSpec((group, head), lambda h, b: (0, h)),
            pl.BlockSpec((group, head), lambda h, b: (0, h)),
            whole((8, head)),
            whole((8, head)),
            VMEM,
        ),
        scratch_shapes=[pltpu.VMEM((group, head), F32), pltpu.VMEM((group, head), F32)]
        + slots
        + sems,
        compiler_params=comm_params(5),
    )(
        q, qraw, k, kt, v, kraw, dz, wo, lse, low, high, cos, sin, cos, sin, gain_q, gain_k,
        part_y.reshape(n, rows, width),
    )
    output = (x2 + branch).astype(BF)

    att_grad = product(n1, dq, dk, dv, into=wo_grad, dims=wo_grad.shape)
    att_share = lax.psum_scatter(
        after(att_grad, gu_share), "fsdp", scatter_dimension=1, tiled=True
    )

    part_n1 = pl.pallas_call(
        qkv_back,
        grid=(blocks,),
        out_shape=shape((group, width), BF),
        in_specs=[
            by_rows(256, qw),
            by_rows(256, kw),
            by_rows(256, kw),
            whole((width, cw)),
        ],
        out_specs=by_rows(256, width),
        compiler_params=plain_params(),
    )(after(dq, att_grad), dk, dv, w_att)
    back_one, dgain_one = pl.pallas_call(
        functools.partial(input_stage, n),
        out_shape=(shape((rows, width), F32), shape((8, width), F32)),
        in_specs=[VMEM] * 3,
        out_specs=(VMEM, VMEM),
        scratch_shapes=slots + sems,
        compiler_params=comm_params(10),
    )(part_n1.reshape(n, rows, width), tokens, gain_one)
    input_grad = (dx2 + back_one).astype(BF)

    def owned(row, count):
        cut = row.reshape(n, nf, 1, count)
        return jnp.pad(cut, ((0, 0), (0, 0), (0, 0), (0, 128 - count)))

    blocks_of = jnp.concatenate(
        [
            owned(dgain_one[0], own_gain),
            owned(dgain_two[0], own_gain),
            owned(dgain_q[0], own_head),
            owned(dgain_k[0], own_head),
            jnp.zeros((n, nf, 4, 128), F32),
        ],
        axis=2,
    ).transpose(1, 0, 2, 3)
    gains = pl.pallas_call(
        functools.partial(gains_back, n, nf),
        out_shape=shape((8, 128), F32),
        in_specs=[VMEM],
        out_specs=VMEM,
        scratch_shapes=[
            pltpu.VMEM((nf - 1, n, 8, 128), F32),
            pltpu.VMEM((n, 8, 128), F32),
            pltpu.VMEM((n - 1, 8, 128), F32),
            dma(n + nf - 2),
            dma(n + nf - 2),
            pltpu.SemaphoreType.DMA,
        ],
        compiler_params=comm_params(7),
    )(blocks_of)

    def swap(number, *arrays):
        count = len(arrays)
        return pl.pallas_call(
            functools.partial(exchange, n, count),
            out_shape=tuple(shape((n,) + a.shape[1:], BF) for a in arrays),
            in_specs=[ANY] * count,
            out_specs=(ANY,) * count,
            scratch_shapes=[dma(count * (n - 1)), dma(count * (n - 1)), dma(count)],
            compiler_params=comm_params(number),
        )(*arrays)

    def spread(arrays, pieces):
        ins = [pl.BlockSpec((1, depth, a.shape[2]), lambda i: (i, 0, 0)) for a in arrays]
        outs = [by_cols(depth, count) for _, _, count in pieces]
        shapes = [shape((depth, n * count), F32) for _, _, count in pieces]
        return pl.pallas_call(
            functools.partial(widen, pieces),
            grid=(n,),
            out_shape=tuple(shapes),
            in_specs=ins,
            out_specs=tuple(outs),
            compiler_params=plain_params(),
        )(*arrays)

    gu_mine, dn_mine = swap(6, gu_share, after(dn_share, gains))
    gate_grad, up_grad, down_grad = spread(
        [gu_mine, dn_mine], [(0, 0, fw), (0, fw, fw), (1, 0, fw)]
    )
    wide_grads = (gate_grad, up_grad, down_grad.T)
    wo_out = att_share[n:].transpose(1, 0, 2).reshape(depth, width).astype(F32)
    (att_mine,) = swap(9, after(att_share, (gains, wide_grads, input_grad, output)))
    wq_grad, wk_grad, wv_grad = spread(
        [att_mine], [(0, 0, qw), (0, qw, kw), (0, qw + kw, kw)]
    )

    return (
        output,
        input_grad,
        gains[0, :own_gain],
        wq_grad,
        wk_grad,
        wv_grad,
        gains[2, :own_head],
        gains[3, :own_head],
        wo_out,
        gains[1, :own_gain],
    ) + wide_grads


def solution(mesh):
    return jax.shard_map(
        functools.partial(shards, mesh.shape["seq"], mesh.shape["fsdp"]),
        mesh=mesh,
        in_specs=(
            P(("fsdp", "seq"), None),
            P("fsdp", None),
            P("fsdp", None),
            P("fsdp", None),
            P(("seq", "fsdp")),
            P(("seq", "fsdp"), None),
            P(("seq", "fsdp"), None),
            P(("seq", "fsdp"), None),
            P(("seq", "fsdp")),
            P(("seq", "fsdp")),
            P(("seq", "fsdp"), None),
            P(("seq", "fsdp")),
            P(("seq", "fsdp"), None),
            P(("seq", "fsdp"), None),
            P(None, ("seq", "fsdp")),
            P(("fsdp", "seq"), None),
        ),
        out_specs=(
            P(("fsdp", "seq"), None),
            P(("fsdp", "seq"), None),
            P(("seq", "fsdp")),
            P(("seq", "fsdp"), None),
            P(("seq", "fsdp"), None),
            P(("seq", "fsdp"), None),
            P(("seq", "fsdp")),
            P(("seq", "fsdp")),
            P(("seq", "fsdp"), None),
            P(("seq", "fsdp")),
            P(("seq", "fsdp"), None),
            P(("seq", "fsdp"), None),
            P(None, ("seq", "fsdp")),
        ),
        check_vma=False,
    )
```

```python
import functools

import jax
import jax.numpy as jnp
import numpy as np
from jax import lax
from jax.experimental import pallas as pl
from jax.experimental.pallas import tpu as pltpu
from jax.sharding import PartitionSpec as P

epsilon = 1e-06
theta = 1000000.0
masked_score = -1e30
log2e = 1.4426950408889634

MESH = pl.DeviceIdType.MESH
ANY = pl.BlockSpec(memory_space=pl.ANY)
VMEM = pl.BlockSpec(memory_space=pltpu.VMEM)
BF = jnp.bfloat16
F32 = jnp.float32
LIMIT = 60 * 1024 * 1024


def dot(a, b):
    return jnp.dot(a, b, preferred_element_type=F32)


def dot_nt(a, b):
    return lax.dot_general(a, b, (((1,), (1,)), ((), ())), preferred_element_type=F32)


def dot_tn(a, b):
    return lax.dot_general(a, b, (((0,), (0,)), ((), ())), preferred_element_type=F32)


def shape(dims, dtype):
    return jax.ShapeDtypeStruct(dims, dtype)


def comm_params(number):
    return pltpu.CompilerParams(
        collective_id=number, has_side_effects=True, vmem_limit_bytes=LIMIT
    )


def plain_params():
    return pltpu.CompilerParams(vmem_limit_bytes=LIMIT)


def remote(src, dst, send, recv, axis, index):
    return pltpu.make_async_remote_copy(
        src_ref=src,
        dst_ref=dst,
        send_sem=send,
        recv_sem=recv,
        device_id={axis: index},
        device_id_type=MESH,
    )


def greet(places):
    barrier = pltpu.get_barrier_semaphore()
    for axis, index in places:
        pl.semaphore_signal(barrier, inc=1, device_id={axis: index}, device_id_type=MESH)
    pl.semaphore_wait(barrier, len(places))


def others(axis, n):
    me = lax.axis_index(axis)
    return [(axis, lax.rem(me + j, n)) for j in range(1, n)]


def square(me):
    return me + 1 - 2 * lax.rem(me, 2), lax.rem(me + 2, 4), 3 - me


def ring_places(n):
    me = lax.axis_index("seq")
    if n == 4:
        across, along, _ = square(me)
        return [("seq", across), ("seq", along)]
    return others("seq", n)


def gather_copies(n):
    return 6 if n == 4 else n - 1


def gather_parts(n, own, out, send, recv, local):
    me = lax.axis_index("seq")
    keep = pltpu.make_async_copy(own, out.at[me], local)
    half = own.shape[0] // 2
    low, high = pl.ds(0, half), pl.ds(half, half)
    if n == 4:
        across, along, _ = square(me)
        moves = [
            (own.at[low], out.at[me, low], across),
            (own.at[high], out.at[me, high], along),
            (own.at[high], out.at[me, high], across),
            (own.at[low], out.at[me, low], along),
            (out.at[across, low], out.at[across, low], along),
            (out.at[along, high], out.at[along, high], across),
        ]
    else:
        moves = [(own, out.at[me], lax.rem(me + j, n)) for j in range(1, n)]
    copies = [
        remote(src, dst, send.at[i], recv.at[i], "seq", to)
        for i, (src, dst, to) in enumerate(moves)
    ]

    def start():
        for copy in copies[:4]:
            copy.start()
        if n != 4:
            for copy in copies[4:]:
                copy.start()
        keep.start()

    def relay():
        if n == 4:
            copies[0].wait_recv()
            copies[4].start()
            copies[1].wait_recv()
            copies[5].start()

    def finish():
        for copy in copies[2:] if n == 4 else copies:
            copy.wait_recv()
        for copy in copies:
            copy.wait_send()
        keep.wait()

    return start, relay, finish


def gather(n, own, out, send, recv, local):
    for part in gather_parts(n, own, out, send, recv, local):
        part()


def scatter_slots(n):
    return 4 if n == 4 else n - 1


def scatter_sum(n, part, slots, stage, send, recv, finish):
    start, relay, total = scatter_parts(n, part, slots, stage, send, recv, finish)
    start()
    relay()
    total()


def scatter_parts(n, part, slots, stage, send, recv, finish):
    me = lax.axis_index("seq")
    rows = part.shape[1]
    half = rows // 2
    low, high = pl.ds(0, half), pl.ds(half, half)
    if n == 4:
        across, along, corner = square(me)
        moves = [
            (part.at[corner, low], slots.at[2, low], along),
            (part.at[corner, high], slots.at[2, high], across),
            (part.at[across, high], slots.at[0, high], across),
            (part.at[along, low], slots.at[1, low], along),
            (stage.at[low], slots.at[0, low], across),
            (stage.at[high], slots.at[1, high], along),
        ]
        count = 2
    else:
        moves = []
        for j in range(1, n):
            to = lax.rem(me + j, n)
            moves.append((part.at[to], slots.at[j - 1], to))
        count = n - 1
    copies = [
        remote(src, dst, send.at[i], recv.at[i], "seq", to)
        for i, (src, dst, to) in enumerate(moves)
    ]

    def start(begin=0, end=4):
        for copy in copies[begin:end] if n == 4 else copies:
            copy.start()

    def relay():
        if n == 4:
            copies[0].wait_recv()
            stage[low] = (part[across, low].astype(F32) + slots[2, low].astype(F32)).astype(BF)
            copies[4].start()
            copies[1].wait_recv()
            stage[high] = (part[along, high].astype(F32) + slots[2, high].astype(F32)).astype(BF)
            copies[5].start()

    def total():
        for copy in copies[2:] if n == 4 else copies:
            copy.wait_recv()
        step = 32

        def chunk(number, carry):
            at = pl.ds(pl.multiple_of(number * step, step), step)
            value = part[me, at].astype(F32)
            for slot in range(count):
                value += slots[slot, at].astype(F32)
            finish(at, value)
            return carry

        lax.fori_loop(0, rows // step, chunk, 0)
        for copy in copies:
            copy.wait_send()

    return start, relay, total


def inverse_rms(values):
    return lax.rsqrt(jnp.mean(values * values, axis=-1, keepdims=True) + epsilon)


def norm_back(values, gain, grad):
    inverse = inverse_rms(values)
    scaled = grad * gain
    back = inverse * scaled - values * (
        inverse * inverse * inverse * jnp.mean(scaled * values, axis=-1, keepdims=True)
    )
    return back, jnp.sum(grad * values * inverse, axis=0, keepdims=True)


def attention_weights_out(n, wq, wk, wv, out, send, recv, local):
    me = lax.axis_index("seq")
    greet(others("seq", n))
    widths = [wq.shape[1] // n, wk.shape[1] // n, wv.shape[1] // n]
    begins = [0, widths[0], widths[0] + widths[1]]
    copies = []
    for j in range(1, n):
        to = lax.rem(me + j, n)
        for i, ref in enumerate((wq, wk, wv)):
            columns = pl.ds(pl.multiple_of(to * widths[i], 128), widths[i])
            copies.append(
                remote(
                    ref.at[:, columns],
                    out.at[me, :, pl.ds(begins[i], widths[i])],
                    send.at[3 * j - 3 + i],
                    recv.at[3 * j - 3 + i],
                    "seq",
                    to,
                )
            )
    for i, ref in enumerate((wq, wk, wv)):
        columns = pl.ds(pl.multiple_of(me * widths[i], 128), widths[i])
        copies.append(
            pltpu.make_async_copy(
                ref.at[:, columns], out.at[me, :, pl.ds(begins[i], widths[i])], local.at[i]
            )
        )
    for copy in copies:
        copy.start()
    for copy in copies:
        copy.wait()


def start_columns(n, views, send, recv, local):
    me = lax.axis_index("seq")
    width = views[0][0].shape[1] // n
    copies, keeps = [], []
    for i, (ref, out, place) in enumerate(views):
        for j in range(1, n):
            to = lax.rem(me + j, n)
            columns = pl.ds(pl.multiple_of(to * width, 128), width)
            k = i * (n - 1) + j - 1
            copies.append(
                remote(
                    ref.at[:, columns],
                    out.at[me, :, pl.ds(place * width, width)],
                    send.at[k],
                    recv.at[k],
                    "seq",
                    to,
                )
            )
        columns = pl.ds(pl.multiple_of(me * width, 128), width)
        keeps.append(
            pltpu.make_async_copy(
                ref.at[:, columns], out.at[me, :, pl.ds(place * width, width)], local.at[i]
            )
        )
    for copy in copies + keeps:
        copy.start()
    return copies + keeps


def gate_up_out(n, nf, wg, wu, gains, gu, all_gains, seen, send, recv, local, gsend, grecv, glocal):
    me, spot = lax.axis_index("seq"), lax.axis_index("fsdp")
    greet(others("seq", n) + others("fsdp", nf))
    small = []
    for j in range(1, n):
        to = lax.rem(me + j, n)
        small.append(
            remote(gains, seen.at[me], gsend.at[j - 1], grecv.at[j - 1], "seq", to)
        )
    keep = pltpu.make_async_copy(gains, seen.at[me], glocal.at[0])
    for copy in small + [keep]:
        copy.start()
    copies = start_columns(n, [(wg, gu, 0), (wu, gu, 1)], send, recv, local)
    for copy in small + [keep]:
        copy.wait()
    wide = [pltpu.make_async_copy(seen, all_gains.at[spot], glocal.at[1])]
    for j in range(1, nf):
        to = lax.rem(spot + j, nf)
        k = n + j - 2
        wide.append(
            remote(seen, all_gains.at[spot], gsend.at[k], grecv.at[k], "fsdp", to)
        )
    for copy in wide:
        copy.start()
    for copy in copies + wide:
        copy.wait()


def line_gather(own, out, send, recv, local, between):
    spot = lax.axis_index("fsdp")
    z = lax.div(spot, 2)
    twin = spot + 1 - 2 * lax.rem(spot, 2)
    keep = pltpu.make_async_copy(own, out.at[spot], local)
    keep.start()

    def up(k):
        block = spot - 2 * k
        return remote(
            own if k == 0 else out.at[block], out.at[block], send.at[k], recv.at[k], "fsdp", spot + 2
        )

    def down(k):
        block = spot + 2 * k
        return remote(
            own if k == 0 else out.at[block],
            out.at[block],
            send.at[3 + k],
            recv.at[3 + k],
            "fsdp",
            spot - 2,
        )

    def over(offset):
        block = spot + 2 * offset
        return remote(
            own if offset == 0 else out.at[block],
            out.at[block],
            send.at[6 + lax.div(block, 2)],
            recv.at[6 + lax.div(block, 2)],
            "fsdp",
            twin,
        )

    def from_twin(offset):
        block = twin + 2 * offset
        return remote(
            own, out.at[block], send.at[6 + lax.div(block, 2)], recv.at[6 + lax.div(block, 2)], "fsdp", twin
        )

    @pl.when(z < 3)
    def _():
        up(0).start()

    @pl.when(z > 0)
    def _():
        down(0).start()

    over(0).start()
    between()
    for k in range(1, 4):

        @pl.when(z >= k)
        def _():
            up(k - 1).wait_recv()
            if k < 3:

                @pl.when(z < 3)
                def _():
                    up(k).start()

            over(-k).start()

        @pl.when(z + k <= 3)
        def _():
            down(k - 1).wait_recv()
            if k < 3:

                @pl.when(z > 0)
                def _():
                    down(k).start()

            over(k).start()

    from_twin(0).wait_recv()
    over(0).wait_send()
    for k in range(1, 4):

        @pl.when(z >= k)
        def _():
            from_twin(-k).wait_recv()
            over(-k).wait_send()

        @pl.when(z + k <= 3)
        def _():
            from_twin(k).wait_recv()
            over(k).wait_send()

    for k in range(3):

        @pl.when((z >= k) & (z < 3))
        def _():
            up(k).wait_send()

        @pl.when((z + k <= 3) & (z > 0))
        def _():
            down(k).wait_send()

    keep.wait()


def greet_line(places):
    spot = lax.axis_index("fsdp")
    z = lax.div(spot, 2)
    twin = spot + 1 - 2 * lax.rem(spot, 2)
    barrier = pltpu.get_barrier_semaphore()
    for axis, index in places + [("fsdp", twin)]:
        pl.semaphore_signal(barrier, inc=1, device_id={axis: index}, device_id_type=MESH)

    @pl.when(z < 3)
    def _():
        pl.semaphore_signal(barrier, inc=1, device_id={"fsdp": spot + 2}, device_id_type=MESH)

    @pl.when(z > 0)
    def _():
        pl.semaphore_signal(barrier, inc=1, device_id={"fsdp": spot - 2}, device_id_type=MESH)

    inner = (z < 3).astype(jnp.int32) + (z > 0).astype(jnp.int32)
    pl.semaphore_wait(barrier, len(places) + 1 + inner)


def entry_stage(n, nf, line, own_gain, x, wd, w_out, gains, lengths, starts, sizes, freq, xg, dn, wo, gain_one, gain_two, gain_q, gain_k, cos, sin, low, high, send, recv, local, wsend, wrecv, wlocal, lsend, lrecv, llocal):
    if line:
        greet_line(others("seq", n))
    else:
        greet(others("seq", n))
    start, relay, finish = gather_parts(n, x, xg, send, recv, local)
    start()
    copies = start_columns(n, [(wd, dn, 0)], wsend, wrecv, wlocal)

    def tables():
        per = 128 // own_gain
        for row in range(n * nf // per):
            seq, first = row * per // nf, row * per % nf
            one = gains[first, seq, 0:1, :]
            two = gains[first, seq, 1:2, :]
            for f in range(first + 1, first + per):
                one += gains[f, seq, 0:1, :]
                two += gains[f, seq, 1:2, :]
            gain_one[:, row * 128 : row * 128 + 128] = one
            gain_two[:, row * 128 : row * 128 + 128] = two
        total = jnp.zeros((8, 128), F32)
        for f in range(nf):
            for seq in range(n):
                total += gains[f, seq]
        gain_q[...] = total[2:3, :]
        gain_k[...] = total[3:4, :]

        group = cos.shape[0]
        border_one = lengths[0, 0]
        border_two = border_one + lengths[0, 1]

        def begin_of(places):
            later = jnp.where(places >= border_one, border_one, 0)
            return jnp.where(places >= border_two, border_two, later)

        step = 128
        lane = lax.broadcasted_iota(jnp.int32, (step, 128), 1)

        def turn(number, carry):
            at = pl.ds(pl.multiple_of(number * step, step), step)
            places = lax.broadcasted_iota(jnp.int32, (step, 128), 0) + number * step
            angle = (places - begin_of(places)).astype(F32) * freq[...]
            cos[at, :] = jnp.cos(angle)
            sine = jnp.sin(angle)
            sin[at, :] = jnp.where(lane < 64, -sine, sine)
            return carry

        lax.fori_loop(0, group // step, turn, 0)
        places = lax.broadcasted_iota(jnp.int32, (8, group), 1)
        end = jnp.where(places >= border_one, border_two, border_one)
        end = jnp.where(places >= border_two, group, end)
        picture = jnp.zeros_like(places)
        for i in range(starts.shape[1]):
            first, count = starts[0, i], sizes[0, i]
            inside = (places >= first) & (places < first + count)
            picture = jnp.where(inside, jnp.maximum(picture, first + count), picture)
        low[...] = begin_of(places)
        high[...] = jnp.maximum(places, jnp.minimum(picture, end) - 1)

    if line:
        line_gather(w_out, wo, lsend, lrecv, llocal, relay)
    else:
        keep = pltpu.make_async_copy(w_out, wo.at[0], llocal)
        keep.start()
        relay()
        keep.wait()
    tables()
    finish()
    for copy in copies:
        copy.wait()


def half_gather(n, begin, cot, cg, send, recv, local):
    at = pl.ds(begin, cot.shape[0] // 2)
    start, relay, finish = gather_parts(n, cot.at[at], cg.at[:, at], send, recv, local)
    step, steps = pl.program_id(0), pl.num_programs(0)

    @pl.when(step == 0)
    def _():
        greet(ring_places(n))
        start()

    @pl.when(step == steps - 1)
    def _():
        relay()

    return finish


def project(n, x_ref, gain_ref, w_ref, gq_ref, gk_ref, cos_ref, sin_ref, cot, n1_ref, qraw_ref, kraw_ref, q_ref, k_ref, v_ref, kt_ref, vt_ref, cg, send, recv, local):
    finish_half = half_gather(n, 0, cot, cg, send, recv, local)
    x = x_ref[...].astype(F32)
    normed = (x * inverse_rms(x) * gain_ref[...]).astype(BF)
    n1_ref[...] = normed
    full = dot(normed, w_ref[...])
    qw, kw = q_ref.shape[1], k_ref.shape[1]
    cos, sin = cos_ref[...], sin_ref[...]

    def prep(head, gain):
        u = head * inverse_rms(head) * gain
        return u * cos + pltpu.roll(u, 64, 1) * sin

    qraw_ref[...] = full[:, :qw]
    kraw_ref[...] = full[:, qw : qw + kw]
    v = full[:, qw + kw :]
    v_ref[...] = v.astype(BF)
    vt_ref[...] = v.T.astype(BF)
    for h in range(qw // 128):
        q_ref[:, h * 128 : h * 128 + 128] = prep(
            full[:, h * 128 : h * 128 + 128], gq_ref[...]
        ).astype(BF)
    for h in range(kw // 128):
        turned = prep(full[:, qw + h * 128 : qw + h * 128 + 128], gk_ref[...])
        k_ref[:, h * 128 : h * 128 + 128] = turned.astype(BF)
        kt_ref[h * 128 : h * 128 + 128, :] = turned.T.astype(BF)

    @pl.when(pl.program_id(0) == pl.num_programs(0) - 1)
    def _():
        finish_half()


def bias_of(low_ref, high_ref, keys):
    key = lax.broadcasted_iota(jnp.int32, (keys, low_ref.shape[1]), 0)
    fine = (key >= low_ref[0:1, :]) & (key <= high_ref[0:1, :])
    return jnp.where(fine, 0.0, masked_score)


def attend(n, q_ref, k_ref, vt_ref, wo_ref, low_ref, high_ref, cot, cg_half, attn_ref, lse_ref, part_ref, cg, bias, send, recv, local):
    finish_half = half_gather(n, cot.shape[0] // 2, cot, cg, send, recv, local)
    keys = k_ref.shape[0]
    bias[...] = bias_of(low_ref, high_ref, keys)
    heads = q_ref.shape[1] // 128
    ratio = heads // (k_ref.shape[1] // 128)
    factor = 128 ** (-0.5) * log2e
    for h in range(heads):
        kv = h // ratio
        scores = dot_nt(
            k_ref[:, kv * 128 : kv * 128 + 128], q_ref[:, h * 128 : h * 128 + 128]
        )
        scores = scores * factor + bias[...]
        top = jnp.max(scores, axis=0, keepdims=True)
        probs = jnp.exp2(scores - top)
        total = jnp.sum(probs, axis=0, keepdims=True)
        mixed = dot(vt_ref[kv * 128 : kv * 128 + 128, :], probs.astype(BF))
        lse_ref[h : h + 1, :] = top + jnp.log2(total)
        attn_ref[:, h * 128 : h * 128 + 128] = (mixed / total).T.astype(BF)
    part_ref[...] = dot(attn_ref[...], wo_ref[...]).astype(BF)

    @pl.when(pl.program_id(0) == pl.num_programs(0) - 1)
    def _():
        finish_half()


def middle_stage(n, part, x, gain, x2, n2, slots, stage, own, send, recv, asend, arecv, local):
    greet(ring_places(n))

    def finish(at, total):
        value = x[at].astype(F32) + total
        x2[at] = value
        own[at] = (value * inverse_rms(value) * gain[...]).astype(BF)

    scatter_sum(n, part, slots, stage, send, recv, finish)
    gather(n, own, n2, asend, arecv, local)


def ffn_forward(n2_ref, wg_ref, wu_ref, gate_ref, up_ref, hidden_ref):
    gate = dot(n2_ref[...], wg_ref[...])
    up = dot(n2_ref[...], wu_ref[...])
    gate_ref[...] = gate
    up_ref[...] = up
    hidden_ref[...] = (gate * jax.nn.sigmoid(gate) * up).astype(BF)


def ffn_back(cot_ref, wd_ref, gate_ref, up_ref, dgate_ref, dup_ref):
    dh = dot(cot_ref[...], wd_ref[...])
    gate = gate_ref[...]
    s = jax.nn.sigmoid(gate)
    dgate_ref[...] = (dh * up_ref[...] * (s * (1.0 + gate * (1.0 - s)))).astype(BF)
    dup_ref[...] = (dh * (gate * s)).astype(BF)


def two_nt(a_ref, b_ref, wa_ref, wb_ref, out_ref):
    out_ref[...] = (dot_nt(a_ref[...], wa_ref[...]) + dot_nt(b_ref[...], wb_ref[...])).astype(BF)


def spread_rows(row, out):
    for i in range(out.shape[0]):
        out[i : i + 1, :] = row[:, i * 128 : i * 128 + 128]


def back_stage(n, part, x2, cot, gain, hidden_far, dn_far, dx2, dz, dgain, part_y, slots, stage, own, send, recv, asend, arecv, local, row, hidden, dn, load):
    greet(ring_places(n))
    loads = [
        pltpu.make_async_copy(hidden_far, hidden, load.at[0]),
        pltpu.make_async_copy(dn_far, dn, load.at[1]),
    ]
    for copy in loads:
        copy.start()
    row[...] = jnp.zeros_like(row)
    rows, width = x2.shape
    step = 512

    def forward(to, carry):
        at = pl.ds(pl.multiple_of(to * rows, rows), rows)

        def columns(number, carry):
            span = pl.ds(pl.multiple_of(number * step, step), step)
            part_y[to, :, span] = dot_nt(hidden[at, :], dn[span, :]).astype(BF)
            return carry

        return lax.fori_loop(0, width // step, columns, carry)

    def finish(at, total):
        back, dg = norm_back(x2[at], gain[...], total)
        value = cot[at].astype(F32) + back
        dx2[at] = value
        own[at] = value.astype(BF)
        row[...] += dg

    start, relay, total = scatter_parts(n, part, slots, stage, send, recv, finish)
    start()
    for copy in loads:
        copy.wait()
    relay()
    lax.fori_loop(0, n // 2, forward, 0)
    total()
    start, relay, end = gather_parts(n, own, dz, asend, arecv, local)
    start()
    spread_rows(row[...], dgain)
    relay()
    lax.fori_loop(n // 2, n, forward, 0)
    end()


def input_stage(n, dq, dk, dv, w, x, gain, out, dgain, part, slots, stage, send, recv, row):
    greet(ring_places(n))
    row[...] = jnp.zeros_like(row)
    me = lax.axis_index("seq")
    rows, width = x.shape
    qw, kw = dq.shape[1], dk.shape[1]
    step = 512

    def block(to):
        at = pl.ds(pl.multiple_of(to * rows, rows), rows)

        def columns(number, carry):
            span = pl.ds(pl.multiple_of(number * step, step), step)
            value = dot_nt(dq[at, :], w[span, pl.ds(0, qw)])
            value += dot_nt(dk[at, :], w[span, pl.ds(qw, kw)])
            value += dot_nt(dv[at, :], w[span, pl.ds(qw + kw, kw)])
            part[to, :, span] = value.astype(BF)
            return carry

        lax.fori_loop(0, width // step, columns, 0)

    def finish(at, total):
        back, dg = norm_back(x[at].astype(F32), gain[...], total)
        out[at] = back
        row[...] += dg

    start, relay, total = scatter_parts(n, part, slots, stage, send, recv, finish)
    if n == 4:
        across, along, corner = square(me)
        block(corner)
        start(0, 2)
        block(across)
        start(2, 3)
        block(along)
        start(3, 4)
        block(me)
    else:
        for j in range(n):
            block(lax.rem(me + j, n))
        start()
    relay()
    total()
    spread_rows(row[...], dgain)


def attend_back(n, q_ref, qraw_ref, k_ref, kt_ref, v_ref, kraw_ref, dz_ref, wo_ref, lse_ref, low_ref, high_ref, cq_ref, sq_ref, ck_ref, sk_ref, gq_ref, gk_ref, part, dq_ref, dk_ref, dv_ref, dgq_ref, dgk_ref, out, dk_sum, dv_sum, slots, stage, send, recv):
    kv, block = pl.program_id(0), pl.program_id(1)
    keys = k_ref.shape[0]
    ratio = q_ref.shape[1] // 128
    scale = 128 ** (-0.5)

    def finish(at, total):
        out[at] = total

    start, relay, total = scatter_parts(n, part, slots, stage, send, recv, finish)
    steps = pl.num_programs(0) * pl.num_programs(1)
    step = kv * pl.num_programs(1) + block

    @pl.when(step == 0)
    def _():
        greet(ring_places(n))
        start()
        dgq_ref[...] = jnp.zeros_like(dgq_ref)
        dgk_ref[...] = jnp.zeros_like(dgk_ref)

    @pl.when(step == steps // 2)
    def _():
        relay()

    @pl.when(block == 0)
    def _():
        dk_sum[...] = jnp.zeros_like(dk_sum)
        dv_sum[...] = jnp.zeros_like(dv_sum)

    bias = bias_of(low_ref, high_ref, keys)
    dattn = dot_nt(dz_ref[...], wo_ref[...]).astype(BF)

    def prep_back(grad, raw, gain, cos, sin):
        du = grad * cos - pltpu.roll(grad, 64, 1) * sin
        return norm_back(raw, gain, du)

    for r in range(ratio):
        span = slice(r * 128, r * 128 + 128)
        qh, dah = q_ref[:, span], dattn[:, span]
        lse = lse_ref[pl.ds(kv * ratio + r, 1), :]
        scores = dot_nt(k_ref[...], qh) * (scale * log2e) + bias
        probs = jnp.exp2(scores - lse)
        dprobs = dot_nt(v_ref[...], dah)
        delta = jnp.sum(probs * dprobs, axis=0, keepdims=True)
        ds = (probs * (dprobs - delta)).astype(BF)
        dv_sum[...] += dot(probs.astype(BF), dah)
        dk_sum[...] += dot(ds, qh)
        dqr = dot(kt_ref[...], ds).T * scale
        back, dg = prep_back(dqr, qraw_ref[:, span], gq_ref[...], cq_ref[...], sq_ref[...])
        dq_ref[:, span] = back.astype(BF)
        dgq_ref[0:1] += dg

    @pl.when(block == pl.num_programs(1) - 1)
    def _():
        dv_ref[...] = dv_sum[...].astype(BF)
        back, dg = prep_back(
            dk_sum[...] * scale, kraw_ref[...], gk_ref[...], ck_ref[...], sk_ref[...]
        )
        dk_ref[...] = back.astype(BF)
        dgk_ref[0:1] += dg

    @pl.when(step == steps - 1)
    def _():
        total()


def gradient(counts, kept, *refs):
    a_ref, bs = refs[0], refs[1 : 1 + len(counts)]
    out_ref, turned, both, got, send, recv = refs[1 + len(counts) + kept :]
    step = pl.program_id(0)
    tiles = sum(counts)
    core = lax.rem(lax.axis_index("fsdp"), 2)
    twin = lax.axis_index("fsdp") + 1 - 2 * core
    blocks, depth, tile = both.shape[1], both.shape[3], both.shape[4]
    piece = min(512, turned.shape[0])
    part = piece // (2 * depth)

    def move(number):
        slot = lax.rem(number, 2)
        return remote(
            both.at[slot, :, 1 - core], got.at[number], send.at[number], recv.at[number], "fsdp", twin
        )

    @pl.when(step == 0)
    def _():
        greet([("fsdp", twin)])
        turned[...] = a_ref[...].T

    begin = 0
    for b_ref, count in zip(bs, counts):

        @pl.when((step >= begin) & (step < begin + count))
        def _(b_ref=b_ref):
            slot = lax.rem(step, 2)

            @pl.when(step >= 2)
            def _():
                move(step - 2).wait_send()

            for i in range(turned.shape[0] // piece):
                rows = dot(turned[i * piece : i * piece + piece, :], b_ref[...]).astype(BF)
                both[slot, i * part : i * part + part] = rows.reshape(part, 2, depth, tile)
            move(step).start()

        begin += count

    @pl.when(step >= 1)
    def _():
        last = step - 1
        move(last).wait_recv()
        lead = out_ref.shape[0]
        inner = blocks // lead
        for i in range(lead):
            own = both[lax.rem(last, 2), i * inner : i * inner + inner, core]
            other = got[last, i * inner : i * inner + inner]
            total = (own.astype(F32) + other.astype(F32)).astype(BF)
            out_ref[i] = total.reshape(inner * depth, tile)

    @pl.when(step == tiles)
    def _():
        if tiles >= 2:
            move(tiles - 2).wait_send()
        move(tiles - 1).wait_send()


def exchange_copies(n, ins, outs, send, recv, local):
    me = lax.axis_index("seq")
    copies = []
    for i, (source, out) in enumerate(zip(ins, outs)):
        for j in range(1, n):
            to = lax.rem(me + j, n)
            k = i * (n - 1) + j - 1
            copies.append(
                remote(source.at[to], out.at[me], send.at[k], recv.at[k], "seq", to)
            )
        copies.append(pltpu.make_async_copy(source.at[me], out.at[me], local.at[i]))
    for copy in copies:
        copy.start()
    return copies


def exchange(n, source, out, send, recv, local):
    greet(others("seq", n))
    for copy in exchange_copies(n, [source], [out], send, recv, local):
        copy.wait()


def widen(pieces, *refs):
    ins, outs = refs[: -len(pieces)], refs[-len(pieces) :]
    for out, (i, begin, count) in zip(outs, pieces):
        out[...] = ins[i][0, :, begin : begin + count].astype(F32)


def exchange_gains(n, nf, gu, dn, one, two, gq, gk, gu_out, dn_out, out, part, wide, mid, seen, send, recv, local, gsend, grecv):
    me, spot = lax.axis_index("seq"), lax.axis_index("fsdp")
    greet(others("seq", n) + others("fsdp", nf))
    part[...] = jnp.zeros_like(part)
    count = one.shape[0]
    per = n * nf // count
    for f in range(nf):
        for seq in range(n):
            row = (seq * nf + f) // per
            part[f, seq, 0:1] = one[row : row + 1]
            part[f, seq, 1:2] = two[row : row + 1]
            part[f, seq, 2:3] = gq[0:1]
            part[f, seq, 3:4] = gk[0:1]
    far = []
    for j in range(1, nf):
        to = lax.rem(spot + j, nf)
        far.append(
            remote(part.at[to], wide.at[j - 1], gsend.at[j - 1], grecv.at[j - 1], "fsdp", to)
        )
    for copy in far:
        copy.start()
    copies = exchange_copies(n, [gu, dn], [gu_out, dn_out], send, recv, local)
    for copy in far:
        copy.wait_recv()
    total = part[spot]
    for j in range(nf - 1):
        total += wide[j]
    mid[...] = total
    near = []
    for j in range(1, n):
        to = lax.rem(me + j, n)
        k = nf + j - 2
        near.append(remote(mid.at[to], seen.at[j - 1], gsend.at[k], grecv.at[k], "seq", to))
    for copy in near:
        copy.start()
    for copy in near:
        copy.wait_recv()
    result = mid[me]
    for j in range(n - 1):
        result += seen[j]
    out[...] = result
    for copy in far + near:
        copy.wait_send()
    for copy in copies:
        copy.wait()


def after(value, done):
    return lax.optimization_barrier((value, done))[0]


def dma(count):
    return pltpu.SemaphoreType.DMA((count,))


def shards(
    n,
    nf,
    tokens,
    seq_lengths,
    pic_starts,
    pic_lengths,
    norm1_gain,
    w_query,
    w_key,
    w_value,
    q_gain,
    k_gain,
    w_out,
    norm2_gain,
    w_gate,
    w_up,
    w_down,
    cotangent,
):
    rows, width = tokens.shape
    group = rows * n
    depth = w_query.shape[0]
    head = q_gain.shape[0] * n * nf
    qw, kw = w_query.shape[1] // n, w_key.shape[1] // n
    cw = qw + 2 * kw
    fw = w_gate.shape[1] // n
    qheads, kheads = qw // head, kw // head
    ratio = qheads // kheads
    own_gain = norm1_gain.shape[0]
    own_head = q_gain.shape[0]

    spot = lax.axis_index("fsdp")
    owner = lax.axis_index("seq") * nf + spot
    lanes = jnp.arange(128, dtype=jnp.int32)[None, :]

    def placed(gain, mine):
        count = gain.shape[0]
        wide = jnp.tile(gain.astype(F32), 128 // count)[None, :]
        return jnp.where(lax.div(lanes, count) == mine, wide, 0.0)

    sharing = 128 // own_gain
    packed = jnp.concatenate(
        [
            placed(norm1_gain, lax.rem(spot, sharing)),
            placed(norm2_gain, lax.rem(spot, sharing)),
            placed(q_gain, owner),
            placed(k_gain, owner),
            jnp.zeros((4, 128), F32),
        ],
        axis=0,
    )
    w_att = pl.pallas_call(
        functools.partial(attention_weights_out, n),
        out_shape=shape((n, depth, cw), BF),
        in_specs=[ANY] * 3,
        out_specs=ANY,
        scratch_shapes=[dma(3 * (n - 1)), dma(3 * (n - 1)), dma(3)],
        compiler_params=comm_params(0),
    )(w_query, w_key, w_value)
    gu, all_gains = pl.pallas_call(
        functools.partial(gate_up_out, n, nf),
        out_shape=(shape((n, depth, 2 * fw), BF), shape((nf, n, 8, 128), F32)),
        in_specs=[ANY] * 3,
        out_specs=(ANY, ANY),
        scratch_shapes=[
            pltpu.VMEM((n, 8, 128), F32),
            dma(2 * (n - 1)),
            dma(2 * (n - 1)),
            dma(2),
            dma(n + nf - 2),
            dma(n + nf - 2),
            dma(2),
        ],
        compiler_params=comm_params(8),
    )(after(w_gate, w_att), w_up, packed)
    gather_sems = [dma(gather_copies(n)), dma(gather_copies(n)), pltpu.SemaphoreType.DMA]
    line = nf == 8
    w_att = lax.all_gather(w_att, "fsdp", axis=1, tiled=True).reshape(width, cw)
    half = head // 2
    powers = -(np.arange(half, dtype=np.float32) * np.float32(2.0) / np.float32(head))
    freq = np.tile((np.float32(theta) ** powers).astype(np.float32), 2)[None, :]
    small = pl.BlockSpec(memory_space=pltpu.SMEM)
    xg, dn, wo, gain_one, gain_two, gain_q, gain_k, cos, sin, low, high = pl.pallas_call(
        functools.partial(entry_stage, n, nf, line, own_gain),
        out_shape=(
            shape((n, rows, width), BF),
            shape((n, depth, fw), BF),
            shape((nf if line else 1, depth, width), BF),
            shape((1, width), F32),
            shape((1, width), F32),
            shape((1, head), F32),
            shape((1, head), F32),
            shape((group, head), F32),
            shape((group, head), F32),
            shape((8, group), jnp.int32),
            shape((8, group), jnp.int32),
        ),
        in_specs=[ANY] * 3 + [VMEM] + [small] * 3 + [VMEM],
        out_specs=(ANY,) * 3 + (VMEM,) * 8,
        scratch_shapes=gather_sems
        + [dma(n - 1), dma(n - 1), dma(1), dma(10), dma(10), pltpu.SemaphoreType.DMA],
        compiler_params=comm_params(1),
    )(after(tokens, gu), w_down.T, w_out, all_gains, seq_lengths, pic_starts, pic_lengths, jnp.asarray(freq))
    wo = wo.reshape(-1, width)
    if not line:
        wo = lax.all_gather(wo, "fsdp", axis=0, tiled=True)
    gu = lax.all_gather(gu, "fsdp", axis=1, tiled=True).reshape(width, 2 * fw)
    dn = lax.all_gather(dn, "fsdp", axis=1, tiled=True).reshape(width, fw)

    def whole(dims):
        return pl.BlockSpec(dims, lambda *ids: (0,) * len(dims))

    def by_rows(count, columns):
        return pl.BlockSpec((count, columns), lambda i: (i, 0))

    def by_cols(count, columns):
        return pl.BlockSpec((count, columns), lambda i: (0, i))

    blocks = group // 256
    n1, qraw, kraw, q, k, v, kt, vt, cg = pl.pallas_call(
        functools.partial(project, n),
        grid=(blocks,),
        out_shape=(
            shape((group, width), BF),
            shape((group, qw), F32),
            shape((group, kw), F32),
            shape((group, qw), BF),
            shape((group, kw), BF),
            shape((group, kw), BF),
            shape((kw, group), BF),
            shape((kw, group), BF),
            shape((n, rows, width), BF),
        ),
        in_specs=[
            by_rows(256, width),
            whole((1, width)),
            whole((width, cw)),
            whole((1, head)),
            whole((1, head)),
            by_rows(256, head),
            by_rows(256, head),
            ANY,
        ],
        out_specs=(
            by_rows(256, width),
            by_rows(256, qw),
            by_rows(256, kw),
            by_rows(256, qw),
            by_rows(256, kw),
            by_rows(256, kw),
            by_cols(kw, 256),
            by_cols(kw, 256),
            ANY,
        ),
        scratch_shapes=gather_sems,
        compiler_params=comm_params(11),
    )(xg.reshape(group, width), gain_one, w_att, gain_q, gain_k, cos, sin, cotangent)

    attn, lse, part_out, cg = pl.pallas_call(
        functools.partial(attend, n),
        grid=(blocks,),
        out_shape=(
            shape((group, qw), BF),
            shape((8, group), F32),
            shape((group, width), BF),
            shape((n, rows, width), BF),
        ),
        in_specs=[
            by_rows(256, qw),
            whole((group, kw)),
            whole((kw, group)),
            whole((qw, width)),
            by_cols(8, 256),
            by_cols(8, 256),
            ANY,
            ANY,
        ],
        out_specs=(by_rows(256, qw), by_cols(8, 256), by_rows(256, width), ANY),
        scratch_shapes=[pltpu.VMEM((group, 256), F32)] + gather_sems,
        input_output_aliases={7: 3},
        compiler_params=comm_params(3),
    )(q, k, vt, wo, low, high, cotangent, cg)
    cg = cg.reshape(group, width)

    slots = [
        pltpu.VMEM((scatter_slots(n), rows, width), BF),
        pltpu.VMEM((rows, width), BF),
    ]
    sems = [dma(max(6, n - 1)), dma(max(6, n - 1))]

    x2, n2 = pl.pallas_call(
        functools.partial(middle_stage, n),
        out_shape=(shape((rows, width), F32), shape((n, rows, width), BF)),
        in_specs=[VMEM] * 3,
        out_specs=(VMEM, ANY),
        scratch_shapes=slots + [pltpu.VMEM((rows, width), BF)] + sems + gather_sems,
        compiler_params=comm_params(2),
    )(part_out.reshape(n, rows, width), tokens, gain_two)
    n2 = n2.reshape(group, width)

    tile = 256
    tiles = fw // tile
    gate, up, hidden = pl.pallas_call(
        ffn_forward,
        grid=(tiles,),
        out_shape=(
            shape((group, fw), F32),
            shape((group, fw), F32),
            shape((group, fw), BF),
        ),
        in_specs=[
            whole((group, width)),
            by_cols(width, tile),
            pl.BlockSpec((width, tile), lambda i: (0, i + tiles)),
        ],
        out_specs=(by_cols(group, tile),) * 3,
        compiler_params=plain_params(),
    )(n2, gu, gu)

    def product(number, a, *bs, into=None, dims=None, spot=0):
        tile = 512
        while any(b.shape[1] % tile for b in bs):
            tile //= 2
        counts = [b.shape[1] // tile for b in bs]
        begins = [sum(counts[:i]) for i in range(len(bs))]
        tiles = sum(counts)

        def spec(begin, count):
            return pl.BlockSpec(
                (group, tile), lambda i: (0, jnp.clip(i - begin, 0, count - 1))
            )

        if dims is None:
            dims = (n, width // n // 2, tiles * tile)
        lead = a.shape[1] // 2 // dims[1]
        across = dims[2] // tile
        kept = [] if into is None else [into]
        blocks = a.shape[1] // (2 * depth)

        def place(i):
            last = jnp.maximum(i - 1, 0)
            return (spot + lax.div(last, across), 0, lax.rem(last, across))

        return pl.pallas_call(
            functools.partial(gradient, counts, len(kept)),
            grid=(tiles + 1,),
            out_shape=shape(dims, BF),
            in_specs=[whole(a.shape)]
            + [spec(b, c) for b, c in zip(begins, counts)]
            + [ANY] * len(kept),
            out_specs=pl.BlockSpec((lead, dims[1], tile), place),
            scratch_shapes=[
                pltpu.VMEM((a.shape[1], group), BF),
                pltpu.VMEM((2, blocks, 2, depth, tile), BF),
                pltpu.VMEM((tiles, blocks, depth, tile), BF),
                dma(tiles),
                dma(tiles),
            ],
            input_output_aliases={} if into is None else {1 + len(bs): 0},
            compiler_params=comm_params(number),
        )(a, *bs, *kept)

    same_core = [[core + 2 * i for i in range(nf // 2)] for core in range(2)]

    def reduce_rows(grad):
        return lax.psum_scatter(
            grad, "fsdp", scatter_dimension=1, tiled=True, axis_index_groups=same_core
        )

    dn_grad = product(12, cg, hidden)
    dn_share = reduce_rows(dn_grad)

    dgate, dup = pl.pallas_call(
        ffn_back,
        grid=(tiles,),
        out_shape=(shape((group, fw), BF), shape((group, fw), BF)),
        in_specs=[
            whole((group, width)),
            by_cols(width, tile),
            by_cols(group, tile),
            by_cols(group, tile),
        ],
        out_specs=(by_cols(group, tile),) * 2,
        compiler_params=plain_params(),
    )(cg, after(dn, dn_grad), gate, up)

    gu_grad = product(13, n2, dgate, dup)
    part_n2 = pl.pallas_call(
        two_nt,
        grid=(blocks,),
        out_shape=shape((group, width), BF),
        in_specs=[
            by_rows(256, fw),
            by_rows(256, fw),
            pl.BlockSpec((width, fw), lambda i: (0, 0)),
            pl.BlockSpec((width, fw), lambda i: (0, 1)),
        ],
        out_specs=by_rows(256, width),
        compiler_params=plain_params(),
    )(after(dgate, gu_grad), dup, gu, gu)
    gu_share = reduce_rows(after(gu_grad, (dn_share, part_n2)))

    dx2, dz, dgain_two, part_y = pl.pallas_call(
        functools.partial(back_stage, n),
        out_shape=(
            shape((rows, width), F32),
            shape((n, rows, width), BF),
            shape((width // 128, 128), F32),
            shape((n, rows, width), BF),
        ),
        in_specs=[VMEM] * 4 + [ANY] * 2,
        out_specs=(VMEM, ANY, VMEM, VMEM),
        scratch_shapes=slots
        + [pltpu.VMEM((rows, width), BF)]
        + sems
        + gather_sems
        + [
            pltpu.VMEM((1, width), F32),
            pltpu.VMEM((group, fw), BF),
            pltpu.VMEM((width, fw), BF),
            dma(2),
        ],
        compiler_params=comm_params(4),
    )(
        after(part_n2, dn_share).reshape(n, rows, width), x2, cotangent, gain_two, hidden, dn,
    )
    dz = dz.reshape(group, width)

    wo_grad = product(14, attn, dz, dims=(n + width // cw, qw // 2, cw), spot=n)

    wide = ratio * head
    dq, dk, dv, dgain_q, dgain_k, branch = pl.pallas_call(
        functools.partial(attend_back, n),
        grid=(kheads, blocks),
        out_shape=(
            shape((group, qw), BF),
            shape((group, kw), BF),
            shape((group, kw), BF),
            shape((8, head), F32),
            shape((8, head), F32),
            shape((rows, width), F32),
        ),
        in_specs=[
            pl.BlockSpec((256, wide), lambda h, b: (b, h)),
            pl.BlockSpec((256, wide), lambda h, b: (b, h)),
            pl.BlockSpec((group, head), lambda h, b: (0, h)),
            pl.BlockSpec((head, group), lambda h, b: (h, 0)),
            pl.BlockSpec((group, head), lambda h, b: (0, h)),
            pl.BlockSpec((group, head), lambda h, b: (0, h)),
            pl.BlockSpec((256, width), lambda h, b: (b, 0)),
            pl.BlockSpec((wide, width), lambda h, b: (h, 0)),
            pl.BlockSpec((8, 256), lambda h, b: (0, b)),
            pl.BlockSpec((8, 256), lambda h, b: (0, b)),
            pl.BlockSpec((8, 256), lambda h, b: (0, b)),
            pl.BlockSpec((256, head), lambda h, b: (b, 0)),
            pl.BlockSpec((256, head), lambda h, b: (b, 0)),
            whole((group, head)),
            whole((group, head)),
            whole((1, head)),
            whole((1, head)),
            VMEM,
        ],
        out_specs=(
            pl.BlockSpec((256, wide), lambda h, b: (b, h)),
            pl.BlockSpec((group, head), lambda h, b: (0, h)),
            pl.BlockSpec((group, head), lambda h, b: (0, h)),
            whole((8, head)),
            whole((8, head)),
            VMEM,
        ),
        scratch_shapes=[pltpu.VMEM((group, head), F32), pltpu.VMEM((group, head), F32)]
        + slots
        + sems,
        compiler_params=comm_params(5),
    )(
        q, qraw, k, kt, v, kraw, dz, wo, lse, low, high, cos, sin, cos, sin, gain_q, gain_k,
        part_y,
    )
    output = (x2 + branch).astype(BF)

    att_grad = product(15, n1, dq, dk, dv, into=wo_grad, dims=wo_grad.shape)
    att_share = reduce_rows(after(att_grad, gu_share))

    back_one, dgain_one = pl.pallas_call(
        functools.partial(input_stage, n),
        out_shape=(shape((rows, width), F32), shape((width // 128, 128), F32)),
        in_specs=[VMEM] * 6,
        out_specs=(VMEM, VMEM),
        scratch_shapes=[pltpu.VMEM((n, rows, width), BF)]
        + slots
        + sems
        + [pltpu.VMEM((1, width), F32)],
        compiler_params=comm_params(10),
    )(after(dq, att_grad), dk, dv, w_att, tokens, gain_one)
    input_grad = (dx2 + back_one).astype(BF)

    gu_mine, dn_mine, gains = pl.pallas_call(
        functools.partial(exchange_gains, n, nf),
        out_shape=(
            shape(gu_share.shape, BF),
            shape(dn_share.shape, BF),
            shape((8, 128), F32),
        ),
        in_specs=[ANY] * 2 + [VMEM] * 4,
        out_specs=(ANY, ANY, VMEM),
        scratch_shapes=[
            pltpu.VMEM((nf, n, 8, 128), F32),
            pltpu.VMEM((nf - 1, n, 8, 128), F32),
            pltpu.VMEM((n, 8, 128), F32),
            pltpu.VMEM((n - 1, 8, 128), F32),
            dma(2 * (n - 1)),
            dma(2 * (n - 1)),
            dma(2),
            dma(n + nf - 2),
            dma(n + nf - 2),
        ],
        compiler_params=comm_params(7),
    )(gu_share, dn_share, dgain_one, dgain_two, dgain_q, dgain_k)

    def owned(row, count, mine):
        return lax.dynamic_slice_in_dim(row, mine * count, count, 0)

    gain_grads = (
        owned(gains[0], own_gain, lax.rem(spot, sharing)),
        owned(gains[1], own_gain, lax.rem(spot, sharing)),
        owned(gains[2], own_head, owner),
        owned(gains[3], own_head, owner),
    )

    def spread(arrays, pieces):
        ins = [pl.BlockSpec((1, depth, a.shape[2]), lambda i: (i, 0, 0)) for a in arrays]
        outs = [by_cols(depth, count) for _, _, count in pieces]
        shapes = [shape((depth, n * count), F32) for _, _, count in pieces]
        return pl.pallas_call(
            functools.partial(widen, pieces),
            grid=(n,),
            out_shape=tuple(shapes),
            in_specs=ins,
            out_specs=tuple(outs),
            compiler_params=plain_params(),
        )(*arrays)

    gate_grad, up_grad, down_grad = spread(
        [gu_mine, dn_mine], [(0, 0, fw), (0, fw, fw), (1, 0, fw)]
    )
    wide_grads = (gate_grad, up_grad, down_grad.T)
    wo_out = att_share[n:].transpose(1, 0, 2).reshape(depth, width).astype(F32)
    att_mine = pl.pallas_call(
        functools.partial(exchange, n),
        out_shape=shape((n, depth, cw), BF),
        in_specs=[ANY],
        out_specs=ANY,
        scratch_shapes=[dma(n - 1), dma(n - 1), dma(1)],
        compiler_params=comm_params(9),
    )(after(att_share, (gain_grads, wide_grads, input_grad, output)))
    wq_grad, wk_grad, wv_grad = spread(
        [att_mine], [(0, 0, qw), (0, qw, kw), (0, qw + kw, kw)]
    )

    return (
        output,
        input_grad,
        gain_grads[0],
        wq_grad,
        wk_grad,
        wv_grad,
        gain_grads[2],
        gain_grads[3],
        wo_out,
        gain_grads[1],
    ) + wide_grads


def solution(mesh):
    return jax.shard_map(
        functools.partial(shards, mesh.shape["seq"], mesh.shape["fsdp"]),
        mesh=mesh,
        in_specs=(
            P(("fsdp", "seq"), None),
            P("fsdp", None),
            P("fsdp", None),
            P("fsdp", None),
            P(("seq", "fsdp")),
            P(("seq", "fsdp"), None),
            P(("seq", "fsdp"), None),
            P(("seq", "fsdp"), None),
            P(("seq", "fsdp")),
            P(("seq", "fsdp")),
            P(("seq", "fsdp"), None),
            P(("seq", "fsdp")),
            P(("seq", "fsdp"), None),
            P(("seq", "fsdp"), None),
            P(None, ("seq", "fsdp")),
            P(("fsdp", "seq"), None),
        ),
        out_specs=(
            P(("fsdp", "seq"), None),
            P(("fsdp", "seq"), None),
            P(("seq", "fsdp")),
            P(("seq", "fsdp"), None),
            P(("seq", "fsdp"), None),
            P(("seq", "fsdp"), None),
            P(("seq", "fsdp")),
            P(("seq", "fsdp")),
            P(("seq", "fsdp"), None),
            P(("seq", "fsdp")),
            P(("seq", "fsdp"), None),
            P(("seq", "fsdp"), None),
            P(None, ("seq", "fsdp")),
        ),
        check_vma=False,
    )
```

```python
import functools

import jax
import jax.numpy as jnp
import numpy as np
from jax import lax
from jax.experimental import pallas as pl
from jax.experimental.pallas import tpu as pltpu
from jax.sharding import PartitionSpec as P

epsilon = 1e-06
theta = 1000000.0
masked_score = -1e30
log2e = 1.4426950408889634

MESH = pl.DeviceIdType.MESH
ANY = pl.BlockSpec(memory_space=pl.ANY)
VMEM = pl.BlockSpec(memory_space=pltpu.VMEM)
BF = jnp.bfloat16
F32 = jnp.float32
LIMIT = 60 * 1024 * 1024


def dot(a, b):
    return jnp.dot(a, b, preferred_element_type=F32)


def dot_nt(a, b):
    return lax.dot_general(a, b, (((1,), (1,)), ((), ())), preferred_element_type=F32)


def dot_tn(a, b):
    return lax.dot_general(a, b, (((0,), (0,)), ((), ())), preferred_element_type=F32)


def shape(dims, dtype):
    return jax.ShapeDtypeStruct(dims, dtype)


def comm_params(number):
    return pltpu.CompilerParams(
        collective_id=number, has_side_effects=True, vmem_limit_bytes=LIMIT
    )


def plain_params():
    return pltpu.CompilerParams(vmem_limit_bytes=LIMIT)


def remote(src, dst, send, recv, axis, index):
    return pltpu.make_async_remote_copy(
        src_ref=src,
        dst_ref=dst,
        send_sem=send,
        recv_sem=recv,
        device_id={axis: index},
        device_id_type=MESH,
    )


def greet(places):
    barrier = pltpu.get_barrier_semaphore()
    for axis, index in places:
        pl.semaphore_signal(barrier, inc=1, device_id={axis: index}, device_id_type=MESH)
    pl.semaphore_wait(barrier, len(places))


def others(axis, n):
    me = lax.axis_index(axis)
    return [(axis, lax.rem(me + j, n)) for j in range(1, n)]


def square(me):
    return me + 1 - 2 * lax.rem(me, 2), lax.rem(me + 2, 4), 3 - me


def ring_places(n):
    me = lax.axis_index("seq")
    if n == 4:
        across, along, _ = square(me)
        return [("seq", across), ("seq", along)]
    return others("seq", n)


def gather_copies(n):
    return 6 if n == 4 else n - 1


def gather_parts(n, own, out, send, recv, local):
    me = lax.axis_index("seq")
    keep = pltpu.make_async_copy(own, out.at[me], local)
    half = own.shape[0] // 2
    low, high = pl.ds(0, half), pl.ds(half, half)
    if n == 4:
        across, along, _ = square(me)
        moves = [
            (own.at[low], out.at[me, low], across),
            (own.at[high], out.at[me, high], along),
            (own.at[high], out.at[me, high], across),
            (own.at[low], out.at[me, low], along),
            (out.at[across, low], out.at[across, low], along),
            (out.at[along, high], out.at[along, high], across),
        ]
    else:
        moves = [(own, out.at[me], lax.rem(me + j, n)) for j in range(1, n)]
    copies = [
        remote(src, dst, send.at[i], recv.at[i], "seq", to)
        for i, (src, dst, to) in enumerate(moves)
    ]

    def start(part=None):
        chosen = range(len(copies))
        if n == 4:
            chosen = {None: (0, 1, 2, 3), 0: (0, 3), 1: (1, 2)}[part]
        if n == 4 or part != 0:
            for i in chosen:
                copies[i].start()
        if part != 0:
            keep.start()

    def relay():
        if n == 4:
            copies[0].wait_recv()
            copies[4].start()
            copies[1].wait_recv()
            copies[5].start()

    def finish():
        for copy in copies[2:] if n == 4 else copies:
            copy.wait_recv()
        for copy in copies:
            copy.wait_send()
        keep.wait()

    return start, relay, finish


def gather(n, own, out, send, recv, local):
    for part in gather_parts(n, own, out, send, recv, local):
        part()


def scatter_slots(n):
    return 4 if n == 4 else n - 1


def scatter_sum(n, part, slots, stage, send, recv, finish):
    start, relay, lower, upper = scatter_parts(n, part, slots, stage, send, recv, finish)
    start()
    relay()
    lower()
    upper()


def scatter_parts(n, part, slots, stage, send, recv, finish):
    me = lax.axis_index("seq")
    rows = part.shape[1]
    half = rows // 2
    low, high = pl.ds(0, half), pl.ds(half, half)
    if n == 4:
        across, along, corner = square(me)
        moves = [
            (part.at[corner, low], slots.at[2, low], along),
            (part.at[corner, high], slots.at[2, high], across),
            (part.at[across, high], slots.at[0, high], across),
            (part.at[along, low], slots.at[1, low], along),
            (stage.at[low], slots.at[0, low], across),
            (stage.at[high], slots.at[1, high], along),
        ]
        count = 2
    else:
        moves = []
        for j in range(1, n):
            to = lax.rem(me + j, n)
            moves.append((part.at[to], slots.at[j - 1], to))
        count = n - 1
    copies = [
        remote(src, dst, send.at[i], recv.at[i], "seq", to)
        for i, (src, dst, to) in enumerate(moves)
    ]

    def start(begin=0, end=4):
        for copy in copies[begin:end] if n == 4 else copies:
            copy.start()

    def relay():
        if n == 4:
            copies[0].wait_recv()
            stage[low] = (part[across, low].astype(F32) + slots[2, low].astype(F32)).astype(BF)
            copies[4].start()
            copies[1].wait_recv()
            stage[high] = (part[along, high].astype(F32) + slots[2, high].astype(F32)).astype(BF)
            copies[5].start()

    step = 32

    def chunk(number, carry):
        at = pl.ds(pl.multiple_of(number * step, step), step)
        value = part[me, at].astype(F32)
        for slot in range(count):
            value += slots[slot, at].astype(F32)
        finish(at, value)
        return carry

    def lower():
        for copy in copies[3:5] if n == 4 else copies:
            copy.wait_recv()
        lax.fori_loop(0, half // step, chunk, 0)

    def upper():
        if n == 4:
            copies[2].wait_recv()
            copies[5].wait_recv()
        lax.fori_loop(half // step, rows // step, chunk, 0)
        for copy in copies:
            copy.wait_send()

    return start, relay, lower, upper


def inverse_rms(values):
    return lax.rsqrt(jnp.mean(values * values, axis=-1, keepdims=True) + epsilon)


def norm_back(values, gain, grad):
    inverse = inverse_rms(values)
    scaled = grad * gain
    back = inverse * scaled - values * (
        inverse * inverse * inverse * jnp.mean(scaled * values, axis=-1, keepdims=True)
    )
    return back, jnp.sum(grad * values * inverse, axis=0, keepdims=True)


def attention_weights_out(n, wq, wk, wv, out, send, recv, local):
    me = lax.axis_index("seq")
    greet(others("seq", n))
    widths = [wq.shape[1] // n, wk.shape[1] // n, wv.shape[1] // n]
    begins = [0, widths[0], widths[0] + widths[1]]
    copies = []
    for j in range(1, n):
        to = lax.rem(me + j, n)
        for i, ref in enumerate((wq, wk, wv)):
            columns = pl.ds(pl.multiple_of(to * widths[i], 128), widths[i])
            copies.append(
                remote(
                    ref.at[:, columns],
                    out.at[me, :, pl.ds(begins[i], widths[i])],
                    send.at[3 * j - 3 + i],
                    recv.at[3 * j - 3 + i],
                    "seq",
                    to,
                )
            )
    for i, ref in enumerate((wq, wk, wv)):
        columns = pl.ds(pl.multiple_of(me * widths[i], 128), widths[i])
        copies.append(
            pltpu.make_async_copy(
                ref.at[:, columns], out.at[me, :, pl.ds(begins[i], widths[i])], local.at[i]
            )
        )
    for copy in copies:
        copy.start()
    for copy in copies:
        copy.wait()


def start_columns(n, views, send, recv, local):
    me = lax.axis_index("seq")
    width = views[0][0].shape[1] // n
    copies, keeps = [], []
    for i, (ref, out, place) in enumerate(views):
        for j in range(1, n):
            to = lax.rem(me + j, n)
            columns = pl.ds(pl.multiple_of(to * width, 128), width)
            k = i * (n - 1) + j - 1
            copies.append(
                remote(
                    ref.at[:, columns],
                    out.at[me, :, pl.ds(place * width, width)],
                    send.at[k],
                    recv.at[k],
                    "seq",
                    to,
                )
            )
        columns = pl.ds(pl.multiple_of(me * width, 128), width)
        keeps.append(
            pltpu.make_async_copy(
                ref.at[:, columns], out.at[me, :, pl.ds(place * width, width)], local.at[i]
            )
        )
    for copy in copies + keeps:
        copy.start()
    return copies + keeps


def gate_up_out(n, nf, wg, wu, gains, gu, all_gains, seen, send, recv, local, gsend, grecv, glocal):
    me, spot = lax.axis_index("seq"), lax.axis_index("fsdp")
    greet(others("seq", n) + others("fsdp", nf))
    small = []
    for j in range(1, n):
        to = lax.rem(me + j, n)
        small.append(
            remote(gains, seen.at[me], gsend.at[j - 1], grecv.at[j - 1], "seq", to)
        )
    keep = pltpu.make_async_copy(gains, seen.at[me], glocal.at[0])
    for copy in small + [keep]:
        copy.start()
    copies = start_columns(n, [(wg, gu, 0), (wu, gu, 1)], send, recv, local)
    for copy in small + [keep]:
        copy.wait()
    wide = [pltpu.make_async_copy(seen, all_gains.at[spot], glocal.at[1])]
    for j in range(1, nf):
        to = lax.rem(spot + j, nf)
        k = n + j - 2
        wide.append(
            remote(seen, all_gains.at[spot], gsend.at[k], grecv.at[k], "fsdp", to)
        )
    for copy in wide:
        copy.start()
    for copy in copies + wide:
        copy.wait()


def line_gather(own, out, send, recv, local, between):
    spot = lax.axis_index("fsdp")
    z = lax.div(spot, 2)
    twin = spot + 1 - 2 * lax.rem(spot, 2)
    keep = pltpu.make_async_copy(own, out.at[spot], local)
    keep.start()

    def up(k):
        block = spot - 2 * k
        return remote(
            own if k == 0 else out.at[block], out.at[block], send.at[k], recv.at[k], "fsdp", spot + 2
        )

    def down(k):
        block = spot + 2 * k
        return remote(
            own if k == 0 else out.at[block],
            out.at[block],
            send.at[3 + k],
            recv.at[3 + k],
            "fsdp",
            spot - 2,
        )

    def over(offset):
        block = spot + 2 * offset
        return remote(
            own if offset == 0 else out.at[block],
            out.at[block],
            send.at[6 + lax.div(block, 2)],
            recv.at[6 + lax.div(block, 2)],
            "fsdp",
            twin,
        )

    def from_twin(offset):
        block = twin + 2 * offset
        return remote(
            own, out.at[block], send.at[6 + lax.div(block, 2)], recv.at[6 + lax.div(block, 2)], "fsdp", twin
        )

    @pl.when(z < 3)
    def _():
        up(0).start()

    @pl.when(z > 0)
    def _():
        down(0).start()

    over(0).start()
    between()
    for k in range(1, 4):

        @pl.when(z >= k)
        def _():
            up(k - 1).wait_recv()
            if k < 3:

                @pl.when(z < 3)
                def _():
                    up(k).start()

            over(-k).start()

        @pl.when(z + k <= 3)
        def _():
            down(k - 1).wait_recv()
            if k < 3:

                @pl.when(z > 0)
                def _():
                    down(k).start()

            over(k).start()

    from_twin(0).wait_recv()
    over(0).wait_send()
    for k in range(1, 4):

        @pl.when(z >= k)
        def _():
            from_twin(-k).wait_recv()
            over(-k).wait_send()

        @pl.when(z + k <= 3)
        def _():
            from_twin(k).wait_recv()
            over(k).wait_send()

    for k in range(3):

        @pl.when((z >= k) & (z < 3))
        def _():
            up(k).wait_send()

        @pl.when((z + k <= 3) & (z > 0))
        def _():
            down(k).wait_send()

    keep.wait()


def greet_line(places):
    spot = lax.axis_index("fsdp")
    z = lax.div(spot, 2)
    twin = spot + 1 - 2 * lax.rem(spot, 2)
    barrier = pltpu.get_barrier_semaphore()
    for axis, index in places + [("fsdp", twin)]:
        pl.semaphore_signal(barrier, inc=1, device_id={axis: index}, device_id_type=MESH)

    @pl.when(z < 3)
    def _():
        pl.semaphore_signal(barrier, inc=1, device_id={"fsdp": spot + 2}, device_id_type=MESH)

    @pl.when(z > 0)
    def _():
        pl.semaphore_signal(barrier, inc=1, device_id={"fsdp": spot - 2}, device_id_type=MESH)

    inner = (z < 3).astype(jnp.int32) + (z > 0).astype(jnp.int32)
    pl.semaphore_wait(barrier, len(places) + 1 + inner)


def entry_stage(n, nf, line, own_gain, x, wd, w_out, gains, lengths, starts, sizes, freq, xg, dn, wo, gain_one, gain_two, gain_q, gain_k, cos, sin, low, high, send, recv, local, wsend, wrecv, wlocal, lsend, lrecv, llocal):
    if line:
        greet_line(others("seq", n))
    else:
        greet(others("seq", n))
    start, relay, finish = gather_parts(n, x, xg, send, recv, local)
    start()
    copies = start_columns(n, [(wd, dn, 0)], wsend, wrecv, wlocal)

    def tables():
        per = 128 // own_gain
        for row in range(n * nf // per):
            seq, first = row * per // nf, row * per % nf
            one = gains[first, seq, 0:1, :]
            two = gains[first, seq, 1:2, :]
            for f in range(first + 1, first + per):
                one += gains[f, seq, 0:1, :]
                two += gains[f, seq, 1:2, :]
            gain_one[:, row * 128 : row * 128 + 128] = one
            gain_two[:, row * 128 : row * 128 + 128] = two
        total = jnp.zeros((8, 128), F32)
        for f in range(nf):
            for seq in range(n):
                total += gains[f, seq]
        gain_q[...] = total[2:3, :]
        gain_k[...] = total[3:4, :]

        group = cos.shape[0]
        border_one = lengths[0, 0]
        border_two = border_one + lengths[0, 1]

        def begin_of(places):
            later = jnp.where(places >= border_one, border_one, 0)
            return jnp.where(places >= border_two, border_two, later)

        step = 128
        lane = lax.broadcasted_iota(jnp.int32, (step, 128), 1)

        def turn(number, carry):
            at = pl.ds(pl.multiple_of(number * step, step), step)
            places = lax.broadcasted_iota(jnp.int32, (step, 128), 0) + number * step
            angle = (places - begin_of(places)).astype(F32) * freq[...]
            cos[at, :] = jnp.cos(angle)
            sine = jnp.sin(angle)
            sin[at, :] = jnp.where(lane < 64, -sine, sine)
            return carry

        lax.fori_loop(0, group // step, turn, 0)
        places = lax.broadcasted_iota(jnp.int32, (8, group), 1)
        end = jnp.where(places >= border_one, border_two, border_one)
        end = jnp.where(places >= border_two, group, end)
        picture = jnp.zeros_like(places)
        for i in range(starts.shape[1]):
            first, count = starts[0, i], sizes[0, i]
            inside = (places >= first) & (places < first + count)
            picture = jnp.where(inside, jnp.maximum(picture, first + count), picture)
        low[...] = begin_of(places)
        high[...] = jnp.maximum(places, jnp.minimum(picture, end) - 1)

    if line:
        line_gather(w_out, wo, lsend, lrecv, llocal, relay)
    else:
        keep = pltpu.make_async_copy(w_out, wo.at[0], llocal)
        keep.start()
        relay()
        keep.wait()
    tables()
    finish()
    for copy in copies:
        copy.wait()


def half_gather(n, begin, cot, cg, send, recv, local):
    at = pl.ds(begin, cot.shape[0] // 2)
    start, relay, finish = gather_parts(n, cot.at[at], cg.at[:, at], send, recv, local)
    step, steps = pl.program_id(0), pl.num_programs(0)

    @pl.when(step == 0)
    def _():
        greet(ring_places(n))
        start()

    @pl.when(step == steps - 1)
    def _():
        relay()

    return finish


def project(n, x_ref, gain_ref, w_ref, gq_ref, gk_ref, cos_ref, sin_ref, cot, n1_ref, qraw_ref, kraw_ref, q_ref, k_ref, v_ref, kt_ref, vt_ref, cg, send, recv, local):
    finish_half = half_gather(n, 0, cot, cg, send, recv, local)
    x = x_ref[...].astype(F32)
    normed = (x * inverse_rms(x) * gain_ref[...]).astype(BF)
    n1_ref[...] = normed.T
    full = dot(normed, w_ref[...])
    qw, kw = q_ref.shape[1], k_ref.shape[1]
    cos, sin = cos_ref[...], sin_ref[...]

    def prep(head, gain):
        u = head * inverse_rms(head) * gain
        return u * cos + pltpu.roll(u, 64, 1) * sin

    qraw_ref[...] = full[:, :qw]
    kraw_ref[...] = full[:, qw : qw + kw]
    v = full[:, qw + kw :]
    v_ref[...] = v.astype(BF)
    vt_ref[...] = v.T.astype(BF)
    for h in range(qw // 128):
        q_ref[:, h * 128 : h * 128 + 128] = prep(
            full[:, h * 128 : h * 128 + 128], gq_ref[...]
        ).astype(BF)
    for h in range(kw // 128):
        turned = prep(full[:, qw + h * 128 : qw + h * 128 + 128], gk_ref[...])
        k_ref[:, h * 128 : h * 128 + 128] = turned.astype(BF)
        kt_ref[h * 128 : h * 128 + 128, :] = turned.T.astype(BF)

    @pl.when(pl.program_id(0) == pl.num_programs(0) - 1)
    def _():
        finish_half()


def bias_of(low_ref, high_ref, keys):
    key = lax.broadcasted_iota(jnp.int32, (keys, low_ref.shape[1]), 0)
    fine = (key >= low_ref[0:1, :]) & (key <= high_ref[0:1, :])
    return jnp.where(fine, 0.0, masked_score)


def attend(n, q_ref, k_ref, vt_ref, wo_ref, low_ref, high_ref, cot, cg_half, attn_ref, lse_ref, part_ref, cg, bias, send, recv, local):
    finish_half = half_gather(n, cot.shape[0] // 2, cot, cg, send, recv, local)
    keys = k_ref.shape[0]
    bias[...] = bias_of(low_ref, high_ref, keys)
    heads = q_ref.shape[1] // 128
    ratio = heads // (k_ref.shape[1] // 128)
    factor = 128 ** (-0.5) * log2e
    for h in range(heads):
        kv = h // ratio
        scores = dot_nt(
            k_ref[:, kv * 128 : kv * 128 + 128], q_ref[:, h * 128 : h * 128 + 128]
        )
        scores = scores * factor + bias[...]
        top = jnp.max(scores, axis=0, keepdims=True)
        probs = jnp.exp2(scores - top)
        total = jnp.sum(probs, axis=0, keepdims=True)
        mixed = dot(vt_ref[kv * 128 : kv * 128 + 128, :], probs.astype(BF))
        lse_ref[h : h + 1, :] = top + jnp.log2(total)
        attn_ref[:, h * 128 : h * 128 + 128] = (mixed / total).T.astype(BF)
    part_ref[...] = dot(attn_ref[...], wo_ref[...]).astype(BF)

    @pl.when(pl.program_id(0) == pl.num_programs(0) - 1)
    def _():
        finish_half()


def middle_stage(n, part, x, gain, x2, n2, slots, stage, own, send, recv, asend, arecv, local):
    greet(ring_places(n))

    def finish(at, total):
        value = x[at].astype(F32) + total
        x2[at] = value
        own[at] = (value * inverse_rms(value) * gain[...]).astype(BF)

    start, relay, lower, upper = scatter_parts(n, part, slots, stage, send, recv, finish)
    send_on, pass_on, end = gather_parts(n, own, n2, asend, arecv, local)
    start()
    relay()
    lower()
    send_on(0)
    upper()
    send_on(1)
    pass_on()
    end()


def ffn_forward(cuts, n2_ref, wg_ref, wu_ref, gate_ref, up_ref, hidden_ref, turned_ref):
    count = n2_ref.shape[1] // cuts
    step = pl.program_id(0)

    @pl.when(step < cuts)
    def _():
        turned_ref[...] = n2_ref[:, pl.ds(pl.multiple_of(step * count, 128), count)].T

    gate = dot(n2_ref[...], wg_ref[...])
    up = dot(n2_ref[...], wu_ref[...])
    gate_ref[...] = gate
    up_ref[...] = up
    hidden_ref[...] = (gate * jax.nn.sigmoid(gate) * up).astype(BF)


def ffn_back(cot_ref, wd_ref, gate_ref, up_ref, dgate_ref, dup_ref):
    dh = dot(cot_ref[...], wd_ref[...])
    gate = gate_ref[...]
    s = jax.nn.sigmoid(gate)
    dgate_ref[...] = (dh * up_ref[...] * (s * (1.0 + gate * (1.0 - s)))).astype(BF)
    dup_ref[...] = (dh * (gate * s)).astype(BF)


def spread_rows(row, out):
    for i in range(out.shape[0]):
        out[i : i + 1, :] = row[:, i * 128 : i * 128 + 128]


def back_stage(n, dgate_far, dup_far, gu_far, x2, cot, gain, hidden_far, dn_far, dx2, dz, dgain, part_y, part, slots, stage, own, send, recv, asend, arecv, local, row, hidden, dn, load, dgate, dup, gu, rload, wload):
    greet(ring_places(n))
    me = lax.axis_index("seq")
    rows, width = x2.shape
    units = dup.shape[1]
    step = 512

    def row_loads(to):
        at = pl.ds(pl.multiple_of(to * rows, rows), rows)
        return [
            pltpu.make_async_copy(dgate_far.at[at], dgate.at[at], rload.at[0, to]),
            pltpu.make_async_copy(dup_far.at[at], dup.at[at], rload.at[1, to]),
        ]

    def weight_load(number):
        at = pl.ds(pl.multiple_of(number * step, step), step)
        return pltpu.make_async_copy(gu_far.at[at], gu.at[at], wload.at[number])

    order = [lax.rem(me + j, n) for j in range(1, n)] + [me]
    if n == 4:
        across, along, corner = square(me)
        order = [corner, across, along, me]
    for copy in row_loads(order[0]):
        copy.start()
    for number in range(width // step):
        weight_load(number).start()
    for to in order[1:]:
        for copy in row_loads(to):
            copy.start()
    loads = [
        pltpu.make_async_copy(hidden_far, hidden, load.at[0]),
        pltpu.make_async_copy(dn_far, dn, load.at[1]),
    ]
    for copy in loads:
        copy.start()
    row[...] = jnp.zeros_like(row)

    def block(to, first=False):
        at = pl.ds(pl.multiple_of(to * rows, rows), rows)
        for copy in row_loads(to):
            copy.wait()

        def columns(number, carry):
            if first:
                weight_load(number).wait()
            span = pl.ds(pl.multiple_of(number * step, step), step)
            value = dot_nt(dgate[at, :], gu[span, pl.ds(0, units)])
            value += dot_nt(dup[at, :], gu[span, pl.ds(units, units)])
            part[to, :, span] = value.astype(BF)
            return carry

        lax.fori_loop(0, width // step, columns, 0)

    def forward(to, carry):
        at = pl.ds(pl.multiple_of(to * rows, rows), rows)

        def columns(number, carry):
            span = pl.ds(pl.multiple_of(number * step, step), step)
            part_y[to, :, span] = dot_nt(hidden[at, :], dn[span, :]).astype(BF)
            return carry

        return lax.fori_loop(0, width // step, columns, carry)

    def finish(at, total):
        back, dg = norm_back(x2[at], gain[...], total)
        value = cot[at].astype(F32) + back
        dx2[at] = value
        own[at] = value.astype(BF)
        row[...] += dg

    start, relay, lower, upper = scatter_parts(n, part, slots, stage, send, recv, finish)
    send_on, pass_on, end = gather_parts(n, own, dz, asend, arecv, local)
    if n == 4:
        block(corner, True)
        start(0, 2)
        block(across)
        start(2, 3)
        block(along)
        start(3, 4)
        relay()
        block(me)
    else:
        block(order[0], True)
        for to in order[1:]:
            block(to)
        start()
    for copy in loads:
        copy.wait()
    lax.fori_loop(0, n // 4, forward, 0)
    lower()
    send_on(0)
    upper()
    send_on(1)
    spread_rows(row[...], dgain)
    pass_on()
    lax.fori_loop(n // 4, n, forward, 0)
    end()


def attend_back(n, q_ref, qraw_ref, k_ref, kt_ref, v_ref, kraw_ref, dz_ref, wo_ref, lse_ref, low_ref, high_ref, cq_ref, sq_ref, ck_ref, sk_ref, gq_ref, gk_ref, attn_ref, part, dq_ref, dk_ref, dv_ref, dgq_ref, dgk_ref, out, grads, dk_sum, dv_sum, slots, stage, send, recv, wo_sum, both, got, done, tsend, trecv, put):
    kv, block = pl.program_id(0), pl.program_id(1)
    keys = k_ref.shape[0]
    ratio = q_ref.shape[1] // 128
    scale = 128 ** (-0.5)

    def finish(at, total):
        out[at] = total

    start, relay, lower, upper = scatter_parts(n, part, slots, stage, send, recv, finish)
    core = lax.rem(lax.axis_index("fsdp"), 2)
    twin = lax.axis_index("fsdp") + 1 - 2 * core
    kheads, pieces, depth = both.shape[0], both.shape[1], both.shape[3]

    def move(number):
        return remote(
            both.at[number, :, 1 - core], got.at[number], tsend.at[number], trecv.at[number], "fsdp", twin
        )

    steps = pl.num_programs(0) * pl.num_programs(1)
    step = kv * pl.num_programs(1) + block

    @pl.when(step == 0)
    def _():
        greet(ring_places(n) + [("fsdp", twin)])
        start()
        dgq_ref[...] = jnp.zeros_like(dgq_ref)
        dgk_ref[...] = jnp.zeros_like(dgk_ref)

    @pl.when(step == steps // 2)
    def _():
        relay()

    @pl.when(block == 0)
    def _():
        dk_sum[...] = jnp.zeros_like(dk_sum)
        dv_sum[...] = jnp.zeros_like(dv_sum)
        wo_sum[...] = jnp.zeros_like(wo_sum)

    bias = bias_of(low_ref, high_ref, keys)
    dattn = dot_nt(dz_ref[...], wo_ref[...]).astype(BF)

    def prep_back(grad, raw, gain, cos, sin):
        du = grad * cos - pltpu.roll(grad, 64, 1) * sin
        return norm_back(raw, gain, du)

    for r in range(ratio):
        span = slice(r * 128, r * 128 + 128)
        qh, dah = q_ref[:, span], dattn[:, span]
        lse = lse_ref[pl.ds(kv * ratio + r, 1), :]
        scores = dot_nt(k_ref[...], qh) * (scale * log2e) + bias
        probs = jnp.exp2(scores - lse)
        dprobs = dot_nt(v_ref[...], dah)
        delta = jnp.sum(probs * dprobs, axis=0, keepdims=True)
        ds = (probs * (dprobs - delta)).astype(BF)
        dv_sum[...] += dot(probs.astype(BF), dah)
        dk_sum[...] += dot(ds, qh)
        dqr = dot(kt_ref[...], ds).T * scale
        back, dg = prep_back(dqr, qraw_ref[:, span], gq_ref[...], cq_ref[...], sq_ref[...])
        dq_ref[:, span] = back.astype(BF)
        dgq_ref[0:1] += dg

    wo_sum[...] += dot_tn(attn_ref[...], dz_ref[...])

    @pl.when(block == pl.num_programs(1) - 1)
    def _():
        both[kv] = wo_sum[...].astype(BF).reshape(both.shape[1:])
        move(kv).start()
        dv_ref[...] = dv_sum[...].astype(BF)
        back, dg = prep_back(
            dk_sum[...] * scale, kraw_ref[...], gk_ref[...], ck_ref[...], sk_ref[...]
        )
        dk_ref[...] = back.astype(BF)
        dgk_ref[0:1] += dg

    @pl.when(step == steps - 1)
    def _():
        cw = grads.shape[2]
        writes = []
        for number in range(kheads):
            move(number).wait_recv()
            value = both[number, :, core].astype(F32) + got[number].astype(F32)
            done[number] = value.astype(BF).reshape(done.shape[1:])
            for i in range(done.shape[2] // cw):
                rows = pl.ds(number * pieces * depth, pieces * depth)
                writes.append(
                    pltpu.make_async_copy(
                        done.at[number, :, pl.ds(i * cw, cw)],
                        grads.at[n + i, rows],
                        put.at[number, i],
                    )
                )
        for copy in writes:
            copy.start()
        lower()
        upper()
        for copy in writes:
            copy.wait()
        for number in range(kheads):
            move(number).wait_send()


def gradient(n, counts, kept, flipped, beside, *refs):
    a_ref, bs = refs[0], refs[1 : 1 + len(counts)]
    refs = refs[1 + len(counts) + kept :]
    if beside:
        given, out_ref, taken, both, got, send, recv, esend, erecv, local = refs[:10]
        refs = refs[10:]
    else:
        out_ref, both, got, send, recv = refs[:5]
        refs = refs[5:]
    turned = a_ref if flipped else refs[0]
    step = pl.program_id(0)
    tiles = sum(counts)
    core = lax.rem(lax.axis_index("fsdp"), 2)
    twin = lax.axis_index("fsdp") + 1 - 2 * core
    blocks, depth, tile = both.shape[1], both.shape[3], both.shape[4]
    piece = min(1024, turned.shape[0])
    part = piece // (2 * depth)

    def move(number):
        slot = lax.rem(number, 2)
        return remote(
            both.at[slot, :, 1 - core], got.at[number], send.at[number], recv.at[number], "fsdp", twin
        )

    @pl.when(step == 0)
    def _():
        greet([("fsdp", twin)] + (others("seq", n) if beside else []))
        if beside:
            for copy in exchange_copies(n, [given], [taken], esend, erecv, local):
                copy.start()
        if not flipped:
            turned[...] = a_ref[...].T

    begin = 0
    for b_ref, count in zip(bs, counts):

        @pl.when((step >= begin) & (step < begin + count))
        def _(b_ref=b_ref):
            slot = lax.rem(step, 2)

            @pl.when(step >= 2)
            def _():
                move(step - 2).wait_send()

            for i in range(turned.shape[0] // piece):
                rows = dot(turned[i * piece : i * piece + piece, :], b_ref[...]).astype(BF)
                both[slot, i * part : i * part + part] = rows.reshape(part, 2, depth, tile)
            move(step).start()

        begin += count

    @pl.when(step >= 1)
    def _():
        last = step - 1
        move(last).wait_recv()
        lead = out_ref.shape[0]
        inner = blocks // lead
        for i in range(lead):
            own = both[lax.rem(last, 2), i * inner : i * inner + inner, core]
            other = got[last, i * inner : i * inner + inner]
            total = (own.astype(F32) + other.astype(F32)).astype(BF)
            out_ref[i] = total.reshape(inner * depth, tile)

    @pl.when(step == tiles)
    def _():
        if tiles >= 2:
            move(tiles - 2).wait_send()
        move(tiles - 1).wait_send()
        if beside:
            for copy in exchange_copies(n, [given], [taken], esend, erecv, local):
                copy.wait()


def exchange_copies(n, ins, outs, send, recv, local):
    me = lax.axis_index("seq")
    copies = []
    for i, (source, out) in enumerate(zip(ins, outs)):
        for j in range(1, n):
            to = lax.rem(me + j, n)
            k = i * (n - 1) + j - 1
            copies.append(
                remote(source.at[to], out.at[me], send.at[k], recv.at[k], "seq", to)
            )
        copies.append(pltpu.make_async_copy(source.at[me], out.at[me], local.at[i]))
    return copies


def exchange(n, source, out, send, recv, local):
    greet(others("seq", n))
    copies = exchange_copies(n, [source], [out], send, recv, local)
    for copy in copies:
        copy.start()
    for copy in copies:
        copy.wait()


def widen(pieces, *refs):
    ins, outs = refs[: -len(pieces)], refs[-len(pieces) :]
    for out, (i, begin, count) in zip(outs, pieces):
        out[...] = ins[i][0, :, begin : begin + count].astype(F32)


def last_stage(n, nf, dq, dk, dv, w, x, gain, gu, two, gq, gk, out, gu_out, gains, part, slots, stage, send, recv, row, small, wide, mid, seen, esend, erecv, local, gsend, grecv):
    me, spot = lax.axis_index("seq"), lax.axis_index("fsdp")
    greet(others("seq", n) + others("fsdp", nf))
    row[...] = jnp.zeros_like(row)
    rows, width = x.shape
    qw, kw = dq.shape[1], dk.shape[1]
    step = 512

    def block(to):
        at = pl.ds(pl.multiple_of(to * rows, rows), rows)

        def columns(number, carry):
            span = pl.ds(pl.multiple_of(number * step, step), step)
            value = dot_nt(dq[at, :], w[span, pl.ds(0, qw)])
            value += dot_nt(dk[at, :], w[span, pl.ds(qw, kw)])
            value += dot_nt(dv[at, :], w[span, pl.ds(qw + kw, kw)])
            part[to, :, span] = value.astype(BF)
            return carry

        lax.fori_loop(0, width // step, columns, 0)

    def finish(at, total):
        back, dg = norm_back(x[at].astype(F32), gain[...], total)
        out[at] = back
        row[...] += dg

    start, relay, lower, upper = scatter_parts(n, part, slots, stage, send, recv, finish)
    exchanges = exchange_copies(n, [gu], [gu_out], esend, erecv, local)
    if n == 4:
        across, along, corner = square(me)
        block(corner)
        start(0, 2)
        block(across)
        start(2, 3)
        block(along)
        start(3, 4)
        relay()
        for copy in exchanges:
            copy.start()
        block(me)
    else:
        for j in range(n):
            block(lax.rem(me + j, n))
        start()
        for copy in exchanges:
            copy.start()
    lower()
    upper()
    small[...] = jnp.zeros_like(small)
    per = 128 * n * nf // width
    one = row[...]
    for f in range(nf):
        for seq in range(n):
            line = (seq * nf + f) // per
            small[f, seq, 0:1] = one[:, line * 128 : line * 128 + 128]
            small[f, seq, 1:2] = two[line : line + 1]
            small[f, seq, 2:3] = gq[0:1]
            small[f, seq, 3:4] = gk[0:1]
    far = []
    for j in range(1, nf):
        to = lax.rem(spot + j, nf)
        far.append(
            remote(small.at[to], wide.at[j - 1], gsend.at[j - 1], grecv.at[j - 1], "fsdp", to)
        )
    for copy in far:
        copy.start()
    for copy in far:
        copy.wait_recv()
    total = small[spot]
    for j in range(nf - 1):
        total += wide[j]
    mid[...] = total
    near = []
    for j in range(1, n):
        to = lax.rem(me + j, n)
        k = nf + j - 2
        near.append(remote(mid.at[to], seen.at[j - 1], gsend.at[k], grecv.at[k], "seq", to))
    for copy in near:
        copy.start()
    for copy in near:
        copy.wait_recv()
    result = mid[me]
    for j in range(n - 1):
        result += seen[j]
    gains[...] = result
    for copy in far + near:
        copy.wait_send()
    for copy in exchanges:
        copy.wait()


def after(value, done):
    return lax.optimization_barrier((value, done))[0]


def dma(count):
    return pltpu.SemaphoreType.DMA((count,))


def shards(
    n,
    nf,
    tokens,
    seq_lengths,
    pic_starts,
    pic_lengths,
    norm1_gain,
    w_query,
    w_key,
    w_value,
    q_gain,
    k_gain,
    w_out,
    norm2_gain,
    w_gate,
    w_up,
    w_down,
    cotangent,
):
    rows, width = tokens.shape
    group = rows * n
    depth = w_query.shape[0]
    head = q_gain.shape[0] * n * nf
    qw, kw = w_query.shape[1] // n, w_key.shape[1] // n
    cw = qw + 2 * kw
    fw = w_gate.shape[1] // n
    qheads, kheads = qw // head, kw // head
    ratio = qheads // kheads
    own_gain = norm1_gain.shape[0]
    own_head = q_gain.shape[0]

    spot = lax.axis_index("fsdp")
    owner = lax.axis_index("seq") * nf + spot
    lanes = jnp.arange(128, dtype=jnp.int32)[None, :]

    def placed(gain, mine):
        count = gain.shape[0]
        wide = jnp.tile(gain.astype(F32), 128 // count)[None, :]
        return jnp.where(lax.div(lanes, count) == mine, wide, 0.0)

    sharing = 128 // own_gain
    packed = jnp.concatenate(
        [
            placed(norm1_gain, lax.rem(spot, sharing)),
            placed(norm2_gain, lax.rem(spot, sharing)),
            placed(q_gain, owner),
            placed(k_gain, owner),
            jnp.zeros((4, 128), F32),
        ],
        axis=0,
    )
    w_att = pl.pallas_call(
        functools.partial(attention_weights_out, n),
        out_shape=shape((n, depth, cw), BF),
        in_specs=[ANY] * 3,
        out_specs=ANY,
        scratch_shapes=[dma(3 * (n - 1)), dma(3 * (n - 1)), dma(3)],
        compiler_params=comm_params(0),
    )(w_query, w_key, w_value)
    gu, all_gains = pl.pallas_call(
        functools.partial(gate_up_out, n, nf),
        out_shape=(shape((n, depth, 2 * fw), BF), shape((nf, n, 8, 128), F32)),
        in_specs=[ANY] * 3,
        out_specs=(ANY, ANY),
        scratch_shapes=[
            pltpu.VMEM((n, 8, 128), F32),
            dma(2 * (n - 1)),
            dma(2 * (n - 1)),
            dma(2),
            dma(n + nf - 2),
            dma(n + nf - 2),
            dma(2),
        ],
        compiler_params=comm_params(8),
    )(after(w_gate, w_att), w_up, packed)
    gather_sems = [dma(gather_copies(n)), dma(gather_copies(n)), pltpu.SemaphoreType.DMA]
    line = nf == 8
    w_att = lax.all_gather(w_att, "fsdp", axis=1, tiled=True).reshape(width, cw)
    half = head // 2
    powers = -(np.arange(half, dtype=np.float32) * np.float32(2.0) / np.float32(head))
    freq = np.tile((np.float32(theta) ** powers).astype(np.float32), 2)[None, :]
    small = pl.BlockSpec(memory_space=pltpu.SMEM)
    xg, dn, wo, gain_one, gain_two, gain_q, gain_k, cos, sin, low, high = pl.pallas_call(
        functools.partial(entry_stage, n, nf, line, own_gain),
        out_shape=(
            shape((n, rows, width), BF),
            shape((n, depth, fw), BF),
            shape((nf if line else 1, depth, width), BF),
            shape((1, width), F32),
            shape((1, width), F32),
            shape((1, head), F32),
            shape((1, head), F32),
            shape((group, head), F32),
            shape((group, head), F32),
            shape((8, group), jnp.int32),
            shape((8, group), jnp.int32),
        ),
        in_specs=[ANY] * 3 + [VMEM] + [small] * 3 + [VMEM],
        out_specs=(ANY,) * 3 + (VMEM,) * 8,
        scratch_shapes=gather_sems
        + [dma(n - 1), dma(n - 1), dma(1), dma(10), dma(10), pltpu.SemaphoreType.DMA],
        compiler_params=comm_params(1),
    )(after(tokens, gu), w_down.T, w_out, all_gains, seq_lengths, pic_starts, pic_lengths, jnp.asarray(freq))
    wo = wo.reshape(-1, width)
    if not line:
        wo = lax.all_gather(wo, "fsdp", axis=0, tiled=True)
    gu = lax.all_gather(gu, "fsdp", axis=1, tiled=True).reshape(width, 2 * fw)
    dn = lax.all_gather(dn, "fsdp", axis=1, tiled=True).reshape(width, fw)

    def whole(dims):
        return pl.BlockSpec(dims, lambda *ids: (0,) * len(dims))

    def by_rows(count, columns):
        return pl.BlockSpec((count, columns), lambda i: (i, 0))

    def by_cols(count, columns):
        return pl.BlockSpec((count, columns), lambda i: (0, i))

    blocks = group // 256
    n1, qraw, kraw, q, k, v, kt, vt, cg = pl.pallas_call(
        functools.partial(project, n),
        grid=(blocks,),
        out_shape=(
            shape((width, group), BF),
            shape((group, qw), F32),
            shape((group, kw), F32),
            shape((group, qw), BF),
            shape((group, kw), BF),
            shape((group, kw), BF),
            shape((kw, group), BF),
            shape((kw, group), BF),
            shape((n, rows, width), BF),
        ),
        in_specs=[
            by_rows(256, width),
            whole((1, width)),
            whole((width, cw)),
            whole((1, head)),
            whole((1, head)),
            by_rows(256, head),
            by_rows(256, head),
            ANY,
        ],
        out_specs=(
            by_cols(width, 256),
            by_rows(256, qw),
            by_rows(256, kw),
            by_rows(256, qw),
            by_rows(256, kw),
            by_rows(256, kw),
            by_cols(kw, 256),
            by_cols(kw, 256),
            ANY,
        ),
        scratch_shapes=gather_sems,
        compiler_params=comm_params(11),
    )(xg.reshape(group, width), gain_one, w_att, gain_q, gain_k, cos, sin, cotangent)

    attn, lse, part_out, cg = pl.pallas_call(
        functools.partial(attend, n),
        grid=(blocks,),
        out_shape=(
            shape((group, qw), BF),
            shape((8, group), F32),
            shape((group, width), BF),
            shape((n, rows, width), BF),
        ),
        in_specs=[
            by_rows(256, qw),
            whole((group, kw)),
            whole((kw, group)),
            whole((qw, width)),
            by_cols(8, 256),
            by_cols(8, 256),
            ANY,
            ANY,
        ],
        out_specs=(by_rows(256, qw), by_cols(8, 256), by_rows(256, width), ANY),
        scratch_shapes=[pltpu.VMEM((group, 256), F32)] + gather_sems,
        input_output_aliases={7: 3},
        compiler_params=comm_params(3),
    )(q, k, vt, wo, low, high, cotangent, cg)
    cg = cg.reshape(group, width)

    slots = [
        pltpu.VMEM((scatter_slots(n), rows, width), BF),
        pltpu.VMEM((rows, width), BF),
    ]
    sems = [dma(max(6, n - 1)), dma(max(6, n - 1))]

    x2, n2 = pl.pallas_call(
        functools.partial(middle_stage, n),
        out_shape=(shape((rows, width), F32), shape((n, rows, width), BF)),
        in_specs=[VMEM] * 3,
        out_specs=(VMEM, ANY),
        scratch_shapes=slots + [pltpu.VMEM((rows, width), BF)] + sems + gather_sems,
        compiler_params=comm_params(2),
    )(part_out.reshape(n, rows, width), tokens, gain_two)
    n2 = n2.reshape(group, width)

    tile = 256
    tiles = fw // tile
    cuts = 1
    while 2 * cuts <= tiles:
        cuts *= 2
    gate, up, hidden, n2_turned = pl.pallas_call(
        functools.partial(ffn_forward, cuts),
        grid=(tiles,),
        out_shape=(
            shape((group, fw), F32),
            shape((group, fw), F32),
            shape((group, fw), BF),
            shape((width, group), BF),
        ),
        in_specs=[
            whole((group, width)),
            by_cols(width, tile),
            pl.BlockSpec((width, tile), lambda i: (0, i + tiles)),
        ],
        out_specs=(by_cols(group, tile),) * 3
        + (pl.BlockSpec((width // cuts, group), lambda i: (jnp.minimum(i, cuts - 1), 0)),),
        compiler_params=plain_params(),
    )(n2, gu, gu)

    def product(number, a, *bs, into=None, flipped=False, given=None):
        tile = 512
        while any(b.shape[1] % tile for b in bs):
            tile //= 2
        counts = [b.shape[1] // tile for b in bs]
        begins = [sum(counts[:i]) for i in range(len(bs))]
        tiles = sum(counts)

        def spec(begin, count):
            return pl.BlockSpec(
                (group, tile), lambda i: (0, jnp.clip(i - begin, 0, count - 1))
            )

        dims = (n, width // n // 2, tiles * tile) if into is None else into.shape
        kept = [] if into is None else [into]
        side = [] if given is None else [given]
        blocks = width // (2 * depth)
        outs = [pl.BlockSpec((n, dims[1], tile), lambda i: (0, 0, jnp.maximum(i - 1, 0)))]
        extra = [dma(n - 1), dma(n - 1), dma(1)] if side else []
        result = pl.pallas_call(
            functools.partial(gradient, n, counts, len(kept), flipped, len(side)),
            grid=(tiles + 1,),
            out_shape=(shape(dims, BF),) + tuple(shape(g.shape, BF) for g in side),
            in_specs=[whole(a.shape)]
            + [spec(b, c) for b, c in zip(begins, counts)]
            + [ANY] * len(kept + side),
            out_specs=tuple(outs + [ANY] * len(side)),
            scratch_shapes=[
                pltpu.VMEM((2, blocks, 2, depth, tile), BF),
                pltpu.VMEM((tiles, blocks, depth, tile), BF),
                dma(tiles),
                dma(tiles),
            ]
            + extra
            + ([] if flipped else [pltpu.VMEM((width, group), BF)]),
            input_output_aliases={} if into is None else {1 + len(bs): 0},
            compiler_params=comm_params(number),
        )(a, *bs, *kept, *side)
        return result if side else result[0]

    same_core = [[core + 2 * i for i in range(nf // 2)] for core in range(2)]

    def reduce_rows(grad):
        return lax.psum_scatter(
            grad, "fsdp", scatter_dimension=1, tiled=True, axis_index_groups=same_core
        )

    dn_grad = product(12, cg, hidden)
    dn_share = reduce_rows(dn_grad)

    dgate, dup = pl.pallas_call(
        ffn_back,
        grid=(tiles,),
        out_shape=(shape((group, fw), BF), shape((group, fw), BF)),
        in_specs=[
            whole((group, width)),
            by_cols(width, tile),
            by_cols(group, tile),
            by_cols(group, tile),
        ],
        out_specs=(by_cols(group, tile),) * 2,
        compiler_params=plain_params(),
    )(cg, after(dn, dn_grad), gate, up)

    gu_grad = product(13, n2_turned, dgate, dup, flipped=True)
    gu_share = reduce_rows(gu_grad)

    dx2, dz, dgain_two, part_y = pl.pallas_call(
        functools.partial(back_stage, n),
        out_shape=(
            shape((rows, width), F32),
            shape((n, rows, width), BF),
            shape((width // 128, 128), F32),
            shape((n, rows, width), BF),
        ),
        in_specs=[ANY] * 3 + [VMEM] * 3 + [ANY] * 2,
        out_specs=(VMEM, ANY, VMEM, VMEM),
        scratch_shapes=[pltpu.VMEM((n, rows, width), BF)]
        + slots
        + [pltpu.VMEM((rows, width), BF)]
        + sems
        + gather_sems
        + [
            pltpu.VMEM((1, width), F32),
            pltpu.VMEM((group, fw), BF),
            pltpu.VMEM((width, fw), BF),
            dma(2),
            pltpu.VMEM((group, fw), BF),
            pltpu.VMEM((group, fw), BF),
            pltpu.VMEM((width, 2 * fw), BF),
            pltpu.SemaphoreType.DMA((2, n)),
            dma(width // 512),
        ],
        compiler_params=comm_params(4),
    )(
        after(dgate, gu_grad), dup, gu, x2, cotangent, gain_two, hidden, dn,
    )
    dz = dz.reshape(group, width)

    wide = ratio * head
    dq, dk, dv, dgain_q, dgain_k, branch, wo_grad = pl.pallas_call(
        functools.partial(attend_back, n),
        grid=(kheads, blocks),
        out_shape=(
            shape((group, qw), BF),
            shape((group, kw), BF),
            shape((group, kw), BF),
            shape((8, head), F32),
            shape((8, head), F32),
            shape((rows, width), F32),
            shape((n + width // cw, width // n // 2, cw), BF),
        ),
        in_specs=[
            pl.BlockSpec((256, wide), lambda h, b: (b, h)),
            pl.BlockSpec((256, wide), lambda h, b: (b, h)),
            pl.BlockSpec((group, head), lambda h, b: (0, h)),
            pl.BlockSpec((head, group), lambda h, b: (h, 0)),
            pl.BlockSpec((group, head), lambda h, b: (0, h)),
            pl.BlockSpec((group, head), lambda h, b: (0, h)),
            pl.BlockSpec((256, width), lambda h, b: (b, 0)),
            pl.BlockSpec((wide, width), lambda h, b: (h, 0)),
            pl.BlockSpec((8, 256), lambda h, b: (0, b)),
            pl.BlockSpec((8, 256), lambda h, b: (0, b)),
            pl.BlockSpec((8, 256), lambda h, b: (0, b)),
            pl.BlockSpec((256, head), lambda h, b: (b, 0)),
            pl.BlockSpec((256, head), lambda h, b: (b, 0)),
            whole((group, head)),
            whole((group, head)),
            whole((1, head)),
            whole((1, head)),
            pl.BlockSpec((256, wide), lambda h, b: (b, h)),
            VMEM,
        ],
        out_specs=(
            pl.BlockSpec((256, wide), lambda h, b: (b, h)),
            pl.BlockSpec((group, head), lambda h, b: (0, h)),
            pl.BlockSpec((group, head), lambda h, b: (0, h)),
            whole((8, head)),
            whole((8, head)),
            VMEM,
            ANY,
        ),
        scratch_shapes=[pltpu.VMEM((group, head), F32), pltpu.VMEM((group, head), F32)]
        + slots
        + sems
        + [
            pltpu.VMEM((wide, width), F32),
            pltpu.VMEM((kheads, wide // (2 * depth), 2, depth, width), BF),
            pltpu.VMEM((kheads, wide // (2 * depth), depth, width), BF),
            pltpu.VMEM((kheads, wide // 2, width), BF),
            dma(kheads),
            dma(kheads),
            pltpu.SemaphoreType.DMA((kheads, width // cw)),
        ],
        compiler_params=comm_params(5),
    )(
        q, qraw, k, kt, v, kraw, dz, wo, lse, low, high, cos, sin, cos, sin, gain_q, gain_k,
        attn, part_y,
    )
    output = (x2 + branch).astype(BF)

    att_grad, dn_mine = product(
        15, n1, dq, dk, dv, into=wo_grad, flipped=True, given=dn_share
    )
    att_share = reduce_rows(after(att_grad, gu_share))

    back_one, gu_mine, gains = pl.pallas_call(
        functools.partial(last_stage, n, nf),
        out_shape=(
            shape((rows, width), F32),
            shape(gu_share.shape, BF),
            shape((8, 128), F32),
        ),
        in_specs=[VMEM] * 6 + [ANY] + [VMEM] * 3,
        out_specs=(VMEM, ANY, VMEM),
        scratch_shapes=[pltpu.VMEM((n, rows, width), BF)]
        + slots
        + sems
        + [
            pltpu.VMEM((1, width), F32),
            pltpu.VMEM((nf, n, 8, 128), F32),
            pltpu.VMEM((nf - 1, n, 8, 128), F32),
            pltpu.VMEM((n, 8, 128), F32),
            pltpu.VMEM((n - 1, 8, 128), F32),
            dma(n - 1),
            dma(n - 1),
            dma(1),
            dma(n + nf - 2),
            dma(n + nf - 2),
        ],
        compiler_params=comm_params(7),
    )(
        after(dq, att_grad), dk, dv, w_att, tokens, gain_one, gu_share,
        dgain_two, dgain_q, dgain_k,
    )
    input_grad = (dx2 + back_one).astype(BF)

    def owned(row, count, mine):
        return lax.dynamic_slice_in_dim(row, mine * count, count, 0)

    gain_grads = (
        owned(gains[0], own_gain, lax.rem(spot, sharing)),
        owned(gains[1], own_gain, lax.rem(spot, sharing)),
        owned(gains[2], own_head, owner),
        owned(gains[3], own_head, owner),
    )

    def spread(arrays, pieces):
        ins = [pl.BlockSpec((1, depth, a.shape[2]), lambda i: (i, 0, 0)) for a in arrays]
        outs = [by_cols(depth, count) for _, _, count in pieces]
        shapes = [shape((depth, n * count), F32) for _, _, count in pieces]
        return pl.pallas_call(
            functools.partial(widen, pieces),
            grid=(n,),
            out_shape=tuple(shapes),
            in_specs=ins,
            out_specs=tuple(outs),
            compiler_params=plain_params(),
        )(*arrays)

    gate_grad, up_grad, down_grad = spread(
        [gu_mine, dn_mine], [(0, 0, fw), (0, fw, fw), (1, 0, fw)]
    )
    wide_grads = (gate_grad, up_grad, down_grad.T)
    wo_out = att_share[n:].transpose(1, 0, 2).reshape(depth, width).astype(F32)
    att_mine = pl.pallas_call(
        functools.partial(exchange, n),
        out_shape=shape((n, depth, cw), BF),
        in_specs=[ANY],
        out_specs=ANY,
        scratch_shapes=[dma(n - 1), dma(n - 1), dma(1)],
        compiler_params=comm_params(9),
    )(after(att_share, (gain_grads, wide_grads, input_grad, output)))
    wq_grad, wk_grad, wv_grad = spread(
        [att_mine], [(0, 0, qw), (0, qw, kw), (0, qw + kw, kw)]
    )

    return (
        output,
        input_grad,
        gain_grads[0],
        wq_grad,
        wk_grad,
        wv_grad,
        gain_grads[2],
        gain_grads[3],
        wo_out,
        gain_grads[1],
    ) + wide_grads


def solution(mesh):
    return jax.shard_map(
        functools.partial(shards, mesh.shape["seq"], mesh.shape["fsdp"]),
        mesh=mesh,
        in_specs=(
            P(("fsdp", "seq"), None),
            P("fsdp", None),
            P("fsdp", None),
            P("fsdp", None),
            P(("seq", "fsdp")),
            P(("seq", "fsdp"), None),
            P(("seq", "fsdp"), None),
            P(("seq", "fsdp"), None),
            P(("seq", "fsdp")),
            P(("seq", "fsdp")),
            P(("seq", "fsdp"), None),
            P(("seq", "fsdp")),
            P(("seq", "fsdp"), None),
            P(("seq", "fsdp"), None),
            P(None, ("seq", "fsdp")),
            P(("fsdp", "seq"), None),
        ),
        out_specs=(
            P(("fsdp", "seq"), None),
            P(("fsdp", "seq"), None),
            P(("seq", "fsdp")),
            P(("seq", "fsdp"), None),
            P(("seq", "fsdp"), None),
            P(("seq", "fsdp"), None),
            P(("seq", "fsdp")),
            P(("seq", "fsdp")),
            P(("seq", "fsdp"), None),
            P(("seq", "fsdp")),
            P(("seq", "fsdp"), None),
            P(("seq", "fsdp"), None),
            P(None, ("seq", "fsdp")),
        ),
        check_vma=False,
    )
```

```python
import functools

import jax
import jax.numpy as jnp
import numpy as np
from jax import lax
from jax.experimental import pallas as pl
from jax.experimental.pallas import tpu as pltpu
from jax.sharding import PartitionSpec as P

epsilon = 1e-06
theta = 1000000.0
masked_score = -1e30
log2e = 1.4426950408889634

MESH = pl.DeviceIdType.MESH
ANY = pl.BlockSpec(memory_space=pl.ANY)
VMEM = pl.BlockSpec(memory_space=pltpu.VMEM)
BF = jnp.bfloat16
F32 = jnp.float32
LIMIT = 60 * 1024 * 1024


def dot(a, b):
    return jnp.dot(a, b, preferred_element_type=F32)


def dot_nt(a, b):
    return lax.dot_general(a, b, (((1,), (1,)), ((), ())), preferred_element_type=F32)


def dot_tn(a, b):
    return lax.dot_general(a, b, (((0,), (0,)), ((), ())), preferred_element_type=F32)


def shape(dims, dtype):
    return jax.ShapeDtypeStruct(dims, dtype)


def comm_params(number):
    return pltpu.CompilerParams(
        collective_id=number, has_side_effects=True, vmem_limit_bytes=LIMIT
    )


def plain_params():
    return pltpu.CompilerParams(vmem_limit_bytes=LIMIT)


def remote(src, dst, send, recv, axis, index):
    return pltpu.make_async_remote_copy(
        src_ref=src,
        dst_ref=dst,
        send_sem=send,
        recv_sem=recv,
        device_id={axis: index},
        device_id_type=MESH,
    )


def greet(places):
    barrier = pltpu.get_barrier_semaphore()
    for axis, index in places:
        pl.semaphore_signal(barrier, inc=1, device_id={axis: index}, device_id_type=MESH)
    pl.semaphore_wait(barrier, len(places))


def others(axis, n):
    me = lax.axis_index(axis)
    return [(axis, lax.rem(me + j, n)) for j in range(1, n)]


def square(me):
    return me + 1 - 2 * lax.rem(me, 2), lax.rem(me + 2, 4), 3 - me


def ring_places(n):
    me = lax.axis_index("seq")
    if n == 4:
        across, along, _ = square(me)
        return [("seq", across), ("seq", along)]
    return others("seq", n)


def gather_copies(n):
    return 6 if n == 4 else n - 1


def gather_parts(n, own, out, send, recv, local):
    me = lax.axis_index("seq")
    keep = pltpu.make_async_copy(own, out.at[me], local)
    half = own.shape[0] // 2
    low, high = pl.ds(0, half), pl.ds(half, half)
    if n == 4:
        across, along, _ = square(me)
        moves = [
            (own.at[low], out.at[me, low], across),
            (own.at[high], out.at[me, high], along),
            (own.at[high], out.at[me, high], across),
            (own.at[low], out.at[me, low], along),
            (out.at[across, low], out.at[across, low], along),
            (out.at[along, high], out.at[along, high], across),
        ]
    else:
        moves = [(own, out.at[me], lax.rem(me + j, n)) for j in range(1, n)]
    copies = [
        remote(src, dst, send.at[i], recv.at[i], "seq", to)
        for i, (src, dst, to) in enumerate(moves)
    ]

    def start(part=None):
        chosen = range(len(copies))
        if n == 4:
            chosen = {None: (0, 1, 2, 3), 0: (0, 3), 1: (1, 2)}[part]
        if n == 4 or part != 0:
            for i in chosen:
                copies[i].start()
        if part != 0:
            keep.start()

    def relay():
        if n == 4:
            copies[0].wait_recv()
            copies[4].start()
            copies[1].wait_recv()
            copies[5].start()

    def finish():
        for copy in copies[2:] if n == 4 else copies:
            copy.wait_recv()
        for copy in copies:
            copy.wait_send()
        keep.wait()

    return start, relay, finish


def gather(n, own, out, send, recv, local):
    for part in gather_parts(n, own, out, send, recv, local):
        part()


def scatter_slots(n):
    return 4 if n == 4 else n - 1


def scatter_sum(n, part, slots, stage, send, recv, finish):
    start, relay, lower, upper = scatter_parts(n, part, slots, stage, send, recv, finish)
    start()
    relay()
    lower()
    upper()


def scatter_parts(n, part, slots, stage, send, recv, finish):
    me = lax.axis_index("seq")
    rows = part.shape[1]
    half = rows // 2
    low, high = pl.ds(0, half), pl.ds(half, half)
    if n == 4:
        across, along, corner = square(me)
        moves = [
            (part.at[corner, low], slots.at[2, low], along),
            (part.at[corner, high], slots.at[2, high], across),
            (part.at[across, high], slots.at[0, high], across),
            (part.at[along, low], slots.at[1, low], along),
            (stage.at[low], slots.at[0, low], across),
            (stage.at[high], slots.at[1, high], along),
        ]
        count = 2
    else:
        moves = []
        for j in range(1, n):
            to = lax.rem(me + j, n)
            moves.append((part.at[to], slots.at[j - 1], to))
        count = n - 1
    copies = [
        remote(src, dst, send.at[i], recv.at[i], "seq", to)
        for i, (src, dst, to) in enumerate(moves)
    ]

    def start(*chosen):
        chosen = chosen if chosen else (0, 1, 3)
        for copy in [copies[i] for i in chosen] if n == 4 else copies:
            copy.start()

    def relay():
        if n == 4:
            copies[0].wait_recv()
            stage[low] = (part[across, low].astype(F32) + slots[2, low].astype(F32)).astype(BF)
            copies[4].start()
            copies[2].start()
            copies[1].wait_recv()
            stage[high] = (part[along, high].astype(F32) + slots[2, high].astype(F32)).astype(BF)
            copies[5].start()

    step = 32

    def chunk(number, carry):
        at = pl.ds(pl.multiple_of(number * step, step), step)
        value = part[me, at].astype(F32)
        for slot in range(count):
            value += slots[slot, at].astype(F32)
        finish(at, value)
        return carry

    def lower():
        for copy in copies[3:5] if n == 4 else copies:
            copy.wait_recv()
        lax.fori_loop(0, half // step, chunk, 0)

    def upper():
        if n == 4:
            copies[2].wait_recv()
            copies[5].wait_recv()
        lax.fori_loop(half // step, rows // step, chunk, 0)
        for copy in copies:
            copy.wait_send()

    return start, relay, lower, upper


def inverse_rms(values):
    return lax.rsqrt(jnp.mean(values * values, axis=-1, keepdims=True) + epsilon)


def norm_back(values, gain, grad):
    inverse = inverse_rms(values)
    scaled = grad * gain
    back = inverse * scaled - values * (
        inverse * inverse * inverse * jnp.mean(scaled * values, axis=-1, keepdims=True)
    )
    return back, jnp.sum(grad * values * inverse, axis=0, keepdims=True)


def start_columns(n, views, send, recv, local, begin=True):
    me = lax.axis_index("seq")
    width = views[0][0].shape[1] // n
    copies, keeps = [], []
    for i, (ref, out, place) in enumerate(views):
        for j in range(1, n):
            to = lax.rem(me + j, n)
            columns = pl.ds(pl.multiple_of(to * width, 128), width)
            k = i * (n - 1) + j - 1
            copies.append(
                remote(
                    ref.at[:, columns],
                    out.at[me, :, pl.ds(place * width, width)],
                    send.at[k],
                    recv.at[k],
                    "seq",
                    to,
                )
            )
        columns = pl.ds(pl.multiple_of(me * width, 128), width)
        keeps.append(
            pltpu.make_async_copy(
                ref.at[:, columns], out.at[me, :, pl.ds(place * width, width)], local.at[i]
            )
        )
    if begin:
        for copy in copies + keeps:
            copy.start()
    return copies + keeps


def line_gather(cell, own, send, recv):
    spot = lax.axis_index("fsdp")
    z = lax.div(spot, 2)
    twin = spot + 1 - 2 * lax.rem(spot, 2)

    def hop(number, block, to):
        source = own if isinstance(block, str) else cell(block)
        target = cell(spot if isinstance(block, str) else block)
        return remote(source, target, send.at[number], recv.at[number], "fsdp", to)

    def up(k):
        return hop(k, "own" if k == 0 else spot - 2 * k, spot + 2)

    def down(k):
        return hop(3 + k, "own" if k == 0 else spot + 2 * k, spot - 2)

    def over(offset):
        return hop(6 + z + offset, "own" if offset == 0 else spot + 2 * offset, twin)

    def from_twin(offset):
        return hop(6 + z + offset, twin + 2 * offset, twin)

    def first():
        @pl.when(z < 3)
        def _():
            up(0).start()

        @pl.when(z > 0)
        def _():
            down(0).start()

        over(0).start()

    def step(k):
        @pl.when(z >= k)
        def _():
            up(k - 1).wait_recv()
            if k < 3:

                @pl.when(z < 3)
                def _():
                    up(k).start()

            over(-k).start()

        @pl.when(z + k <= 3)
        def _():
            down(k - 1).wait_recv()
            if k < 3:

                @pl.when(z > 0)
                def _():
                    down(k).start()

            over(k).start()

    def finish():
        from_twin(0).wait_recv()
        over(0).wait_send()
        for k in range(1, 4):

            @pl.when(z >= k)
            def _():
                from_twin(-k).wait_recv()
                over(-k).wait_send()

            @pl.when(z + k <= 3)
            def _():
                from_twin(k).wait_recv()
                over(k).wait_send()

        for k in range(3):

            @pl.when((z >= k) & (z < 3))
            def _():
                up(k).wait_send()

            @pl.when((z + k <= 3) & (z > 0))
            def _():
                down(k).wait_send()

    return first, step, finish


def entry_stage(n, nf, line, own_gain, own_head, wq, wk, wv, wg, wu, x, w_out, raw, lengths, starts, sizes, freq, w_att, gu, xg, wo, gain_one, gain_two, gain_q, gain_k, cos, sin, low, high, mine, seen, gains, qsend, qrecv, qlocal, wsend, wrecv, wlocal, send, recv, local, gsend, grecv, glocal, asend, arecv, osend, orecv, olocal):
    me, spot = lax.axis_index("seq"), lax.axis_index("fsdp")
    greet(others("seq", n) + others("fsdp", nf))
    place = spot if line else 0
    if line:
        o_first, o_step, o_finish = line_gather(lambda f: wo.at[f], w_out, osend, orecv)
        a_first, a_step, a_finish = line_gather(
            lambda f: w_att.at[:, f], w_att.at[:, spot], asend, arecv
        )
        o_first()
    widths = [wq.shape[1] // n, wk.shape[1] // n, wv.shape[1] // n]
    begins = [0, widths[0], widths[0] + widths[1]]
    near = []
    for j in range(1, n):
        to = lax.rem(me + j, n)
        for i, ref in enumerate((wq, wk, wv)):
            columns = pl.ds(pl.multiple_of(to * widths[i], 128), widths[i])
            near.append(
                remote(
                    ref.at[:, columns],
                    w_att.at[me, place, :, pl.ds(begins[i], widths[i])],
                    qsend.at[3 * j - 3 + i],
                    qrecv.at[3 * j - 3 + i],
                    "seq",
                    to,
                )
            )
    for i, ref in enumerate((wq, wk, wv)):
        columns = pl.ds(pl.multiple_of(me * widths[i], 128), widths[i])
        near.append(
            pltpu.make_async_copy(
                ref.at[:, columns],
                w_att.at[me, place, :, pl.ds(begins[i], widths[i])],
                qlocal.at[i],
            )
        )
    for copy in near:
        copy.start()
    mine[...] = jnp.zeros_like(mine)
    for count, first, index in (
        (own_gain, 0, lax.rem(spot, 128 // own_gain)),
        (own_head, 2, me * nf + spot),
    ):
        for at in range(128 // count):

            @pl.when(index == at)
            def _():
                for i in (first, first + 1):
                    mine[i : i + 1, at * count : at * count + count] = raw[
                        :, i * 128 : i * 128 + count
                    ]

    small = [pltpu.make_async_copy(mine, seen.at[me], glocal.at[0])]
    for j in range(1, n):
        to = lax.rem(me + j, n)
        small.append(remote(mine, seen.at[me], gsend.at[j - 1], grecv.at[j - 1], "seq", to))
    keep = pltpu.make_async_copy(w_out, wo.at[place], olocal)
    for copy in small + [keep]:
        copy.start()
    def rope():
        group = cos.shape[0]
        border_one = lengths[0, 0]
        border_two = border_one + lengths[0, 1]

        def begin_of(places):
            later = jnp.where(places >= border_one, border_one, 0)
            return jnp.where(places >= border_two, border_two, later)

        step = 128
        lane = lax.broadcasted_iota(jnp.int32, (step, 128), 1)

        def turn(number, carry):
            at = pl.ds(pl.multiple_of(number * step, step), step)
            places = lax.broadcasted_iota(jnp.int32, (step, 128), 0) + number * step
            angle = (places - begin_of(places)).astype(F32) * freq[...]
            cos[at, :] = jnp.cos(angle)
            sine = jnp.sin(angle)
            sin[at, :] = jnp.where(lane < 64, -sine, sine)
            return carry

        lax.fori_loop(0, group // step, turn, 0)
        places = lax.broadcasted_iota(jnp.int32, (8, group), 1)
        end = jnp.where(places >= border_one, border_two, border_one)
        end = jnp.where(places >= border_two, group, end)
        picture = jnp.zeros_like(places)
        for i in range(starts.shape[1]):
            first, count = starts[0, i], sizes[0, i]
            inside = (places >= first) & (places < first + count)
            picture = jnp.where(inside, jnp.maximum(picture, first + count), picture)
        low[...] = begin_of(places)
        high[...] = jnp.maximum(places, jnp.minimum(picture, end) - 1)

    rope()
    for copy in near:
        copy.wait()
    if line:
        a_first()
    copies = start_columns(n, [(wg, gu, 0), (wu, gu, 1)], wsend, wrecv, wlocal)
    start, relay, finish = gather_parts(n, x, xg, send, recv, local)
    start()
    if line:
        o_step(1)
    for copy in small:
        copy.wait()
    wide = [pltpu.make_async_copy(seen, gains.at[spot], glocal.at[1])]
    for j in range(1, nf):
        to = lax.rem(spot + j, nf)
        k = n + j - 2
        wide.append(remote(seen, gains.at[spot], gsend.at[k], grecv.at[k], "fsdp", to))
    for copy in wide:
        copy.start()

    def unpack():
        per = 128 // own_gain
        for row in range(n * nf // per):
            seq, first = row * per // nf, row * per % nf
            one = gains[first, seq, 0:1, :]
            two = gains[first, seq, 1:2, :]
            for f in range(first + 1, first + per):
                one += gains[f, seq, 0:1, :]
                two += gains[f, seq, 1:2, :]
            gain_one[:, row * 128 : row * 128 + 128] = one
            gain_two[:, row * 128 : row * 128 + 128] = two
        total = jnp.zeros((8, 128), F32)
        for f in range(nf):
            for seq in range(n):
                total += gains[f, seq]
        gain_q[...] = total[2:3, :]
        gain_k[...] = total[3:4, :]

    if line:
        o_step(2)
        a_step(1)
    relay()
    if line:
        o_step(3)
        a_step(2)
        a_step(3)
        o_finish()
        a_finish()
    finish()
    keep.wait()
    for copy in wide:
        copy.wait()
    unpack()
    for copy in copies:
        copy.wait()


def half_gather(n, begin, cot, cg, send, recv, local, places, beside):
    at = pl.ds(begin, cot.shape[0] // 2)
    start, relay, finish = gather_parts(n, cot.at[at], cg.at[:, at], send, recv, local)
    step, steps = pl.program_id(0), pl.num_programs(0)

    @pl.when(step == 0)
    def _():
        greet(places)
        start()
        beside()

    @pl.when(step == steps - 1)
    def _():
        relay()

    return finish


def project(n, x_ref, gain_ref, w_ref, gq_ref, gk_ref, cos_ref, sin_ref, cot, n1_ref, qraw_ref, kraw_ref, q_ref, k_ref, v_ref, kt_ref, vt_ref, cg, send, recv, local):
    finish_half = half_gather(n, 0, cot, cg, send, recv, local, ring_places(n), lambda: None)
    x = x_ref[...].astype(F32)
    normed = (x * inverse_rms(x) * gain_ref[...]).astype(BF)
    n1_ref[...] = normed.T
    full = dot(normed, w_ref[...])
    qw, kw = q_ref.shape[1], k_ref.shape[1]
    cos, sin = cos_ref[...], sin_ref[...]

    def prep(head, gain):
        u = head * inverse_rms(head) * gain
        return u * cos + pltpu.roll(u, 64, 1) * sin

    qraw_ref[...] = full[:, :qw]
    kraw_ref[...] = full[:, qw : qw + kw]
    v = full[:, qw + kw :]
    v_ref[...] = v.astype(BF)
    vt_ref[...] = v.T.astype(BF)
    for h in range(qw // 128):
        q_ref[:, h * 128 : h * 128 + 128] = prep(
            full[:, h * 128 : h * 128 + 128], gq_ref[...]
        ).astype(BF)
    for h in range(kw // 128):
        turned = prep(full[:, qw + h * 128 : qw + h * 128 + 128], gk_ref[...])
        k_ref[:, h * 128 : h * 128 + 128] = turned.astype(BF)
        kt_ref[h * 128 : h * 128 + 128, :] = turned.T.astype(BF)

    @pl.when(pl.program_id(0) == pl.num_programs(0) - 1)
    def _():
        finish_half()


def bias_of(low_ref, high_ref, keys):
    key = lax.broadcasted_iota(jnp.int32, (keys, low_ref.shape[1]), 0)
    fine = (key >= low_ref[0:1, :]) & (key <= high_ref[0:1, :])
    return jnp.where(fine, 0.0, masked_score)


def attend(n, q_ref, k_ref, vt_ref, wo_ref, low_ref, high_ref, cot, cg_half, wd, attn_ref, lse_ref, part_ref, cg, dn, bias, send, recv, local, wsend, wrecv, wlocal):
    copies = start_columns(n, [(wd, dn, 0)], wsend, wrecv, wlocal, False)

    def beside():
        for copy in copies:
            copy.start()

    finish_half = half_gather(
        n, cot.shape[0] // 2, cot, cg, send, recv, local, others("seq", n), beside
    )
    keys = k_ref.shape[0]
    bias[...] = bias_of(low_ref, high_ref, keys)
    heads = q_ref.shape[1] // 128
    ratio = heads // (k_ref.shape[1] // 128)
    factor = 128 ** (-0.5) * log2e
    for h in range(heads):
        kv = h // ratio
        scores = dot_nt(
            k_ref[:, kv * 128 : kv * 128 + 128], q_ref[:, h * 128 : h * 128 + 128]
        )
        scores = scores * factor + bias[...]
        top = jnp.max(scores, axis=0, keepdims=True)
        probs = jnp.exp2(scores - top)
        total = jnp.sum(probs, axis=0, keepdims=True)
        mixed = dot(vt_ref[kv * 128 : kv * 128 + 128, :], probs.astype(BF))
        lse_ref[h : h + 1, :] = top + jnp.log2(total)
        attn_ref[:, h * 128 : h * 128 + 128] = (mixed / total).T.astype(BF)
    part_ref[...] = dot(attn_ref[...], wo_ref[...]).astype(BF)

    @pl.when(pl.program_id(0) == pl.num_programs(0) - 1)
    def _():
        finish_half()
        for copy in copies:
            copy.wait()


def middle_stage(n, part, x, gain, x2, n2, slots, stage, own, send, recv, asend, arecv, local):
    greet(ring_places(n))

    def finish(at, total):
        value = x[at].astype(F32) + total
        x2[at] = value
        own[at] = (value * inverse_rms(value) * gain[...]).astype(BF)

    start, relay, lower, upper = scatter_parts(n, part, slots, stage, send, recv, finish)
    send_on, pass_on, end = gather_parts(n, own, n2, asend, arecv, local)
    start()
    relay()
    lower()
    send_on(0)
    upper()
    send_on(1)
    pass_on()
    end()


def ffn_forward(cuts, n2_ref, wg_ref, wu_ref, gate_ref, up_ref, hidden_ref, turned_ref):
    count = n2_ref.shape[1] // cuts
    step = pl.program_id(0)

    @pl.when(step < cuts)
    def _():
        turned_ref[...] = n2_ref[:, pl.ds(pl.multiple_of(step * count, 128), count)].T

    gate = dot(n2_ref[...], wg_ref[...])
    up = dot(n2_ref[...], wu_ref[...])
    s = jax.nn.sigmoid(gate)
    silu = gate * s
    gate_ref[...] = up * (s * (1.0 + gate * (1.0 - s)))
    up_ref[...] = silu
    hidden_ref[...] = (silu * up).astype(BF)


def ffn_back(cot_ref, wd_ref, gate_ref, up_ref, dgate_ref, dup_ref):
    dh = dot(cot_ref[...], wd_ref[...])
    dgate_ref[...] = (dh * gate_ref[...]).astype(BF)
    dup_ref[...] = (dh * up_ref[...]).astype(BF)


def spread_rows(row, out):
    for i in range(out.shape[0]):
        out[i : i + 1, :] = row[:, i * 128 : i * 128 + 128]


def back_stage(n, dgate_far, dup_far, gu_far, x2, cot, gain, hidden_far, dn_far, dx2, dz, dgain, part_y, part, slots, stage, own, send, recv, asend, arecv, local, row, hidden, dn, load, dgate, dup, gu, rload, wload):
    greet(ring_places(n))
    me = lax.axis_index("seq")
    rows, width = x2.shape
    units = dup.shape[1]
    step = 512

    def row_loads(to):
        at = pl.ds(pl.multiple_of(to * rows, rows), rows)
        return [
            pltpu.make_async_copy(dgate_far.at[at], dgate.at[at], rload.at[0, to]),
            pltpu.make_async_copy(dup_far.at[at], dup.at[at], rload.at[1, to]),
        ]

    def weight_load(number):
        at = pl.ds(pl.multiple_of(number * step, step), step)
        return pltpu.make_async_copy(gu_far.at[at], gu.at[at], wload.at[number])

    order = [lax.rem(me + j, n) for j in range(1, n)] + [me]
    if n == 4:
        across, along, corner = square(me)
        order = [corner, across, along, me]
    for copy in row_loads(order[0]):
        copy.start()
    for number in range(width // step):
        weight_load(number).start()
    for copy in row_loads(order[1]):
        copy.start()
    loads = [
        pltpu.make_async_copy(hidden_far, hidden, load.at[0]),
        pltpu.make_async_copy(dn_far, dn, load.at[1]),
    ]

    def others_loads():
        for to in order[2:]:
            for copy in row_loads(to):
                copy.start()
        for copy in loads:
            copy.start()

    row[...] = jnp.zeros_like(row)

    def block(to, first=False):
        at = pl.ds(pl.multiple_of(to * rows, rows), rows)
        for copy in row_loads(to):
            copy.wait()

        def columns(number, carry):
            if first:
                weight_load(number).wait()
            span = pl.ds(pl.multiple_of(number * step, step), step)
            value = dot_nt(dgate[at, :], gu[span, pl.ds(0, units)])
            value += dot_nt(dup[at, :], gu[span, pl.ds(units, units)])
            part[to, :, span] = value.astype(BF)
            return carry

        lax.fori_loop(0, width // step, columns, 0)

    def forward(to, carry):
        at = pl.ds(pl.multiple_of(to * rows, rows), rows)

        def columns(number, carry):
            span = pl.ds(pl.multiple_of(number * step, step), step)
            part_y[to, :, span] = dot_nt(hidden[at, :], dn[span, :]).astype(BF)
            return carry

        return lax.fori_loop(0, width // step, columns, carry)

    def finish(at, total):
        back, dg = norm_back(x2[at], gain[...], total)
        value = cot[at].astype(F32) + back
        dx2[at] = value
        own[at] = value.astype(BF)
        row[...] += dg

    start, relay, lower, upper = scatter_parts(n, part, slots, stage, send, recv, finish)
    send_on, pass_on, end = gather_parts(n, own, dz, asend, arecv, local)
    if n == 4:
        block(corner, True)
        start(0, 1)
        others_loads()
        block(across)
        block(along)
        start(3)
        relay()
        block(me)
    else:
        block(order[0], True)
        others_loads()
        for to in order[1:]:
            block(to)
        start()
    for copy in loads:
        copy.wait()
    lax.fori_loop(0, n // 4, forward, 0)
    lower()
    send_on(0)
    upper()
    send_on(1)
    spread_rows(row[...], dgain)
    pass_on()
    lax.fori_loop(n // 4, n, forward, 0)
    end()


def attend_back(n, q_ref, qraw_ref, k_ref, kt_ref, v_ref, kraw_ref, dz_ref, wo_ref, lse_ref, low_ref, high_ref, cq_ref, sq_ref, ck_ref, sk_ref, gq_ref, gk_ref, attn_ref, part, x2, dq_ref, dk_ref, dv_ref, dgq_ref, dgk_ref, out, grads, dk_sum, dv_sum, slots, stage, send, recv, wo_sum, both, got, done, tsend, trecv, put):
    kv, block = pl.program_id(0), pl.program_id(1)
    keys = k_ref.shape[0]
    ratio = q_ref.shape[1] // 128
    scale = 128 ** (-0.5)

    def finish(at, total):
        out[at] = (x2[at] + total).astype(BF)

    start, relay, lower, upper = scatter_parts(n, part, slots, stage, send, recv, finish)
    core = lax.rem(lax.axis_index("fsdp"), 2)
    twin = lax.axis_index("fsdp") + 1 - 2 * core
    kheads, pieces, depth = both.shape[0], both.shape[1], both.shape[3]

    def move(number):
        return remote(
            both.at[number, :, 1 - core], got.at[number], tsend.at[number], trecv.at[number], "fsdp", twin
        )

    steps = pl.num_programs(0) * pl.num_programs(1)
    step = kv * pl.num_programs(1) + block

    @pl.when(step == 0)
    def _():
        greet(ring_places(n) + [("fsdp", twin)])
        start()
        dgq_ref[...] = jnp.zeros_like(dgq_ref)
        dgk_ref[...] = jnp.zeros_like(dgk_ref)

    @pl.when(step == steps // 2)
    def _():
        relay()

    @pl.when(block == 0)
    def _():
        dk_sum[...] = jnp.zeros_like(dk_sum)
        dv_sum[...] = jnp.zeros_like(dv_sum)
        wo_sum[...] = jnp.zeros_like(wo_sum)

    bias = bias_of(low_ref, high_ref, keys)
    dattn = dot_nt(dz_ref[...], wo_ref[...]).astype(BF)

    def prep_back(grad, raw, gain, cos, sin):
        du = grad * cos - pltpu.roll(grad, 64, 1) * sin
        return norm_back(raw, gain, du)

    for r in range(ratio):
        span = slice(r * 128, r * 128 + 128)
        qh, dah = q_ref[:, span], dattn[:, span]
        lse = lse_ref[pl.ds(kv * ratio + r, 1), :]
        scores = dot_nt(k_ref[...], qh) * (scale * log2e) + bias
        probs = jnp.exp2(scores - lse)
        dprobs = dot_nt(v_ref[...], dah)
        delta = jnp.sum(probs * dprobs, axis=0, keepdims=True)
        ds = (probs * (dprobs - delta)).astype(BF)
        dv_sum[...] += dot(probs.astype(BF), dah)
        dk_sum[...] += dot(ds, qh)
        dqr = dot(kt_ref[...], ds).T * scale
        back, dg = prep_back(dqr, qraw_ref[:, span], gq_ref[...], cq_ref[...], sq_ref[...])
        dq_ref[:, span] = back.astype(BF)
        dgq_ref[0:1] += dg

    wo_sum[...] += dot_tn(attn_ref[...], dz_ref[...])

    @pl.when(block == pl.num_programs(1) - 1)
    def _():
        both[kv] = wo_sum[...].astype(BF).reshape(both.shape[1:])
        move(kv).start()
        dv_ref[...] = dv_sum[...].astype(BF)
        back, dg = prep_back(
            dk_sum[...] * scale, kraw_ref[...], gk_ref[...], ck_ref[...], sk_ref[...]
        )
        dk_ref[...] = back.astype(BF)
        dgk_ref[0:1] += dg

    @pl.when(step == steps - 1)
    def _():
        cw = grads.shape[2]
        writes = []
        for number in range(kheads):
            move(number).wait_recv()
            value = both[number, :, core].astype(F32) + got[number].astype(F32)
            done[number] = value.astype(BF).reshape(done.shape[1:])
            for i in range(done.shape[2] // cw):
                rows = pl.ds(number * pieces * depth, pieces * depth)
                writes.append(
                    pltpu.make_async_copy(
                        done.at[number, :, pl.ds(i * cw, cw)],
                        grads.at[n + i, rows],
                        put.at[number, i],
                    )
                )
        for copy in writes:
            copy.start()
        lower()
        upper()
        for copy in writes:
            copy.wait()
        for number in range(kheads):
            move(number).wait_send()


def gradient(n, counts, kept, flipped, beside, *refs):
    a_ref, bs = refs[0], refs[1 : 1 + len(counts)]
    refs = refs[1 + len(counts) + kept :]
    if beside:
        given, out_ref, taken, both, got, send, recv, esend, erecv, local = refs[:10]
        refs = refs[10:]
    else:
        out_ref, both, got, send, recv = refs[:5]
        refs = refs[5:]
    turned = a_ref if flipped else refs[0]
    step = pl.program_id(0)
    tiles = sum(counts)
    core = lax.rem(lax.axis_index("fsdp"), 2)
    twin = lax.axis_index("fsdp") + 1 - 2 * core
    blocks, depth, tile = both.shape[1], both.shape[3], both.shape[4]
    piece = min(1024, turned.shape[0])
    part = piece // (2 * depth)

    def move(number):
        slot = lax.rem(number, 2)
        return remote(
            both.at[slot, :, 1 - core], got.at[number], send.at[number], recv.at[number], "fsdp", twin
        )

    @pl.when(step == 0)
    def _():
        greet([("fsdp", twin)] + (others("seq", n) if beside else []))
        if beside:
            for copy in exchange_copies(n, [given], [taken], esend, erecv, local):
                copy.start()
        if not flipped:
            turned[...] = a_ref[...].T

    begin = 0
    for b_ref, count in zip(bs, counts):

        @pl.when((step >= begin) & (step < begin + count))
        def _(b_ref=b_ref):
            slot = lax.rem(step, 2)

            @pl.when(step >= 2)
            def _():
                move(step - 2).wait_send()

            for i in range(turned.shape[0] // piece):
                rows = dot(turned[i * piece : i * piece + piece, :], b_ref[...]).astype(BF)
                both[slot, i * part : i * part + part] = rows.reshape(part, 2, depth, tile)
            move(step).start()

        begin += count

    @pl.when(step >= 1)
    def _():
        last = step - 1
        move(last).wait_recv()
        lead = out_ref.shape[0]
        inner = blocks // lead
        for i in range(lead):
            own = both[lax.rem(last, 2), i * inner : i * inner + inner, core]
            other = got[last, i * inner : i * inner + inner]
            total = (own.astype(F32) + other.astype(F32)).astype(BF)
            out_ref[i] = total.reshape(inner * depth, tile)

    @pl.when(step == tiles)
    def _():
        if tiles >= 2:
            move(tiles - 2).wait_send()
        move(tiles - 1).wait_send()
        if beside:
            for copy in exchange_copies(n, [given], [taken], esend, erecv, local):
                copy.wait()


def exchange_copies(n, ins, outs, send, recv, local):
    me = lax.axis_index("seq")
    copies = []
    for i, (source, out) in enumerate(zip(ins, outs)):
        for j in range(1, n):
            to = lax.rem(me + j, n)
            k = i * (n - 1) + j - 1
            copies.append(
                remote(source.at[to], out.at[me], send.at[k], recv.at[k], "seq", to)
            )
        copies.append(pltpu.make_async_copy(source.at[me], out.at[me], local.at[i]))
    return copies


def exchange(n, source, out, send, recv, local):
    greet(others("seq", n))
    copies = exchange_copies(n, [source], [out], send, recv, local)
    for copy in copies:
        copy.start()
    for copy in copies:
        copy.wait()


def write_out(nf, own_gain, own_head, y, dx, gains, att, o, gu, dn, out, dx_out, g_one, q_out, k_out, v_out, g_q, g_k, o_out, g_two, gate_out, up_out, down_out):
    out[...] = y[...]
    dx_out[...] = dx[...]
    qw, kw = q_out.shape[1], k_out.shape[1]
    q_out[...] = att[0, :, :qw].astype(F32)
    k_out[...] = att[0, :, qw : qw + kw].astype(F32)
    v_out[...] = att[0, :, qw + kw :].astype(F32)
    o_out[...] = o[0].astype(F32)
    units = gate_out.shape[1]
    gate_out[...] = gu[0, :, :units].astype(F32)
    up_out[...] = gu[0, :, units:].astype(F32)
    down_out[...] = dn[0].astype(F32)

    @pl.when(pl.program_id(0) == 0)
    def _():
        spot = lax.axis_index("fsdp")
        owner = lax.axis_index("seq") * nf + spot
        begin = lax.rem(spot, 128 // own_gain) * own_gain
        wide = pltpu.roll(gains[...], lax.rem(128 - begin, 128), 1)
        g_one[...] = wide[0:1, :own_gain]
        g_two[...] = wide[1:2, :own_gain]
        heads = pltpu.roll(gains[...], lax.rem(128 - owner * own_head, 128), 1)
        g_q[...] = heads[2:3, :own_head]
        g_k[...] = heads[3:4, :own_head]


def last_stage(n, nf, dq, dk, dv, w, x, dx2, gain, gu, two, gq, gk, out, gu_out, gains, part, slots, stage, send, recv, row, small, wide, mid, seen, esend, erecv, local, gsend, grecv):
    me, spot = lax.axis_index("seq"), lax.axis_index("fsdp")
    greet(others("seq", n) + others("fsdp", nf))
    row[...] = jnp.zeros_like(row)
    rows, width = x.shape
    qw, kw = dq.shape[1], dk.shape[1]
    step = 512

    def block(to):
        at = pl.ds(pl.multiple_of(to * rows, rows), rows)

        def columns(number, carry):
            span = pl.ds(pl.multiple_of(number * step, step), step)
            value = dot_nt(dq[at, :], w[span, pl.ds(0, qw)])
            value += dot_nt(dk[at, :], w[span, pl.ds(qw, kw)])
            value += dot_nt(dv[at, :], w[span, pl.ds(qw + kw, kw)])
            part[to, :, span] = value.astype(BF)
            return carry

        lax.fori_loop(0, width // step, columns, 0)

    def finish(at, total):
        back, dg = norm_back(x[at].astype(F32), gain[...], total)
        out[at] = (dx2[at] + back).astype(BF)
        row[...] += dg

    start, relay, lower, upper = scatter_parts(n, part, slots, stage, send, recv, finish)
    exchanges = exchange_copies(n, [gu], [gu_out], esend, erecv, local)
    if n == 4:
        across, along, corner = square(me)
        block(corner)
        start(0, 1)
        block(across)
        block(along)
        start(3)
        relay()
        for copy in exchanges:
            copy.start()
        block(me)
    else:
        for j in range(n):
            block(lax.rem(me + j, n))
        start()
        for copy in exchanges:
            copy.start()
    lower()
    upper()
    small[...] = jnp.zeros_like(small)
    per = 128 * n * nf // width
    one = row[...]
    for f in range(nf):
        for seq in range(n):
            line = (seq * nf + f) // per
            small[f, seq, 0:1] = one[:, line * 128 : line * 128 + 128]
            small[f, seq, 1:2] = two[line : line + 1]
            small[f, seq, 2:3] = gq[0:1]
            small[f, seq, 3:4] = gk[0:1]
    far = []
    for j in range(1, nf):
        to = lax.rem(spot + j, nf)
        far.append(
            remote(small.at[to], wide.at[j - 1], gsend.at[j - 1], grecv.at[j - 1], "fsdp", to)
        )
    for copy in far:
        copy.start()
    for copy in far:
        copy.wait_recv()
    total = small[spot]
    for j in range(nf - 1):
        total += wide[j]
    mid[...] = total
    near = []
    for j in range(1, n):
        to = lax.rem(me + j, n)
        k = nf + j - 2
        near.append(remote(mid.at[to], seen.at[j - 1], gsend.at[k], grecv.at[k], "seq", to))
    for copy in near:
        copy.start()
    for copy in near:
        copy.wait_recv()
    result = mid[me]
    for j in range(n - 1):
        result += seen[j]
    gains[...] = result
    for copy in far + near:
        copy.wait_send()
    for copy in exchanges:
        copy.wait()


def after(value, done):
    return lax.optimization_barrier((value, done))[0]


def dma(count):
    return pltpu.SemaphoreType.DMA((count,))


def shards(
    n,
    nf,
    tokens,
    seq_lengths,
    pic_starts,
    pic_lengths,
    norm1_gain,
    w_query,
    w_key,
    w_value,
    q_gain,
    k_gain,
    w_out,
    norm2_gain,
    w_gate,
    w_up,
    w_down,
    cotangent,
):
    rows, width = tokens.shape
    group = rows * n
    depth = w_query.shape[0]
    head = q_gain.shape[0] * n * nf
    qw, kw = w_query.shape[1] // n, w_key.shape[1] // n
    cw = qw + 2 * kw
    fw = w_gate.shape[1] // n
    qheads, kheads = qw // head, kw // head
    ratio = qheads // kheads
    own_gain = norm1_gain.shape[0]
    own_head = q_gain.shape[0]

    entries = []
    for gain in (norm1_gain, norm2_gain, q_gain, k_gain):
        entries += [gain, jnp.zeros((128 - gain.shape[0],), BF)]
    packed = jnp.concatenate(entries).astype(F32)[None, :]

    gather_sems = [dma(gather_copies(n)), dma(gather_copies(n)), pltpu.SemaphoreType.DMA]
    line = nf == 8
    half = head // 2
    powers = -(np.arange(half, dtype=np.float32) * np.float32(2.0) / np.float32(head))
    freq = np.tile((np.float32(theta) ** powers).astype(np.float32), 2)[None, :]
    small = pl.BlockSpec(memory_space=pltpu.SMEM)
    held = nf if line else 1
    w_att, gu, xg, wo, gain_one, gain_two, gain_q, gain_k, cos, sin, low, high = pl.pallas_call(
        functools.partial(entry_stage, n, nf, line, own_gain, own_head),
        out_shape=(
            shape((n, held, depth, cw), BF),
            shape((n, depth, 2 * fw), BF),
            shape((n, rows, width), BF),
            shape((held, depth, width), BF),
            shape((1, width), F32),
            shape((1, width), F32),
            shape((1, head), F32),
            shape((1, head), F32),
            shape((group, head), F32),
            shape((group, head), F32),
            shape((8, group), jnp.int32),
            shape((8, group), jnp.int32),
        ),
        in_specs=[ANY] * 7 + [VMEM] + [small] * 3 + [VMEM],
        out_specs=(ANY,) * 4 + (VMEM,) * 8,
        scratch_shapes=[
            pltpu.VMEM((8, 128), F32),
            pltpu.VMEM((n, 8, 128), F32),
            pltpu.VMEM((nf, n, 8, 128), F32),
            dma(3 * (n - 1)),
            dma(3 * (n - 1)),
            dma(3),
            dma(2 * (n - 1)),
            dma(2 * (n - 1)),
            dma(2),
        ]
        + gather_sems
        + [
            dma(n + nf - 2),
            dma(n + nf - 2),
            dma(2),
            dma(10),
            dma(10),
            dma(10),
            dma(10),
            pltpu.SemaphoreType.DMA,
        ],
        compiler_params=comm_params(0),
    )(
        w_query, w_key, w_value, w_gate, w_up, tokens, w_out, packed,
        seq_lengths, pic_starts, pic_lengths, jnp.asarray(freq),
    )
    wo = wo.reshape(-1, width)
    w_att = w_att.reshape(n, -1, cw)
    if not line:
        wo = lax.all_gather(wo, "fsdp", axis=0, tiled=True)
        w_att = lax.all_gather(w_att, "fsdp", axis=1, tiled=True)
    w_att = w_att.reshape(width, cw)
    gu = lax.all_gather(gu, "fsdp", axis=1, tiled=True).reshape(width, 2 * fw)

    def whole(dims):
        return pl.BlockSpec(dims, lambda *ids: (0,) * len(dims))

    def by_rows(count, columns):
        return pl.BlockSpec((count, columns), lambda i: (i, 0))

    def by_cols(count, columns):
        return pl.BlockSpec((count, columns), lambda i: (0, i))

    blocks = group // 256
    n1, qraw, kraw, q, k, v, kt, vt, cg = pl.pallas_call(
        functools.partial(project, n),
        grid=(blocks,),
        out_shape=(
            shape((width, group), BF),
            shape((group, qw), F32),
            shape((group, kw), F32),
            shape((group, qw), BF),
            shape((group, kw), BF),
            shape((group, kw), BF),
            shape((kw, group), BF),
            shape((kw, group), BF),
            shape((n, rows, width), BF),
        ),
        in_specs=[
            by_rows(256, width),
            whole((1, width)),
            whole((width, cw)),
            whole((1, head)),
            whole((1, head)),
            by_rows(256, head),
            by_rows(256, head),
            ANY,
        ],
        out_specs=(
            by_cols(width, 256),
            by_rows(256, qw),
            by_rows(256, kw),
            by_rows(256, qw),
            by_rows(256, kw),
            by_rows(256, kw),
            by_cols(kw, 256),
            by_cols(kw, 256),
            ANY,
        ),
        scratch_shapes=gather_sems,
        compiler_params=comm_params(11),
    )(xg.reshape(group, width), gain_one, w_att, gain_q, gain_k, cos, sin, cotangent)

    attn, lse, part_out, cg, dn = pl.pallas_call(
        functools.partial(attend, n),
        grid=(blocks,),
        out_shape=(
            shape((group, qw), BF),
            shape((8, group), F32),
            shape((group, width), BF),
            shape((n, rows, width), BF),
            shape((n, depth, fw), BF),
        ),
        in_specs=[
            by_rows(256, qw),
            whole((group, kw)),
            whole((kw, group)),
            whole((qw, width)),
            by_cols(8, 256),
            by_cols(8, 256),
            ANY,
            ANY,
            ANY,
        ],
        out_specs=(by_rows(256, qw), by_cols(8, 256), by_rows(256, width), ANY, ANY),
        scratch_shapes=[pltpu.VMEM((group, 256), F32)]
        + gather_sems
        + [dma(n - 1), dma(n - 1), dma(1)],
        input_output_aliases={7: 3},
        compiler_params=comm_params(3),
    )(q, k, vt, wo, low, high, cotangent, cg, w_down.T)
    cg = cg.reshape(group, width)
    dn = lax.all_gather(dn, "fsdp", axis=1, tiled=True).reshape(width, fw)

    slots = [
        pltpu.VMEM((scatter_slots(n), rows, width), BF),
        pltpu.VMEM((rows, width), BF),
    ]
    sems = [dma(max(6, n - 1)), dma(max(6, n - 1))]

    x2, n2 = pl.pallas_call(
        functools.partial(middle_stage, n),
        out_shape=(shape((rows, width), F32), shape((n, rows, width), BF)),
        in_specs=[VMEM] * 3,
        out_specs=(VMEM, ANY),
        scratch_shapes=slots + [pltpu.VMEM((rows, width), BF)] + sems + gather_sems,
        compiler_params=comm_params(2),
    )(part_out.reshape(n, rows, width), tokens, gain_two)
    n2 = n2.reshape(group, width)

    tile = 256
    tiles = fw // tile
    cuts = 1
    while 2 * cuts <= tiles:
        cuts *= 2
    gate, up, hidden, n2_turned = pl.pallas_call(
        functools.partial(ffn_forward, cuts),
        grid=(tiles,),
        out_shape=(
            shape((group, fw), F32),
            shape((group, fw), F32),
            shape((group, fw), BF),
            shape((width, group), BF),
        ),
        in_specs=[
            whole((group, width)),
            by_cols(width, tile),
            pl.BlockSpec((width, tile), lambda i: (0, i + tiles)),
        ],
        out_specs=(by_cols(group, tile),) * 3
        + (pl.BlockSpec((width // cuts, group), lambda i: (jnp.minimum(i, cuts - 1), 0)),),
        compiler_params=plain_params(),
    )(n2, gu, gu)

    def product(number, a, *bs, into=None, flipped=False, given=None):
        tile = 512
        while any(b.shape[1] % tile for b in bs):
            tile //= 2
        counts = [b.shape[1] // tile for b in bs]
        begins = [sum(counts[:i]) for i in range(len(bs))]
        tiles = sum(counts)

        def spec(begin, count):
            return pl.BlockSpec(
                (group, tile), lambda i: (0, jnp.clip(i - begin, 0, count - 1))
            )

        dims = (n, width // n // 2, tiles * tile) if into is None else into.shape
        kept = [] if into is None else [into]
        side = [] if given is None else [given]
        blocks = width // (2 * depth)
        outs = [pl.BlockSpec((n, dims[1], tile), lambda i: (0, 0, jnp.maximum(i - 1, 0)))]
        extra = [dma(n - 1), dma(n - 1), dma(1)] if side else []
        result = pl.pallas_call(
            functools.partial(gradient, n, counts, len(kept), flipped, len(side)),
            grid=(tiles + 1,),
            out_shape=(shape(dims, BF),) + tuple(shape(g.shape, BF) for g in side),
            in_specs=[whole(a.shape)]
            + [spec(b, c) for b, c in zip(begins, counts)]
            + [ANY] * len(kept + side),
            out_specs=tuple(outs + [ANY] * len(side)),
            scratch_shapes=[
                pltpu.VMEM((2, blocks, 2, depth, tile), BF),
                pltpu.VMEM((tiles, blocks, depth, tile), BF),
                dma(tiles),
                dma(tiles),
            ]
            + extra
            + ([] if flipped else [pltpu.VMEM((width, group), BF)]),
            input_output_aliases={} if into is None else {1 + len(bs): 0},
            compiler_params=comm_params(number),
        )(a, *bs, *kept, *side)
        return result if side else result[0]

    same_core = [[core + 2 * i for i in range(nf // 2)] for core in range(2)]

    def reduce_rows(grad):
        return lax.psum_scatter(
            grad, "fsdp", scatter_dimension=1, tiled=True, axis_index_groups=same_core
        )

    dn_grad = product(12, cg, hidden)
    dn_share = reduce_rows(dn_grad)

    dgate, dup = pl.pallas_call(
        ffn_back,
        grid=(tiles,),
        out_shape=(shape((group, fw), BF), shape((group, fw), BF)),
        in_specs=[
            whole((group, width)),
            by_cols(width, tile),
            by_cols(group, tile),
            by_cols(group, tile),
        ],
        out_specs=(by_cols(group, tile),) * 2,
        compiler_params=plain_params(),
    )(cg, after(dn, dn_grad), gate, up)

    gu_grad = product(13, n2_turned, dgate, dup, flipped=True)
    gu_share = reduce_rows(gu_grad)

    dx2, dz, dgain_two, part_y = pl.pallas_call(
        functools.partial(back_stage, n),
        out_shape=(
            shape((rows, width), F32),
            shape((n, rows, width), BF),
            shape((width // 128, 128), F32),
            shape((n, rows, width), BF),
        ),
        in_specs=[ANY] * 3 + [VMEM] * 3 + [ANY] * 2,
        out_specs=(VMEM, ANY, VMEM, VMEM),
        scratch_shapes=[pltpu.VMEM((n, rows, width), BF)]
        + slots
        + [pltpu.VMEM((rows, width), BF)]
        + sems
        + gather_sems
        + [
            pltpu.VMEM((1, width), F32),
            pltpu.VMEM((group, fw), BF),
            pltpu.VMEM((width, fw), BF),
            dma(2),
            pltpu.VMEM((group, fw), BF),
            pltpu.VMEM((group, fw), BF),
            pltpu.VMEM((width, 2 * fw), BF),
            pltpu.SemaphoreType.DMA((2, n)),
            dma(width // 512),
        ],
        compiler_params=comm_params(4),
    )(
        after(dgate, gu_grad), dup, gu, x2, cotangent, gain_two, hidden, dn,
    )
    dz = dz.reshape(group, width)

    wide = ratio * head
    dq, dk, dv, dgain_q, dgain_k, branch, wo_grad = pl.pallas_call(
        functools.partial(attend_back, n),
        grid=(kheads, blocks),
        out_shape=(
            shape((group, qw), BF),
            shape((group, kw), BF),
            shape((group, kw), BF),
            shape((8, head), F32),
            shape((8, head), F32),
            shape((rows, width), BF),
            shape((n + width // cw, width // n // 2, cw), BF),
        ),
        in_specs=[
            pl.BlockSpec((256, wide), lambda h, b: (b, h)),
            pl.BlockSpec((256, wide), lambda h, b: (b, h)),
            pl.BlockSpec((group, head), lambda h, b: (0, h)),
            pl.BlockSpec((head, group), lambda h, b: (h, 0)),
            pl.BlockSpec((group, head), lambda h, b: (0, h)),
            pl.BlockSpec((group, head), lambda h, b: (0, h)),
            pl.BlockSpec((256, width), lambda h, b: (b, 0)),
            pl.BlockSpec((wide, width), lambda h, b: (h, 0)),
            pl.BlockSpec((8, 256), lambda h, b: (0, b)),
            pl.BlockSpec((8, 256), lambda h, b: (0, b)),
            pl.BlockSpec((8, 256), lambda h, b: (0, b)),
            pl.BlockSpec((256, head), lambda h, b: (b, 0)),
            pl.BlockSpec((256, head), lambda h, b: (b, 0)),
            whole((group, head)),
            whole((group, head)),
            whole((1, head)),
            whole((1, head)),
            pl.BlockSpec((256, wide), lambda h, b: (b, h)),
            VMEM,
            VMEM,
        ],
        out_specs=(
            pl.BlockSpec((256, wide), lambda h, b: (b, h)),
            pl.BlockSpec((group, head), lambda h, b: (0, h)),
            pl.BlockSpec((group, head), lambda h, b: (0, h)),
            whole((8, head)),
            whole((8, head)),
            VMEM,
            ANY,
        ),
        scratch_shapes=[pltpu.VMEM((group, head), F32), pltpu.VMEM((group, head), F32)]
        + slots
        + sems
        + [
            pltpu.VMEM((wide, width), F32),
            pltpu.VMEM((kheads, wide // (2 * depth), 2, depth, width), BF),
            pltpu.VMEM((kheads, wide // (2 * depth), depth, width), BF),
            pltpu.VMEM((kheads, wide // 2, width), BF),
            dma(kheads),
            dma(kheads),
            pltpu.SemaphoreType.DMA((kheads, width // cw)),
        ],
        compiler_params=comm_params(5),
    )(
        q, qraw, k, kt, v, kraw, dz, wo, lse, low, high, cos, sin, cos, sin, gain_q, gain_k,
        attn, part_y, x2,
    )

    att_grad, dn_mine = product(
        15, n1, dq, dk, dv, into=wo_grad, flipped=True, given=dn_share
    )
    att_share = reduce_rows(after(att_grad, gu_share))

    input_raw, gu_mine, gains = pl.pallas_call(
        functools.partial(last_stage, n, nf),
        out_shape=(
            shape((rows, width), BF),
            shape(gu_share.shape, BF),
            shape((8, 128), F32),
        ),
        in_specs=[VMEM] * 7 + [ANY] + [VMEM] * 3,
        out_specs=(VMEM, ANY, VMEM),
        scratch_shapes=[pltpu.VMEM((n, rows, width), BF)]
        + slots
        + sems
        + [
            pltpu.VMEM((1, width), F32),
            pltpu.VMEM((nf, n, 8, 128), F32),
            pltpu.VMEM((nf - 1, n, 8, 128), F32),
            pltpu.VMEM((n, 8, 128), F32),
            pltpu.VMEM((n - 1, 8, 128), F32),
            dma(n - 1),
            dma(n - 1),
            dma(1),
            dma(n + nf - 2),
            dma(n + nf - 2),
        ],
        compiler_params=comm_params(7),
    )(
        after(dq, att_grad), dk, dv, w_att, tokens, dx2, gain_one, gu_share,
        dgain_two, dgain_q, dgain_k,
    )
    att_mine = pl.pallas_call(
        functools.partial(exchange, n),
        out_shape=shape((n, depth, cw), BF),
        in_specs=[ANY],
        out_specs=ANY,
        scratch_shapes=[dma(n - 1), dma(n - 1), dma(1)],
        compiler_params=comm_params(9),
    )(after(att_share, gains))

    def slab(count):
        return pl.BlockSpec((1, depth, count), lambda i: (i, 0, 0))

    each = width // n
    per = cw // each
    results = pl.pallas_call(
        functools.partial(write_out, nf, own_gain, own_head),
        grid=(n,),
        out_shape=(
            shape((rows, width), BF),
            shape((rows, width), BF),
            shape((1, own_gain), F32),
            shape(w_query.shape, F32),
            shape(w_key.shape, F32),
            shape(w_value.shape, F32),
            shape((1, own_head), F32),
            shape((1, own_head), F32),
            shape(w_out.shape, F32),
            shape((1, own_gain), F32),
            shape(w_gate.shape, F32),
            shape(w_up.shape, F32),
            shape(w_gate.shape, F32),
        ),
        in_specs=[
            by_rows(rows // n, width),
            by_rows(rows // n, width),
            whole((8, 128)),
            slab(cw),
            pl.BlockSpec(
                (1, depth, each), lambda i: (n + lax.div(i, per), 0, lax.rem(i, per))
            ),
            slab(2 * fw),
            slab(fw),
        ],
        out_specs=(
            by_rows(rows // n, width),
            by_rows(rows // n, width),
            whole((1, own_gain)),
            by_cols(depth, qw),
            by_cols(depth, kw),
            by_cols(depth, kw),
            whole((1, own_head)),
            whole((1, own_head)),
            by_cols(depth, each),
            whole((1, own_gain)),
            by_cols(depth, fw),
            by_cols(depth, fw),
            by_cols(depth, fw),
        ),
        compiler_params=plain_params(),
    )(branch, input_raw, gains, att_mine, att_share, gu_mine, dn_mine)
    flat = [r.reshape(-1) if i in (2, 6, 7, 9) else r for i, r in enumerate(results)]
    return tuple(flat[:-1]) + (flat[-1].T,)


def solution(mesh):
    return jax.shard_map(
        functools.partial(shards, mesh.shape["seq"], mesh.shape["fsdp"]),
        mesh=mesh,
        in_specs=(
            P(("fsdp", "seq"), None),
            P("fsdp", None),
            P("fsdp", None),
            P("fsdp", None),
            P(("seq", "fsdp")),
            P(("seq", "fsdp"), None),
            P(("seq", "fsdp"), None),
            P(("seq", "fsdp"), None),
            P(("seq", "fsdp")),
            P(("seq", "fsdp")),
            P(("seq", "fsdp"), None),
            P(("seq", "fsdp")),
            P(("seq", "fsdp"), None),
            P(("seq", "fsdp"), None),
            P(None, ("seq", "fsdp")),
            P(("fsdp", "seq"), None),
        ),
        out_specs=(
            P(("fsdp", "seq"), None),
            P(("fsdp", "seq"), None),
            P(("seq", "fsdp")),
            P(("seq", "fsdp"), None),
            P(("seq", "fsdp"), None),
            P(("seq", "fsdp"), None),
            P(("seq", "fsdp")),
            P(("seq", "fsdp")),
            P(("seq", "fsdp"), None),
            P(("seq", "fsdp")),
            P(("seq", "fsdp"), None),
            P(("seq", "fsdp"), None),
            P(None, ("seq", "fsdp")),
        ),
        check_vma=False,
    )
```

```python
import functools

import jax
import jax.numpy as jnp
import numpy as np
from jax import lax
from jax.experimental import pallas as pl
from jax.experimental.pallas import tpu as pltpu
from jax.sharding import PartitionSpec as P

epsilon = 1e-06
theta = 1000000.0
masked_score = -1e30
log2e = 1.4426950408889634

MESH = pl.DeviceIdType.MESH
ANY = pl.BlockSpec(memory_space=pl.ANY)
VMEM = pl.BlockSpec(memory_space=pltpu.VMEM)
BF = jnp.bfloat16
F32 = jnp.float32
LIMIT = 60 * 1024 * 1024


def dot(a, b):
    return jnp.dot(a, b, preferred_element_type=F32)


def dot_nt(a, b):
    return lax.dot_general(a, b, (((1,), (1,)), ((), ())), preferred_element_type=F32)


def dot_tn(a, b):
    return lax.dot_general(a, b, (((0,), (0,)), ((), ())), preferred_element_type=F32)


def shape(dims, dtype):
    return jax.ShapeDtypeStruct(dims, dtype)


def comm_params(number):
    return pltpu.CompilerParams(
        collective_id=number, has_side_effects=True, vmem_limit_bytes=LIMIT
    )


def plain_params():
    return pltpu.CompilerParams(vmem_limit_bytes=LIMIT)


def remote(src, dst, send, recv, axis, index):
    return pltpu.make_async_remote_copy(
        src_ref=src,
        dst_ref=dst,
        send_sem=send,
        recv_sem=recv,
        device_id={axis: index},
        device_id_type=MESH,
    )


def greet(places):
    barrier = pltpu.get_barrier_semaphore()
    for axis, index in places:
        pl.semaphore_signal(barrier, inc=1, device_id={axis: index}, device_id_type=MESH)
    pl.semaphore_wait(barrier, len(places))


def others(axis, n):
    me = lax.axis_index(axis)
    return [(axis, lax.rem(me + j, n)) for j in range(1, n)]


def square(me):
    return me + 1 - 2 * lax.rem(me, 2), lax.rem(me + 2, 4), 3 - me


def ring_places(n):
    me = lax.axis_index("seq")
    if n == 4:
        across, along, _ = square(me)
        return [("seq", across), ("seq", along)]
    return others("seq", n)


def gather_copies(n):
    return 6 if n == 4 else n - 1


def gather_parts(n, own, out, send, recv, local):
    me = lax.axis_index("seq")
    keep = pltpu.make_async_copy(own, out.at[me], local)
    half = own.shape[0] // 2
    low, high = pl.ds(0, half), pl.ds(half, half)
    if n == 4:
        across, along, _ = square(me)
        moves = [
            (own.at[low], out.at[me, low], across),
            (own.at[high], out.at[me, high], along),
            (own.at[high], out.at[me, high], across),
            (own.at[low], out.at[me, low], along),
            (out.at[across, low], out.at[across, low], along),
            (out.at[along, high], out.at[along, high], across),
        ]
    else:
        moves = [(own, out.at[me], lax.rem(me + j, n)) for j in range(1, n)]
    copies = [
        remote(src, dst, send.at[i], recv.at[i], "seq", to)
        for i, (src, dst, to) in enumerate(moves)
    ]

    def start(part=None):
        chosen = range(len(copies))
        if n == 4:
            chosen = {None: (0, 1, 2, 3), 0: (0, 3), 1: (1, 2)}[part]
        if n == 4 or part != 0:
            for i in chosen:
                copies[i].start()
        if part != 0:
            keep.start()

    def relay():
        if n == 4:
            copies[0].wait_recv()
            copies[4].start()
            copies[1].wait_recv()
            copies[5].start()

    def finish():
        for copy in copies[2:] if n == 4 else copies:
            copy.wait_recv()
        for copy in copies:
            copy.wait_send()
        keep.wait()

    return start, relay, finish


def scatter_slots(n):
    return 4 if n == 4 else n - 1


def scatter_parts(n, part, slots, stage, send, recv, finish, held=False):
    me = lax.axis_index("seq")
    rows = part.shape[1]
    half = rows // 2
    low, high = pl.ds(0, half), pl.ds(half, half)
    if n == 4:
        across, along, corner = square(me)
        moves = [
            (part.at[corner, low], slots.at[2, low], along),
            (part.at[corner, high], slots.at[2, high], across),
            (part.at[across, high], slots.at[0, high], across),
            (part.at[along, low], slots.at[1, low], along),
            (stage.at[low], slots.at[0, low], across),
            (stage.at[high], slots.at[1, high], along),
        ]
        count = 2
    else:
        moves = []
        for j in range(1, n):
            to = lax.rem(me + j, n)
            moves.append((part.at[to], slots.at[j - 1], to))
        count = n - 1
    copies = [
        remote(src, dst, send.at[i], recv.at[i], "seq", to)
        for i, (src, dst, to) in enumerate(moves)
    ]

    def start(*chosen):
        chosen = chosen if chosen else (0, 1, 3) if held else (0, 1, 2, 3)
        for copy in [copies[i] for i in chosen] if n == 4 else copies:
            copy.start()

    def relay():
        if n == 4:
            copies[0].wait_recv()
            stage[low] = (part[across, low].astype(F32) + slots[2, low].astype(F32)).astype(BF)
            copies[4].start()
            if held:
                copies[2].start()
            copies[1].wait_recv()
            stage[high] = (part[along, high].astype(F32) + slots[2, high].astype(F32)).astype(BF)
            copies[5].start()

    step = 32

    def chunk(number, carry):
        at = pl.ds(pl.multiple_of(number * step, step), step)
        value = part[me, at].astype(F32)
        for slot in range(count):
            value += slots[slot, at].astype(F32)
        finish(at, value)
        return carry

    def lower():
        for copy in copies[3:5] if n == 4 else copies:
            copy.wait_recv()
        lax.fori_loop(0, half // step, chunk, 0)

    def upper():
        if n == 4:
            copies[2].wait_recv()
            copies[5].wait_recv()
        lax.fori_loop(half // step, rows // step, chunk, 0)
        for copy in copies:
            copy.wait_send()

    return start, relay, lower, upper


def inverse_rms(values):
    return lax.rsqrt(jnp.mean(values * values, axis=-1, keepdims=True) + epsilon)


def norm_back(values, gain, grad):
    inverse = inverse_rms(values)
    scaled = grad * gain
    back = inverse * scaled - values * (
        inverse * inverse * inverse * jnp.mean(scaled * values, axis=-1, keepdims=True)
    )
    return back, jnp.sum(grad * values * inverse, axis=0, keepdims=True)


def start_columns(n, views, send, recv, local, begin=True):
    me = lax.axis_index("seq")
    width = views[0][0].shape[1] // n
    copies, keeps = [], []
    for i, (ref, out, place) in enumerate(views):
        for j in range(1, n):
            to = lax.rem(me + j, n)
            columns = pl.ds(pl.multiple_of(to * width, 128), width)
            k = i * (n - 1) + j - 1
            copies.append(
                remote(
                    ref.at[:, columns],
                    out.at[me, :, pl.ds(place * width, width)],
                    send.at[k],
                    recv.at[k],
                    "seq",
                    to,
                )
            )
        columns = pl.ds(pl.multiple_of(me * width, 128), width)
        keeps.append(
            pltpu.make_async_copy(
                ref.at[:, columns], out.at[me, :, pl.ds(place * width, width)], local.at[i]
            )
        )
    if begin:
        for copy in copies + keeps:
            copy.start()
    return copies + keeps


def line_gather(cell, own, send, recv):
    spot = lax.axis_index("fsdp")
    z = lax.div(spot, 2)
    twin = spot + 1 - 2 * lax.rem(spot, 2)

    def hop(number, block, to):
        source = own if isinstance(block, str) else cell(block)
        target = cell(spot if isinstance(block, str) else block)
        return remote(source, target, send.at[number], recv.at[number], "fsdp", to)

    def up(k):
        return hop(k, "own" if k == 0 else spot - 2 * k, spot + 2)

    def down(k):
        return hop(3 + k, "own" if k == 0 else spot + 2 * k, spot - 2)

    def over(offset):
        return hop(6 + z + offset, "own" if offset == 0 else spot + 2 * offset, twin)

    def from_twin(offset):
        return hop(6 + z + offset, twin + 2 * offset, twin)

    def first():
        @pl.when(z < 3)
        def _():
            up(0).start()

        @pl.when(z > 0)
        def _():
            down(0).start()

        over(0).start()

    def step(k):
        @pl.when(z >= k)
        def _():
            up(k - 1).wait_recv()
            if k < 3:

                @pl.when(z < 3)
                def _():
                    up(k).start()

            over(-k).start()

        @pl.when(z + k <= 3)
        def _():
            down(k - 1).wait_recv()
            if k < 3:

                @pl.when(z > 0)
                def _():
                    down(k).start()

            over(k).start()

    def finish():
        from_twin(0).wait_recv()
        over(0).wait_send()
        for k in range(1, 4):

            @pl.when(z >= k)
            def _():
                from_twin(-k).wait_recv()
                over(-k).wait_send()

            @pl.when(z + k <= 3)
            def _():
                from_twin(k).wait_recv()
                over(k).wait_send()

        for k in range(3):

            @pl.when((z >= k) & (z < 3))
            def _():
                up(k).wait_send()

            @pl.when((z + k <= 3) & (z > 0))
            def _():
                down(k).wait_send()

    return first, step, finish


def entry_stage(n, nf, line, own_gain, own_head, wq, wk, wv, wg, wu, x, w_out, raw, lengths, starts, sizes, freq, w_att, gu, xg, wo, gain_one, gain_two, gain_q, gain_k, cos, sin, low, high, mine, seen, gains, qsend, qrecv, qlocal, wsend, wrecv, wlocal, send, recv, local, gsend, grecv, glocal, asend, arecv, osend, orecv, olocal):
    me, spot = lax.axis_index("seq"), lax.axis_index("fsdp")
    greet(others("seq", n) + others("fsdp", nf))
    place = spot if line else 0
    if line:
        o_first, o_step, o_finish = line_gather(lambda f: wo.at[f], w_out, osend, orecv)
        a_first, a_step, a_finish = line_gather(
            lambda f: w_att.at[:, f], w_att.at[:, spot], asend, arecv
        )
        o_first()
    widths = [wq.shape[1] // n, wk.shape[1] // n, wv.shape[1] // n]
    begins = [0, widths[0], widths[0] + widths[1]]
    near = []
    for j in range(1, n):
        to = lax.rem(me + j, n)
        for i, ref in enumerate((wq, wk, wv)):
            columns = pl.ds(pl.multiple_of(to * widths[i], 128), widths[i])
            near.append(
                remote(
                    ref.at[:, columns],
                    w_att.at[me, place, :, pl.ds(begins[i], widths[i])],
                    qsend.at[3 * j - 3 + i],
                    qrecv.at[3 * j - 3 + i],
                    "seq",
                    to,
                )
            )
    for i, ref in enumerate((wq, wk, wv)):
        columns = pl.ds(pl.multiple_of(me * widths[i], 128), widths[i])
        near.append(
            pltpu.make_async_copy(
                ref.at[:, columns],
                w_att.at[me, place, :, pl.ds(begins[i], widths[i])],
                qlocal.at[i],
            )
        )
    for copy in near:
        copy.start()
    mine[...] = jnp.zeros_like(mine)
    for count, first, index in (
        (own_gain, 0, lax.rem(spot, 128 // own_gain)),
        (own_head, 2, me * nf + spot),
    ):
        for at in range(128 // count):

            @pl.when(index == at)
            def _():
                for i in (first, first + 1):
                    mine[i : i + 1, at * count : at * count + count] = raw[
                        :, i * 128 : i * 128 + count
                    ]

    small = [pltpu.make_async_copy(mine, seen.at[me], glocal.at[0])]
    for j in range(1, n):
        to = lax.rem(me + j, n)
        small.append(remote(mine, seen.at[me], gsend.at[j - 1], grecv.at[j - 1], "seq", to))
    keep = pltpu.make_async_copy(w_out, wo.at[place], olocal)
    for copy in small + [keep]:
        copy.start()
    def rope():
        group = cos.shape[0]
        border_one = lengths[0, 0]
        border_two = border_one + lengths[0, 1]

        def begin_of(places):
            later = jnp.where(places >= border_one, border_one, 0)
            return jnp.where(places >= border_two, border_two, later)

        step = 128
        lane = lax.broadcasted_iota(jnp.int32, (step, 128), 1)

        def turn(number, carry):
            at = pl.ds(pl.multiple_of(number * step, step), step)
            places = lax.broadcasted_iota(jnp.int32, (step, 128), 0) + number * step
            angle = (places - begin_of(places)).astype(F32) * freq[...]
            cos[at, :] = jnp.cos(angle)
            sine = jnp.sin(angle)
            sin[at, :] = jnp.where(lane < 64, -sine, sine)
            return carry

        lax.fori_loop(0, group // step, turn, 0)
        places = lax.broadcasted_iota(jnp.int32, (8, group), 1)
        end = jnp.where(places >= border_one, border_two, border_one)
        end = jnp.where(places >= border_two, group, end)
        picture = jnp.zeros_like(places)
        for i in range(starts.shape[1]):
            first, count = starts[0, i], sizes[0, i]
            inside = (places >= first) & (places < first + count)
            picture = jnp.where(inside, jnp.maximum(picture, first + count), picture)
        low[...] = begin_of(places)
        high[...] = jnp.maximum(places, jnp.minimum(picture, end) - 1)

    rope()
    for copy in near:
        copy.wait()
    if line:
        a_first()
    copies = start_columns(n, [(wg, gu, 0), (wu, gu, 1)], wsend, wrecv, wlocal)
    start, relay, finish = gather_parts(n, x, xg, send, recv, local)
    start()
    if line:
        o_step(1)
    for copy in small:
        copy.wait()
    wide = [pltpu.make_async_copy(seen, gains.at[spot], glocal.at[1])]
    for j in range(1, nf):
        to = lax.rem(spot + j, nf)
        k = n + j - 2
        wide.append(remote(seen, gains.at[spot], gsend.at[k], grecv.at[k], "fsdp", to))
    for copy in wide:
        copy.start()

    def unpack():
        per = 128 // own_gain
        for row in range(n * nf // per):
            seq, first = row * per // nf, row * per % nf
            one = gains[first, seq, 0:1, :]
            two = gains[first, seq, 1:2, :]
            for f in range(first + 1, first + per):
                one += gains[f, seq, 0:1, :]
                two += gains[f, seq, 1:2, :]
            gain_one[:, row * 128 : row * 128 + 128] = one
            gain_two[:, row * 128 : row * 128 + 128] = two
        total = jnp.zeros((8, 128), F32)
        for f in range(nf):
            for seq in range(n):
                total += gains[f, seq]
        gain_q[...] = total[2:3, :]
        gain_k[...] = total[3:4, :]

    if line:
        o_step(2)
        a_step(1)
    relay()
    if line:
        o_step(3)
        a_step(2)
        a_step(3)
        o_finish()
        a_finish()
    finish()
    keep.wait()
    for copy in wide:
        copy.wait()
    unpack()
    for copy in copies:
        copy.wait()


def half_gather(n, begin, cot, cg, send, recv, local, places, beside):
    at = pl.ds(begin, cot.shape[0] // 2)
    start, relay, finish = gather_parts(n, cot.at[at], cg.at[:, at], send, recv, local)
    step, steps = pl.program_id(0), pl.num_programs(0)

    @pl.when(step == 0)
    def _():
        greet(places)
        start()
        beside()

    @pl.when(step == steps - 1)
    def _():
        relay()

    return finish


def project(n, x_ref, gain_ref, w_ref, gq_ref, gk_ref, cos_ref, sin_ref, cot, n1_ref, qraw_ref, kraw_ref, q_ref, k_ref, v_ref, kt_ref, vt_ref, cg, send, recv, local):
    finish_half = half_gather(n, 0, cot, cg, send, recv, local, ring_places(n), lambda: None)
    x = x_ref[...].astype(F32)
    normed = (x * inverse_rms(x) * gain_ref[...]).astype(BF)
    n1_ref[...] = normed.T
    full = dot(normed, w_ref[...])
    qw, kw = q_ref.shape[1], k_ref.shape[1]
    cos, sin = cos_ref[...], sin_ref[...]

    def prep(head, gain):
        u = head * inverse_rms(head) * gain
        return u * cos + pltpu.roll(u, 64, 1) * sin

    qraw_ref[...] = full[:, :qw]
    kraw_ref[...] = full[:, qw : qw + kw]
    v = full[:, qw + kw :]
    v_ref[...] = v.astype(BF)
    vt_ref[...] = v.T.astype(BF)
    for h in range(qw // 128):
        q_ref[:, h * 128 : h * 128 + 128] = prep(
            full[:, h * 128 : h * 128 + 128], gq_ref[...]
        ).astype(BF)
    for h in range(kw // 128):
        turned = prep(full[:, qw + h * 128 : qw + h * 128 + 128], gk_ref[...])
        k_ref[:, h * 128 : h * 128 + 128] = turned.astype(BF)
        kt_ref[h * 128 : h * 128 + 128, :] = turned.T.astype(BF)

    @pl.when(pl.program_id(0) == pl.num_programs(0) - 1)
    def _():
        finish_half()


def bias_of(low_ref, high_ref, keys):
    key = lax.broadcasted_iota(jnp.int32, (keys, low_ref.shape[1]), 0)
    fine = (key >= low_ref[0:1, :]) & (key <= high_ref[0:1, :])
    return jnp.where(fine, 0.0, masked_score)


def attend(n, q_ref, k_ref, vt_ref, wo_ref, low_ref, high_ref, cot, cg_half, wd, attn_ref, lse_ref, part_ref, cg, dn, bias, send, recv, local, wsend, wrecv, wlocal):
    copies = start_columns(n, [(wd, dn, 0)], wsend, wrecv, wlocal, False)

    def beside():
        for copy in copies:
            copy.start()

    finish_half = half_gather(
        n, cot.shape[0] // 2, cot, cg, send, recv, local, others("seq", n), beside
    )
    keys = k_ref.shape[0]
    bias[...] = bias_of(low_ref, high_ref, keys)
    heads = q_ref.shape[1] // 128
    ratio = heads // (k_ref.shape[1] // 128)
    factor = 128 ** (-0.5) * log2e
    for h in range(heads):
        kv = h // ratio
        scores = dot_nt(
            k_ref[:, kv * 128 : kv * 128 + 128], q_ref[:, h * 128 : h * 128 + 128]
        )
        scores = scores * factor + bias[...]
        top = jnp.max(scores, axis=0, keepdims=True)
        probs = jnp.exp2(scores - top)
        total = jnp.sum(probs, axis=0, keepdims=True)
        mixed = dot(vt_ref[kv * 128 : kv * 128 + 128, :], probs.astype(BF))
        lse_ref[h : h + 1, :] = top + jnp.log2(total)
        attn_ref[:, h * 128 : h * 128 + 128] = (mixed / total).T.astype(BF)
    part_ref[...] = dot(attn_ref[...], wo_ref[...]).astype(BF)

    @pl.when(pl.program_id(0) == pl.num_programs(0) - 1)
    def _():
        finish_half()
        for copy in copies:
            copy.wait()


def middle_stage(n, part, x, gain, x2, n2, slots, stage, own, send, recv, asend, arecv, local):
    greet(ring_places(n))

    def finish(at, total):
        value = x[at].astype(F32) + total
        x2[at] = value
        own[at] = (value * inverse_rms(value) * gain[...]).astype(BF)

    start, relay, lower, upper = scatter_parts(n, part, slots, stage, send, recv, finish, True)
    send_on, pass_on, end = gather_parts(n, own, n2, asend, arecv, local)
    start()
    relay()
    lower()
    send_on(0)
    upper()
    send_on(1)
    pass_on()
    end()


def ffn_forward(cuts, n2_ref, wg_ref, wu_ref, gate_ref, up_ref, hidden_ref, turned_ref):
    count = n2_ref.shape[1] // cuts
    step = pl.program_id(0)

    @pl.when(step < cuts)
    def _():
        turned_ref[...] = n2_ref[:, pl.ds(pl.multiple_of(step * count, 128), count)].T

    gate = dot(n2_ref[...], wg_ref[...])
    up = dot(n2_ref[...], wu_ref[...])
    s = jax.nn.sigmoid(gate)
    silu = gate * s
    gate_ref[...] = up * (s * (1.0 + gate * (1.0 - s)))
    up_ref[...] = silu
    hidden_ref[...] = (silu * up).astype(BF)


def ffn_back(cot_ref, wd_ref, gate_ref, up_ref, dgate_ref, dup_ref):
    dh = dot(cot_ref[...], wd_ref[...])
    dgate_ref[...] = (dh * gate_ref[...]).astype(BF)
    dup_ref[...] = (dh * up_ref[...]).astype(BF)


def spread_rows(row, out):
    for i in range(out.shape[0]):
        out[i : i + 1, :] = row[:, i * 128 : i * 128 + 128]


def back_stage(n, dgate_far, dup_far, gu_far, x2, cot, gain, hidden_far, dn_far, dx2, dz, dgain, part_y, part, slots, stage, own, send, recv, asend, arecv, local, row, hidden, dn, load, dgate, dup, gu, rload, wload):
    greet(ring_places(n))
    me = lax.axis_index("seq")
    rows, width = x2.shape
    units = dup.shape[1]
    step = 512

    def row_loads(to):
        at = pl.ds(pl.multiple_of(to * rows, rows), rows)
        return [
            pltpu.make_async_copy(dgate_far.at[at], dgate.at[at], rload.at[0, to]),
            pltpu.make_async_copy(dup_far.at[at], dup.at[at], rload.at[1, to]),
        ]

    def weight_load(number):
        at = pl.ds(pl.multiple_of(number * step, step), step)
        return pltpu.make_async_copy(gu_far.at[at], gu.at[at], wload.at[number])

    order = [lax.rem(me + j, n) for j in range(1, n)] + [me]
    if n == 4:
        across, along, corner = square(me)
        order = [corner, across, along, me]
    for copy in row_loads(order[0]):
        copy.start()
    for number in range(width // step):
        weight_load(number).start()
    for copy in row_loads(order[1]):
        copy.start()
    loads = [
        pltpu.make_async_copy(hidden_far, hidden, load.at[0]),
        pltpu.make_async_copy(dn_far, dn, load.at[1]),
    ]

    def others_loads():
        for to in order[2:]:
            for copy in row_loads(to):
                copy.start()
        for copy in loads:
            copy.start()

    row[...] = jnp.zeros_like(row)

    def block(to, first=False):
        at = pl.ds(pl.multiple_of(to * rows, rows), rows)
        for copy in row_loads(to):
            copy.wait()

        def columns(number, carry):
            if first:
                weight_load(number).wait()
            span = pl.ds(pl.multiple_of(number * step, step), step)
            value = dot_nt(dgate[at, :], gu[span, pl.ds(0, units)])
            value += dot_nt(dup[at, :], gu[span, pl.ds(units, units)])
            part[to, :, span] = value.astype(BF)
            return carry

        lax.fori_loop(0, width // step, columns, 0)

    def forward(to, carry):
        at = pl.ds(pl.multiple_of(to * rows, rows), rows)

        def columns(number, carry):
            span = pl.ds(pl.multiple_of(number * step, step), step)
            part_y[to, :, span] = dot_nt(hidden[at, :], dn[span, :]).astype(BF)
            return carry

        return lax.fori_loop(0, width // step, columns, carry)

    def finish(at, total):
        back, dg = norm_back(x2[at], gain[...], total)
        value = cot[at].astype(F32) + back
        dx2[at] = value
        own[at] = value.astype(BF)
        row[...] += dg

    start, relay, lower, upper = scatter_parts(n, part, slots, stage, send, recv, finish, True)
    send_on, pass_on, end = gather_parts(n, own, dz, asend, arecv, local)
    if n == 4:
        block(corner, True)
        start(0, 1)
        others_loads()
        block(across)
        block(along)
        start(3)
        relay()
        block(me)
    else:
        block(order[0], True)
        others_loads()
        for to in order[1:]:
            block(to)
        start()
    for copy in loads:
        copy.wait()
    lax.fori_loop(0, n // 4, forward, 0)
    lower()
    send_on(0)
    upper()
    send_on(1)
    spread_rows(row[...], dgain)
    pass_on()
    lax.fori_loop(n // 4, n, forward, 0)
    end()


def attend_back(n, q_ref, qraw_ref, k_ref, kt_ref, v_ref, kraw_ref, dz_ref, wo_ref, lse_ref, low_ref, high_ref, cq_ref, sq_ref, ck_ref, sk_ref, gq_ref, gk_ref, attn_ref, part, x2, dq_ref, dk_ref, dv_ref, dgq_ref, dgk_ref, out, grads, dk_sum, dv_sum, slots, stage, send, recv, wo_sum, both, got, done, tsend, trecv, put):
    kv, block = pl.program_id(0), pl.program_id(1)
    keys = k_ref.shape[0]
    ratio = q_ref.shape[1] // 128
    scale = 128 ** (-0.5)

    def finish(at, total):
        out[at] = (x2[at] + total).astype(BF)

    start, relay, lower, upper = scatter_parts(n, part, slots, stage, send, recv, finish)
    core = lax.rem(lax.axis_index("fsdp"), 2)
    twin = lax.axis_index("fsdp") + 1 - 2 * core
    kheads, pieces, depth = both.shape[0], both.shape[1], both.shape[3]

    def move(number):
        return remote(
            both.at[number, :, 1 - core], got.at[number], tsend.at[number], trecv.at[number], "fsdp", twin
        )

    steps = pl.num_programs(0) * pl.num_programs(1)
    step = kv * pl.num_programs(1) + block

    @pl.when(step == 0)
    def _():
        greet(ring_places(n) + [("fsdp", twin)])
        start()
        dgq_ref[...] = jnp.zeros_like(dgq_ref)
        dgk_ref[...] = jnp.zeros_like(dgk_ref)

    @pl.when(step == steps * 3 // 8)
    def _():
        relay()

    @pl.when(block == 0)
    def _():
        dk_sum[...] = jnp.zeros_like(dk_sum)
        dv_sum[...] = jnp.zeros_like(dv_sum)
        wo_sum[...] = jnp.zeros_like(wo_sum)

    bias = bias_of(low_ref, high_ref, keys)
    dattn = dot_nt(dz_ref[...], wo_ref[...]).astype(BF)

    def prep_back(grad, raw, gain, cos, sin):
        du = grad * cos - pltpu.roll(grad, 64, 1) * sin
        return norm_back(raw, gain, du)

    for r in range(ratio):
        span = slice(r * 128, r * 128 + 128)
        qh, dah = q_ref[:, span], dattn[:, span]
        lse = lse_ref[pl.ds(kv * ratio + r, 1), :]
        scores = dot_nt(k_ref[...], qh) * (scale * log2e) + bias
        probs = jnp.exp2(scores - lse)
        dprobs = dot_nt(v_ref[...], dah)
        delta = jnp.sum(probs * dprobs, axis=0, keepdims=True)
        ds = (probs * (dprobs - delta)).astype(BF)
        dv_sum[...] += dot(probs.astype(BF), dah)
        dk_sum[...] += dot(ds, qh)
        dqr = dot(kt_ref[...], ds).T * scale
        back, dg = prep_back(dqr, qraw_ref[:, span], gq_ref[...], cq_ref[...], sq_ref[...])
        dq_ref[:, span] = back.astype(BF)
        dgq_ref[0:1] += dg

    wo_sum[...] += dot_tn(attn_ref[...], dz_ref[...])

    @pl.when(block == pl.num_programs(1) - 1)
    def _():
        both[kv] = wo_sum[...].astype(BF).reshape(both.shape[1:])
        move(kv).start()
        dv_ref[...] = dv_sum[...].astype(BF)
        back, dg = prep_back(
            dk_sum[...] * scale, kraw_ref[...], gk_ref[...], ck_ref[...], sk_ref[...]
        )
        dk_ref[...] = back.astype(BF)
        dgk_ref[0:1] += dg

    @pl.when(step == steps - 1)
    def _():
        cw = grads.shape[2]
        writes = []
        for number in range(kheads):
            move(number).wait_recv()
            value = both[number, :, core].astype(F32) + got[number].astype(F32)
            done[number] = value.astype(BF).reshape(done.shape[1:])
            for i in range(done.shape[2] // cw):
                rows = pl.ds(number * pieces * depth, pieces * depth)
                writes.append(
                    pltpu.make_async_copy(
                        done.at[number, :, pl.ds(i * cw, cw)],
                        grads.at[n + i, rows],
                        put.at[number, i],
                    )
                )
        for copy in writes:
            copy.start()
        lower()
        upper()
        for copy in writes:
            copy.wait()
        for number in range(kheads):
            move(number).wait_send()


def gradient(n, counts, kept, flipped, beside, *refs):
    a_ref, bs = refs[0], refs[1 : 1 + len(counts)]
    refs = refs[1 + len(counts) + kept :]
    if beside:
        given, out_ref, taken, both, got, send, recv, esend, erecv, local = refs[:10]
        refs = refs[10:]
    else:
        out_ref, both, got, send, recv = refs[:5]
        refs = refs[5:]
    turned = a_ref if flipped else refs[0]
    step = pl.program_id(0)
    tiles = sum(counts)
    core = lax.rem(lax.axis_index("fsdp"), 2)
    twin = lax.axis_index("fsdp") + 1 - 2 * core
    blocks, depth, tile = both.shape[1], both.shape[3], both.shape[4]
    piece = min(1024, turned.shape[0])
    part = piece // (2 * depth)

    def move(number):
        slot = lax.rem(number, 2)
        return remote(
            both.at[slot, :, 1 - core], got.at[number], send.at[number], recv.at[number], "fsdp", twin
        )

    @pl.when(step == 0)
    def _():
        greet([("fsdp", twin)] + (others("seq", n) if beside else []))
        if beside:
            for copy in exchange_copies(n, [given], [taken], esend, erecv, local):
                copy.start()
        if not flipped:
            turned[...] = a_ref[...].T

    begin = 0
    for b_ref, count in zip(bs, counts):

        @pl.when((step >= begin) & (step < begin + count))
        def _(b_ref=b_ref):
            slot = lax.rem(step, 2)

            @pl.when(step >= 2)
            def _():
                move(step - 2).wait_send()

            for i in range(turned.shape[0] // piece):
                rows = dot(turned[i * piece : i * piece + piece, :], b_ref[...]).astype(BF)
                both[slot, i * part : i * part + part] = rows.reshape(part, 2, depth, tile)
            move(step).start()

        begin += count

    @pl.when(step >= 1)
    def _():
        last = step - 1
        move(last).wait_recv()
        lead = out_ref.shape[0]
        inner = blocks // lead
        for i in range(lead):
            own = both[lax.rem(last, 2), i * inner : i * inner + inner, core]
            other = got[last, i * inner : i * inner + inner]
            total = (own.astype(F32) + other.astype(F32)).astype(BF)
            out_ref[i] = total.reshape(inner * depth, tile)

    @pl.when(step == tiles)
    def _():
        if tiles >= 2:
            move(tiles - 2).wait_send()
        move(tiles - 1).wait_send()
        if beside:
            for copy in exchange_copies(n, [given], [taken], esend, erecv, local):
                copy.wait()


def exchange_copies(n, ins, outs, send, recv, local):
    me = lax.axis_index("seq")
    copies = []
    for i, (source, out) in enumerate(zip(ins, outs)):
        for j in range(1, n):
            to = lax.rem(me + j, n)
            k = i * (n - 1) + j - 1
            copies.append(
                remote(source.at[to], out.at[me], send.at[k], recv.at[k], "seq", to)
            )
        copies.append(pltpu.make_async_copy(source.at[me], out.at[me], local.at[i]))
    return copies


def exchange(n, source, out, send, recv, local):
    greet(others("seq", n))
    copies = exchange_copies(n, [source], [out], send, recv, local)
    for copy in copies:
        copy.start()
    for copy in copies:
        copy.wait()


def write_out(nf, own_gain, own_head, y, dx, gains, att, o, gu, dn, out, dx_out, g_one, q_out, k_out, v_out, g_q, g_k, o_out, g_two, gate_out, up_out, down_out):
    out[...] = y[...]
    dx_out[...] = dx[...]
    qw, kw = q_out.shape[1], k_out.shape[1]
    q_out[...] = att[0, :, :qw].astype(F32)
    k_out[...] = att[0, :, qw : qw + kw].astype(F32)
    v_out[...] = att[0, :, qw + kw :].astype(F32)
    o_out[...] = o[0].astype(F32)
    units = gate_out.shape[1]
    gate_out[...] = gu[0, :, :units].astype(F32)
    up_out[...] = gu[0, :, units:].astype(F32)
    down_out[...] = dn[0].astype(F32)

    @pl.when(pl.program_id(0) == 0)
    def _():
        spot = lax.axis_index("fsdp")
        owner = lax.axis_index("seq") * nf + spot
        begin = lax.rem(spot, 128 // own_gain) * own_gain
        wide = pltpu.roll(gains[...], lax.rem(128 - begin, 128), 1)
        g_one[...] = wide[0:1, :own_gain]
        g_two[...] = wide[1:2, :own_gain]
        heads = pltpu.roll(gains[...], lax.rem(128 - owner * own_head, 128), 1)
        g_q[...] = heads[2:3, :own_head]
        g_k[...] = heads[3:4, :own_head]


def last_stage(n, nf, dq, dk, dv, w, x, dx2, gain, gu, two, gq, gk, out, gu_out, gains, part, slots, stage, send, recv, row, small, wide, mid, seen, esend, erecv, local, gsend, grecv):
    me, spot = lax.axis_index("seq"), lax.axis_index("fsdp")
    greet(others("seq", n) + others("fsdp", nf))
    row[...] = jnp.zeros_like(row)
    rows, width = x.shape
    qw, kw = dq.shape[1], dk.shape[1]
    step = 512

    def block(to):
        at = pl.ds(pl.multiple_of(to * rows, rows), rows)

        def columns(number, carry):
            span = pl.ds(pl.multiple_of(number * step, step), step)
            value = dot_nt(dq[at, :], w[span, pl.ds(0, qw)])
            value += dot_nt(dk[at, :], w[span, pl.ds(qw, kw)])
            value += dot_nt(dv[at, :], w[span, pl.ds(qw + kw, kw)])
            part[to, :, span] = value.astype(BF)
            return carry

        lax.fori_loop(0, width // step, columns, 0)

    def finish(at, total):
        back, dg = norm_back(x[at].astype(F32), gain[...], total)
        out[at] = (dx2[at] + back).astype(BF)
        row[...] += dg

    start, relay, lower, upper = scatter_parts(n, part, slots, stage, send, recv, finish)
    exchanges = exchange_copies(n, [gu], [gu_out], esend, erecv, local)
    if n == 4:
        across, along, corner = square(me)
        block(corner)
        start(0, 1)
        block(across)
        start(2)
        block(along)
        start(3)
        relay()
        for copy in exchanges:
            copy.start()
        block(me)
    else:
        for j in range(n):
            block(lax.rem(me + j, n))
        start()
        for copy in exchanges:
            copy.start()
    lower()
    upper()
    small[...] = jnp.zeros_like(small)
    per = 128 * n * nf // width
    one = row[...]
    for f in range(nf):
        for seq in range(n):
            line = (seq * nf + f) // per
            small[f, seq, 0:1] = one[:, line * 128 : line * 128 + 128]
            small[f, seq, 1:2] = two[line : line + 1]
            small[f, seq, 2:3] = gq[0:1]
            small[f, seq, 3:4] = gk[0:1]
    far = []
    for j in range(1, nf):
        to = lax.rem(spot + j, nf)
        far.append(
            remote(small.at[to], wide.at[j - 1], gsend.at[j - 1], grecv.at[j - 1], "fsdp", to)
        )
    for copy in far:
        copy.start()
    for copy in far:
        copy.wait_recv()
    total = small[spot]
    for j in range(nf - 1):
        total += wide[j]
    mid[...] = total
    near = []
    for j in range(1, n):
        to = lax.rem(me + j, n)
        k = nf + j - 2
        near.append(remote(mid.at[to], seen.at[j - 1], gsend.at[k], grecv.at[k], "seq", to))
    for copy in near:
        copy.start()
    for copy in near:
        copy.wait_recv()
    result = mid[me]
    for j in range(n - 1):
        result += seen[j]
    gains[...] = result
    for copy in far + near:
        copy.wait_send()
    for copy in exchanges:
        copy.wait()


def after(value, done):
    return lax.optimization_barrier((value, done))[0]


def dma(count):
    return pltpu.SemaphoreType.DMA((count,))


def shards(
    n,
    nf,
    tokens,
    seq_lengths,
    pic_starts,
    pic_lengths,
    norm1_gain,
    w_query,
    w_key,
    w_value,
    q_gain,
    k_gain,
    w_out,
    norm2_gain,
    w_gate,
    w_up,
    w_down,
    cotangent,
):
    rows, width = tokens.shape
    group = rows * n
    depth = w_query.shape[0]
    head = q_gain.shape[0] * n * nf
    qw, kw = w_query.shape[1] // n, w_key.shape[1] // n
    cw = qw + 2 * kw
    fw = w_gate.shape[1] // n
    qheads, kheads = qw // head, kw // head
    ratio = qheads // kheads
    own_gain = norm1_gain.shape[0]
    own_head = q_gain.shape[0]

    entries = []
    for gain in (norm1_gain, norm2_gain, q_gain, k_gain):
        entries += [gain, jnp.zeros((128 - gain.shape[0],), BF)]
    packed = jnp.concatenate(entries).astype(F32)[None, :]

    gather_sems = [dma(gather_copies(n)), dma(gather_copies(n)), pltpu.SemaphoreType.DMA]
    line = nf == 8
    half = head // 2
    powers = -(np.arange(half, dtype=np.float32) * np.float32(2.0) / np.float32(head))
    freq = np.tile((np.float32(theta) ** powers).astype(np.float32), 2)[None, :]
    small = pl.BlockSpec(memory_space=pltpu.SMEM)
    held = nf if line else 1
    w_att, gu, xg, wo, gain_one, gain_two, gain_q, gain_k, cos, sin, low, high = pl.pallas_call(
        functools.partial(entry_stage, n, nf, line, own_gain, own_head),
        out_shape=(
            shape((n, held, depth, cw), BF),
            shape((n, depth, 2 * fw), BF),
            shape((n, rows, width), BF),
            shape((held, depth, width), BF),
            shape((1, width), F32),
            shape((1, width), F32),
            shape((1, head), F32),
            shape((1, head), F32),
            shape((group, head), F32),
            shape((group, head), F32),
            shape((8, group), jnp.int32),
            shape((8, group), jnp.int32),
        ),
        in_specs=[ANY] * 7 + [VMEM] + [small] * 3 + [VMEM],
        out_specs=(ANY,) * 4 + (VMEM,) * 8,
        scratch_shapes=[
            pltpu.VMEM((8, 128), F32),
            pltpu.VMEM((n, 8, 128), F32),
            pltpu.VMEM((nf, n, 8, 128), F32),
            dma(3 * (n - 1)),
            dma(3 * (n - 1)),
            dma(3),
            dma(2 * (n - 1)),
            dma(2 * (n - 1)),
            dma(2),
        ]
        + gather_sems
        + [
            dma(n + nf - 2),
            dma(n + nf - 2),
            dma(2),
            dma(10),
            dma(10),
            dma(10),
            dma(10),
            pltpu.SemaphoreType.DMA,
        ],
        compiler_params=comm_params(0),
    )(
        w_query, w_key, w_value, w_gate, w_up, tokens, w_out, packed,
        seq_lengths, pic_starts, pic_lengths, jnp.asarray(freq),
    )
    wo = wo.reshape(-1, width)
    w_att = w_att.reshape(n, -1, cw)
    if not line:
        wo = lax.all_gather(wo, "fsdp", axis=0, tiled=True)
        w_att = lax.all_gather(w_att, "fsdp", axis=1, tiled=True)
    w_att = w_att.reshape(width, cw)
    gu = lax.all_gather(gu, "fsdp", axis=1, tiled=True).reshape(width, 2 * fw)

    def whole(dims):
        return pl.BlockSpec(dims, lambda *ids: (0,) * len(dims))

    def by_rows(count, columns):
        return pl.BlockSpec((count, columns), lambda i: (i, 0))

    def by_cols(count, columns):
        return pl.BlockSpec((count, columns), lambda i: (0, i))

    blocks = group // 256
    n1, qraw, kraw, q, k, v, kt, vt, cg = pl.pallas_call(
        functools.partial(project, n),
        grid=(blocks,),
        out_shape=(
            shape((width, group), BF),
            shape((group, qw), F32),
            shape((group, kw), F32),
            shape((group, qw), BF),
            shape((group, kw), BF),
            shape((group, kw), BF),
            shape((kw, group), BF),
            shape((kw, group), BF),
            shape((n, rows, width), BF),
        ),
        in_specs=[
            by_rows(256, width),
            whole((1, width)),
            whole((width, cw)),
            whole((1, head)),
            whole((1, head)),
            by_rows(256, head),
            by_rows(256, head),
            ANY,
        ],
        out_specs=(
            by_cols(width, 256),
            by_rows(256, qw),
            by_rows(256, kw),
            by_rows(256, qw),
            by_rows(256, kw),
            by_rows(256, kw),
            by_cols(kw, 256),
            by_cols(kw, 256),
            ANY,
        ),
        scratch_shapes=gather_sems,
        compiler_params=comm_params(11),
    )(xg.reshape(group, width), gain_one, w_att, gain_q, gain_k, cos, sin, cotangent)

    attn, lse, part_out, cg, dn = pl.pallas_call(
        functools.partial(attend, n),
        grid=(blocks,),
        out_shape=(
            shape((group, qw), BF),
            shape((8, group), F32),
            shape((group, width), BF),
            shape((n, rows, width), BF),
            shape((n, depth, fw), BF),
        ),
        in_specs=[
            by_rows(256, qw),
            whole((group, kw)),
            whole((kw, group)),
            whole((qw, width)),
            by_cols(8, 256),
            by_cols(8, 256),
            ANY,
            ANY,
            ANY,
        ],
        out_specs=(by_rows(256, qw), by_cols(8, 256), by_rows(256, width), ANY, ANY),
        scratch_shapes=[pltpu.VMEM((group, 256), F32)]
        + gather_sems
        + [dma(n - 1), dma(n - 1), dma(1)],
        input_output_aliases={7: 3},
        compiler_params=comm_params(3),
    )(q, k, vt, wo, low, high, cotangent, cg, w_down.T)
    cg = cg.reshape(group, width)
    dn = lax.all_gather(dn, "fsdp", axis=1, tiled=True).reshape(width, fw)

    slots = [
        pltpu.VMEM((scatter_slots(n), rows, width), BF),
        pltpu.VMEM((rows, width), BF),
    ]
    sems = [dma(max(6, n - 1)), dma(max(6, n - 1))]

    x2, n2 = pl.pallas_call(
        functools.partial(middle_stage, n),
        out_shape=(shape((rows, width), F32), shape((n, rows, width), BF)),
        in_specs=[VMEM] * 3,
        out_specs=(VMEM, ANY),
        scratch_shapes=slots + [pltpu.VMEM((rows, width), BF)] + sems + gather_sems,
        compiler_params=comm_params(2),
    )(part_out.reshape(n, rows, width), tokens, gain_two)
    n2 = n2.reshape(group, width)

    tile = 256
    tiles = fw // tile
    cuts = 1
    while 2 * cuts <= tiles:
        cuts *= 2
    gate, up, hidden, n2_turned = pl.pallas_call(
        functools.partial(ffn_forward, cuts),
        grid=(tiles,),
        out_shape=(
            shape((group, fw), F32),
            shape((group, fw), F32),
            shape((group, fw), BF),
            shape((width, group), BF),
        ),
        in_specs=[
            whole((group, width)),
            by_cols(width, tile),
            pl.BlockSpec((width, tile), lambda i: (0, i + tiles)),
        ],
        out_specs=(by_cols(group, tile),) * 3
        + (pl.BlockSpec((width // cuts, group), lambda i: (jnp.minimum(i, cuts - 1), 0)),),
        compiler_params=plain_params(),
    )(n2, gu, gu)

    def product(number, a, *bs, into=None, flipped=False, given=None):
        tile = 512
        while any(b.shape[1] % tile for b in bs):
            tile //= 2
        counts = [b.shape[1] // tile for b in bs]
        begins = [sum(counts[:i]) for i in range(len(bs))]
        tiles = sum(counts)

        def spec(begin, count):
            return pl.BlockSpec(
                (group, tile), lambda i: (0, jnp.clip(i - begin, 0, count - 1))
            )

        dims = (n, width // n // 2, tiles * tile) if into is None else into.shape
        kept = [] if into is None else [into]
        side = [] if given is None else [given]
        blocks = width // (2 * depth)
        outs = [pl.BlockSpec((n, dims[1], tile), lambda i: (0, 0, jnp.maximum(i - 1, 0)))]
        extra = [dma(n - 1), dma(n - 1), dma(1)] if side else []
        result = pl.pallas_call(
            functools.partial(gradient, n, counts, len(kept), flipped, len(side)),
            grid=(tiles + 1,),
            out_shape=(shape(dims, BF),) + tuple(shape(g.shape, BF) for g in side),
            in_specs=[whole(a.shape)]
            + [spec(b, c) for b, c in zip(begins, counts)]
            + [ANY] * len(kept + side),
            out_specs=tuple(outs + [ANY] * len(side)),
            scratch_shapes=[
                pltpu.VMEM((2, blocks, 2, depth, tile), BF),
                pltpu.VMEM((tiles, blocks, depth, tile), BF),
                dma(tiles),
                dma(tiles),
            ]
            + extra
            + ([] if flipped else [pltpu.VMEM((width, group), BF)]),
            input_output_aliases={} if into is None else {1 + len(bs): 0},
            compiler_params=comm_params(number),
        )(a, *bs, *kept, *side)
        return result if side else result[0]

    same_core = [[core + 2 * i for i in range(nf // 2)] for core in range(2)]

    def reduce_rows(grad):
        return lax.psum_scatter(
            grad, "fsdp", scatter_dimension=1, tiled=True, axis_index_groups=same_core
        )

    dn_grad = product(12, cg, hidden)
    dn_share = reduce_rows(dn_grad)

    dgate, dup = pl.pallas_call(
        ffn_back,
        grid=(tiles,),
        out_shape=(shape((group, fw), BF), shape((group, fw), BF)),
        in_specs=[
            whole((group, width)),
            by_cols(width, tile),
            by_cols(group, tile),
            by_cols(group, tile),
        ],
        out_specs=(by_cols(group, tile),) * 2,
        compiler_params=plain_params(),
    )(cg, after(dn, dn_grad), gate, up)

    gu_grad = product(13, n2_turned, dgate, dup, flipped=True)
    gu_share = reduce_rows(gu_grad)

    dx2, dz, dgain_two, part_y = pl.pallas_call(
        functools.partial(back_stage, n),
        out_shape=(
            shape((rows, width), F32),
            shape((n, rows, width), BF),
            shape((width // 128, 128), F32),
            shape((n, rows, width), BF),
        ),
        in_specs=[ANY] * 3 + [VMEM] * 3 + [ANY] * 2,
        out_specs=(VMEM, ANY, VMEM, VMEM),
        scratch_shapes=[pltpu.VMEM((n, rows, width), BF)]
        + slots
        + [pltpu.VMEM((rows, width), BF)]
        + sems
        + gather_sems
        + [
            pltpu.VMEM((1, width), F32),
            pltpu.VMEM((group, fw), BF),
            pltpu.VMEM((width, fw), BF),
            dma(2),
            pltpu.VMEM((group, fw), BF),
            pltpu.VMEM((group, fw), BF),
            pltpu.VMEM((width, 2 * fw), BF),
            pltpu.SemaphoreType.DMA((2, n)),
            dma(width // 512),
        ],
        compiler_params=comm_params(4),
    )(
        after(dgate, gu_grad), dup, gu, x2, cotangent, gain_two, hidden, dn,
    )
    dz = dz.reshape(group, width)

    wide = ratio * head
    dq, dk, dv, dgain_q, dgain_k, branch, wo_grad = pl.pallas_call(
        functools.partial(attend_back, n),
        grid=(kheads, blocks),
        out_shape=(
            shape((group, qw), BF),
            shape((group, kw), BF),
            shape((group, kw), BF),
            shape((8, head), F32),
            shape((8, head), F32),
            shape((rows, width), BF),
            shape((n + width // cw, width // n // 2, cw), BF),
        ),
        in_specs=[
            pl.BlockSpec((256, wide), lambda h, b: (b, h)),
            pl.BlockSpec((256, wide), lambda h, b: (b, h)),
            pl.BlockSpec((group, head), lambda h, b: (0, h)),
            pl.BlockSpec((head, group), lambda h, b: (h, 0)),
            pl.BlockSpec((group, head), lambda h, b: (0, h)),
            pl.BlockSpec((group, head), lambda h, b: (0, h)),
            pl.BlockSpec((256, width), lambda h, b: (b, 0)),
            pl.BlockSpec((wide, width), lambda h, b: (h, 0)),
            pl.BlockSpec((8, 256), lambda h, b: (0, b)),
            pl.BlockSpec((8, 256), lambda h, b: (0, b)),
            pl.BlockSpec((8, 256), lambda h, b: (0, b)),
            pl.BlockSpec((256, head), lambda h, b: (b, 0)),
            pl.BlockSpec((256, head), lambda h, b: (b, 0)),
            whole((group, head)),
            whole((group, head)),
            whole((1, head)),
            whole((1, head)),
            pl.BlockSpec((256, wide), lambda h, b: (b, h)),
            VMEM,
            VMEM,
        ],
        out_specs=(
            pl.BlockSpec((256, wide), lambda h, b: (b, h)),
            pl.BlockSpec((group, head), lambda h, b: (0, h)),
            pl.BlockSpec((group, head), lambda h, b: (0, h)),
            whole((8, head)),
            whole((8, head)),
            VMEM,
            ANY,
        ),
        scratch_shapes=[pltpu.VMEM((group, head), F32), pltpu.VMEM((group, head), F32)]
        + slots
        + sems
        + [
            pltpu.VMEM((wide, width), F32),
            pltpu.VMEM((kheads, wide // (2 * depth), 2, depth, width), BF),
            pltpu.VMEM((kheads, wide // (2 * depth), depth, width), BF),
            pltpu.VMEM((kheads, wide // 2, width), BF),
            dma(kheads),
            dma(kheads),
            pltpu.SemaphoreType.DMA((kheads, width // cw)),
        ],
        compiler_params=comm_params(5),
    )(
        q, qraw, k, kt, v, kraw, dz, wo, lse, low, high, cos, sin, cos, sin, gain_q, gain_k,
        attn, part_y, x2,
    )

    att_grad, dn_mine = product(
        15, n1, dq, dk, dv, into=wo_grad, flipped=True, given=dn_share
    )
    att_share = reduce_rows(after(att_grad, gu_share))

    input_raw, gu_mine, gains = pl.pallas_call(
        functools.partial(last_stage, n, nf),
        out_shape=(
            shape((rows, width), BF),
            shape(gu_share.shape, BF),
            shape((8, 128), F32),
        ),
        in_specs=[VMEM] * 7 + [ANY] + [VMEM] * 3,
        out_specs=(VMEM, ANY, VMEM),
        scratch_shapes=[pltpu.VMEM((n, rows, width), BF)]
        + slots
        + sems
        + [
            pltpu.VMEM((1, width), F32),
            pltpu.VMEM((nf, n, 8, 128), F32),
            pltpu.VMEM((nf - 1, n, 8, 128), F32),
            pltpu.VMEM((n, 8, 128), F32),
            pltpu.VMEM((n - 1, 8, 128), F32),
            dma(n - 1),
            dma(n - 1),
            dma(1),
            dma(n + nf - 2),
            dma(n + nf - 2),
        ],
        compiler_params=comm_params(7),
    )(
        after(dq, att_grad), dk, dv, w_att, tokens, dx2, gain_one, gu_share,
        dgain_two, dgain_q, dgain_k,
    )
    att_mine = pl.pallas_call(
        functools.partial(exchange, n),
        out_shape=shape((n, depth, cw), BF),
        in_specs=[ANY],
        out_specs=ANY,
        scratch_shapes=[dma(n - 1), dma(n - 1), dma(1)],
        compiler_params=comm_params(9),
    )(after(att_share, gains))

    def slab(count):
        return pl.BlockSpec((1, depth, count), lambda i: (i, 0, 0))

    each = width // n
    per = cw // each
    results = pl.pallas_call(
        functools.partial(write_out, nf, own_gain, own_head),
        grid=(n,),
        out_shape=(
            shape((rows, width), BF),
            shape((rows, width), BF),
            shape((1, own_gain), F32),
            shape(w_query.shape, F32),
            shape(w_key.shape, F32),
            shape(w_value.shape, F32),
            shape((1, own_head), F32),
            shape((1, own_head), F32),
            shape(w_out.shape, F32),
            shape((1, own_gain), F32),
            shape(w_gate.shape, F32),
            shape(w_up.shape, F32),
            shape(w_gate.shape, F32),
        ),
        in_specs=[
            by_rows(rows // n, width),
            by_rows(rows // n, width),
            whole((8, 128)),
            slab(cw),
            pl.BlockSpec(
                (1, depth, each), lambda i: (n + lax.div(i, per), 0, lax.rem(i, per))
            ),
            slab(2 * fw),
            slab(fw),
        ],
        out_specs=(
            by_rows(rows // n, width),
            by_rows(rows // n, width),
            whole((1, own_gain)),
            by_cols(depth, qw),
            by_cols(depth, kw),
            by_cols(depth, kw),
            whole((1, own_head)),
            whole((1, own_head)),
            by_cols(depth, each),
            whole((1, own_gain)),
            by_cols(depth, fw),
            by_cols(depth, fw),
            by_cols(depth, fw),
        ),
        compiler_params=plain_params(),
    )(branch, input_raw, gains, att_mine, att_share, gu_mine, dn_mine)
    flat = [r.reshape(-1) if i in (2, 6, 7, 9) else r for i, r in enumerate(results)]
    return tuple(flat[:-1]) + (flat[-1].T,)


def solution(mesh):
    return jax.shard_map(
        functools.partial(shards, mesh.shape["seq"], mesh.shape["fsdp"]),
        mesh=mesh,
        in_specs=(
            P(("fsdp", "seq"), None),
            P("fsdp", None),
            P("fsdp", None),
            P("fsdp", None),
            P(("seq", "fsdp")),
            P(("seq", "fsdp"), None),
            P(("seq", "fsdp"), None),
            P(("seq", "fsdp"), None),
            P(("seq", "fsdp")),
            P(("seq", "fsdp")),
            P(("seq", "fsdp"), None),
            P(("seq", "fsdp")),
            P(("seq", "fsdp"), None),
            P(("seq", "fsdp"), None),
            P(None, ("seq", "fsdp")),
            P(("fsdp", "seq"), None),
        ),
        out_specs=(
            P(("fsdp", "seq"), None),
            P(("fsdp", "seq"), None),
            P(("seq", "fsdp")),
            P(("seq", "fsdp"), None),
            P(("seq", "fsdp"), None),
            P(("seq", "fsdp"), None),
            P(("seq", "fsdp")),
            P(("seq", "fsdp")),
            P(("seq", "fsdp"), None),
            P(("seq", "fsdp")),
            P(("seq", "fsdp"), None),
            P(("seq", "fsdp"), None),
            P(None, ("seq", "fsdp")),
        ),
        check_vma=False,
    )
```

```python
import functools

import jax
import jax.numpy as jnp
import numpy as np
from jax import lax
from jax.experimental import pallas as pl
from jax.experimental.pallas import tpu as pltpu
from jax.sharding import PartitionSpec as P

epsilon = 1e-06
theta = 1000000.0
masked_score = -1e30
log2e = 1.4426950408889634

MESH = pl.DeviceIdType.MESH
ANY = pl.BlockSpec(memory_space=pl.ANY)
VMEM = pl.BlockSpec(memory_space=pltpu.VMEM)
BF = jnp.bfloat16
F32 = jnp.float32
LIMIT = 60 * 1024 * 1024


def dot(a, b):
    return jnp.dot(a, b, preferred_element_type=F32)


def dot_nt(a, b):
    return lax.dot_general(a, b, (((1,), (1,)), ((), ())), preferred_element_type=F32)


def dot_tn(a, b):
    return lax.dot_general(a, b, (((0,), (0,)), ((), ())), preferred_element_type=F32)


def shape(dims, dtype):
    return jax.ShapeDtypeStruct(dims, dtype)


def comm_params(number):
    return pltpu.CompilerParams(
        collective_id=number, has_side_effects=True, vmem_limit_bytes=LIMIT
    )


def plain_params():
    return pltpu.CompilerParams(vmem_limit_bytes=LIMIT)


def remote(src, dst, send, recv, axis, index):
    return pltpu.make_async_remote_copy(
        src_ref=src,
        dst_ref=dst,
        send_sem=send,
        recv_sem=recv,
        device_id={axis: index},
        device_id_type=MESH,
    )


def greet(places):
    barrier = pltpu.get_barrier_semaphore()
    for axis, index in places:
        pl.semaphore_signal(barrier, inc=1, device_id={axis: index}, device_id_type=MESH)
    pl.semaphore_wait(barrier, len(places))


def others(axis, n):
    me = lax.axis_index(axis)
    return [(axis, lax.rem(me + j, n)) for j in range(1, n)]


def square(me):
    return me + 1 - 2 * lax.rem(me, 2), lax.rem(me + 2, 4), 3 - me


def ring_places(n):
    me = lax.axis_index("seq")
    if n == 4:
        across, along, _ = square(me)
        return [("seq", across), ("seq", along)]
    return others("seq", n)


def gather_copies(n):
    return 6 if n == 4 else n - 1


def gather_parts(n, own, out, send, recv, local):
    me = lax.axis_index("seq")
    keep = pltpu.make_async_copy(own, out.at[me], local)
    half = own.shape[0] // 2
    low, high = pl.ds(0, half), pl.ds(half, half)
    if n == 4:
        across, along, _ = square(me)
        moves = [
            (own.at[low], out.at[me, low], across),
            (own.at[high], out.at[me, high], along),
            (own.at[high], out.at[me, high], across),
            (own.at[low], out.at[me, low], along),
            (out.at[across, low], out.at[across, low], along),
            (out.at[along, high], out.at[along, high], across),
        ]
    else:
        moves = [(own, out.at[me], lax.rem(me + j, n)) for j in range(1, n)]
    copies = [
        remote(src, dst, send.at[i], recv.at[i], "seq", to)
        for i, (src, dst, to) in enumerate(moves)
    ]

    def start(part=None):
        chosen = range(len(copies))
        if n == 4:
            chosen = {None: (0, 1, 2, 3), 0: (0, 3), 1: (1, 2), 2: (0, 1), 3: (2, 3)}[part]
        if n == 4 or part not in (0, 2):
            for i in chosen:
                copies[i].start()
        if part not in (0, 2):
            keep.start()

    def relay():
        if n == 4:
            copies[0].wait_recv()
            copies[4].start()
            copies[1].wait_recv()
            copies[5].start()

    def finish():
        for copy in copies[2:] if n == 4 else copies:
            copy.wait_recv()
        for copy in copies:
            copy.wait_send()
        keep.wait()

    return start, relay, finish


def scatter_slots(n):
    return 4 if n == 4 else n - 1


def scatter_parts(n, part, slots, stage, send, recv, finish, held=False):
    me = lax.axis_index("seq")
    rows = part.shape[1]
    half = rows // 2
    low, high = pl.ds(0, half), pl.ds(half, half)
    if n == 4:
        across, along, corner = square(me)
        moves = [
            (part.at[corner, low], slots.at[2, low], along),
            (part.at[corner, high], slots.at[2, high], across),
            (part.at[across, high], slots.at[0, high], across),
            (part.at[along, low], slots.at[1, low], along),
            (stage.at[low], slots.at[0, low], across),
            (stage.at[high], slots.at[1, high], along),
        ]
        count = 2
    else:
        moves = []
        for j in range(1, n):
            to = lax.rem(me + j, n)
            moves.append((part.at[to], slots.at[j - 1], to))
        count = n - 1
    copies = [
        remote(src, dst, send.at[i], recv.at[i], "seq", to)
        for i, (src, dst, to) in enumerate(moves)
    ]

    def start(*chosen):
        chosen = chosen if chosen else (0, 1, 3) if held else (0, 1, 2, 3)
        for copy in [copies[i] for i in chosen] if n == 4 else copies:
            copy.start()

    def relay():
        if n == 4:
            copies[0].wait_recv()
            stage[low] = (part[across, low].astype(F32) + slots[2, low].astype(F32)).astype(BF)
            copies[4].start()
            if held:
                copies[2].start()
            copies[1].wait_recv()
            stage[high] = (part[along, high].astype(F32) + slots[2, high].astype(F32)).astype(BF)
            copies[5].start()

    step = 32

    def chunk(number, carry):
        at = pl.ds(pl.multiple_of(number * step, step), step)
        value = part[me, at].astype(F32)
        for slot in range(count):
            value += slots[slot, at].astype(F32)
        finish(at, value)
        return carry

    def lower():
        for copy in copies[3:5] if n == 4 else copies:
            copy.wait_recv()
        lax.fori_loop(0, half // step, chunk, 0)

    def upper():
        if n == 4:
            copies[2].wait_recv()
            copies[5].wait_recv()
        lax.fori_loop(half // step, rows // step, chunk, 0)
        for copy in copies:
            copy.wait_send()

    return start, relay, lower, upper


def inverse_rms(values):
    return lax.rsqrt(jnp.mean(values * values, axis=-1, keepdims=True) + epsilon)


def norm_back(values, gain, grad):
    inverse = inverse_rms(values)
    scaled = grad * gain
    back = inverse * scaled - values * (
        inverse * inverse * inverse * jnp.mean(scaled * values, axis=-1, keepdims=True)
    )
    return back, jnp.sum(grad * values * inverse, axis=0, keepdims=True)


def start_columns(n, views, send, recv, local, begin=True):
    me = lax.axis_index("seq")
    width = views[0][0].shape[1] // n
    copies, keeps = [], []
    for i, (ref, out, place) in enumerate(views):
        for j in range(1, n):
            to = lax.rem(me + j, n)
            columns = pl.ds(pl.multiple_of(to * width, 128), width)
            k = i * (n - 1) + j - 1
            copies.append(
                remote(
                    ref.at[:, columns],
                    out.at[me, :, pl.ds(place * width, width)],
                    send.at[k],
                    recv.at[k],
                    "seq",
                    to,
                )
            )
        columns = pl.ds(pl.multiple_of(me * width, 128), width)
        keeps.append(
            pltpu.make_async_copy(
                ref.at[:, columns], out.at[me, :, pl.ds(place * width, width)], local.at[i]
            )
        )
    if begin:
        for copy in copies + keeps:
            copy.start()
    return copies + keeps


def line_gather(cell, own, send, recv):
    spot = lax.axis_index("fsdp")
    z = lax.div(spot, 2)
    twin = spot + 1 - 2 * lax.rem(spot, 2)

    def hop(number, block, to):
        source = own if isinstance(block, str) else cell(block)
        target = cell(spot if isinstance(block, str) else block)
        return remote(source, target, send.at[number], recv.at[number], "fsdp", to)

    def up(k):
        return hop(k, "own" if k == 0 else spot - 2 * k, spot + 2)

    def down(k):
        return hop(3 + k, "own" if k == 0 else spot + 2 * k, spot - 2)

    def over(offset):
        return hop(6 + z + offset, "own" if offset == 0 else spot + 2 * offset, twin)

    def from_twin(offset):
        return hop(6 + z + offset, twin + 2 * offset, twin)

    def first():
        @pl.when(z < 3)
        def _():
            up(0).start()

        @pl.when(z > 0)
        def _():
            down(0).start()

        over(0).start()

    def step(k):
        @pl.when(z >= k)
        def _():
            up(k - 1).wait_recv()
            if k < 3:

                @pl.when(z < 3)
                def _():
                    up(k).start()

            over(-k).start()

        @pl.when(z + k <= 3)
        def _():
            down(k - 1).wait_recv()
            if k < 3:

                @pl.when(z > 0)
                def _():
                    down(k).start()

            over(k).start()

    def finish():
        from_twin(0).wait_recv()
        over(0).wait_send()
        for k in range(1, 4):

            @pl.when(z >= k)
            def _():
                from_twin(-k).wait_recv()
                over(-k).wait_send()

            @pl.when(z + k <= 3)
            def _():
                from_twin(k).wait_recv()
                over(k).wait_send()

        for k in range(3):

            @pl.when((z >= k) & (z < 3))
            def _():
                up(k).wait_send()

            @pl.when((z + k <= 3) & (z > 0))
            def _():
                down(k).wait_send()

    return first, step, finish


def entry_stage(n, nf, line, own_gain, own_head, wq, wk, wv, wg, wu, x, w_out, raw, lengths, starts, sizes, freq, w_att, gu, xg, wo, gain_one, gain_two, gain_q, gain_k, cos, sin, low, high, mine, seen, gains, qsend, qrecv, qlocal, wsend, wrecv, wlocal, send, recv, local, gsend, grecv, glocal, asend, arecv, osend, orecv, olocal):
    me, spot = lax.axis_index("seq"), lax.axis_index("fsdp")
    greet(others("seq", n) + others("fsdp", nf))
    place = spot if line else 0
    if line:
        o_first, o_step, o_finish = line_gather(lambda f: wo.at[f], w_out, osend, orecv)
        a_first, a_step, a_finish = line_gather(
            lambda f: w_att.at[:, f], w_att.at[:, spot], asend, arecv
        )
        o_first()
    widths = [wq.shape[1] // n, wk.shape[1] // n, wv.shape[1] // n]
    begins = [0, widths[0], widths[0] + widths[1]]
    near = []
    for j in range(1, n):
        to = lax.rem(me + j, n)
        for i, ref in enumerate((wq, wk, wv)):
            columns = pl.ds(pl.multiple_of(to * widths[i], 128), widths[i])
            near.append(
                remote(
                    ref.at[:, columns],
                    w_att.at[me, place, :, pl.ds(begins[i], widths[i])],
                    qsend.at[3 * j - 3 + i],
                    qrecv.at[3 * j - 3 + i],
                    "seq",
                    to,
                )
            )
    for i, ref in enumerate((wq, wk, wv)):
        columns = pl.ds(pl.multiple_of(me * widths[i], 128), widths[i])
        near.append(
            pltpu.make_async_copy(
                ref.at[:, columns],
                w_att.at[me, place, :, pl.ds(begins[i], widths[i])],
                qlocal.at[i],
            )
        )
    for copy in near:
        copy.start()
    mine[...] = jnp.zeros_like(mine)
    for count, first, index in (
        (own_gain, 0, lax.rem(spot, 128 // own_gain)),
        (own_head, 2, me * nf + spot),
    ):
        for at in range(128 // count):

            @pl.when(index == at)
            def _():
                for i in (first, first + 1):
                    mine[i : i + 1, at * count : at * count + count] = raw[
                        :, i * 128 : i * 128 + count
                    ].astype(F32)

    small = [pltpu.make_async_copy(mine, seen.at[me], glocal.at[0])]
    for j in range(1, n):
        to = lax.rem(me + j, n)
        small.append(remote(mine, seen.at[me], gsend.at[j - 1], grecv.at[j - 1], "seq", to))
    keep = pltpu.make_async_copy(w_out, wo.at[place], olocal)
    for copy in small + [keep]:
        copy.start()
    def rope():
        group = cos.shape[0]
        border_one = lengths[0, 0]
        border_two = border_one + lengths[0, 1]

        def begin_of(places):
            later = jnp.where(places >= border_one, border_one, 0)
            return jnp.where(places >= border_two, border_two, later)

        step = 128
        lane = lax.broadcasted_iota(jnp.int32, (step, 128), 1)

        def turn(number, carry):
            at = pl.ds(pl.multiple_of(number * step, step), step)
            places = lax.broadcasted_iota(jnp.int32, (step, 128), 0) + number * step
            angle = (places - begin_of(places)).astype(F32) * freq[...]
            cos[at, :] = jnp.cos(angle)
            sine = jnp.sin(angle)
            sin[at, :] = jnp.where(lane < 64, -sine, sine)
            return carry

        lax.fori_loop(0, group // step, turn, 0)
        places = lax.broadcasted_iota(jnp.int32, (8, group), 1)
        end = jnp.where(places >= border_one, border_two, border_one)
        end = jnp.where(places >= border_two, group, end)
        picture = jnp.zeros_like(places)
        for i in range(starts.shape[1]):
            first, count = starts[0, i], sizes[0, i]
            inside = (places >= first) & (places < first + count)
            picture = jnp.where(inside, jnp.maximum(picture, first + count), picture)
        low[...] = begin_of(places)
        high[...] = jnp.maximum(places, jnp.minimum(picture, end) - 1)

    start, relay, finish = gather_parts(n, x, xg, send, recv, local)
    start(2)
    rope()
    if line:
        o_step(1)
        o_step(2)
    for copy in near:
        copy.wait()
    if line:
        a_first()
    copies = start_columns(n, [(wg, gu, 0), (wu, gu, 1)], wsend, wrecv, wlocal)
    start(3)
    for copy in small:
        copy.wait()
    wide = [pltpu.make_async_copy(seen, gains.at[spot], glocal.at[1])]
    for j in range(1, nf):
        to = lax.rem(spot + j, nf)
        k = n + j - 2
        wide.append(remote(seen, gains.at[spot], gsend.at[k], grecv.at[k], "fsdp", to))
    for copy in wide:
        copy.start()

    def unpack():
        per = 128 // own_gain
        for row in range(n * nf // per):
            seq, first = row * per // nf, row * per % nf
            one = gains[first, seq, 0:1, :]
            two = gains[first, seq, 1:2, :]
            for f in range(first + 1, first + per):
                one += gains[f, seq, 0:1, :]
                two += gains[f, seq, 1:2, :]
            gain_one[:, row * 128 : row * 128 + 128] = one
            gain_two[:, row * 128 : row * 128 + 128] = two
        total = jnp.zeros((8, 128), F32)
        for f in range(nf):
            for seq in range(n):
                total += gains[f, seq]
        gain_q[...] = total[2:3, :]
        gain_k[...] = total[3:4, :]

    relay()
    if line:
        o_step(3)
        a_step(1)
        a_step(2)
        a_step(3)
        o_finish()
        a_finish()
    finish()
    keep.wait()
    for copy in wide:
        copy.wait()
    unpack()
    for copy in copies:
        copy.wait()


def half_gather(n, begin, cot, cg, send, recv, local, places, beside):
    at = pl.ds(begin, cot.shape[0] // 2)
    start, relay, finish = gather_parts(n, cot.at[at], cg.at[:, at], send, recv, local)
    step, steps = pl.program_id(0), pl.num_programs(0)

    @pl.when(step == 0)
    def _():
        greet(places)
        start()
        beside()

    @pl.when(step == steps - 1)
    def _():
        relay()

    return finish


def project(n, x_ref, gain_ref, w_ref, gq_ref, gk_ref, cos_ref, sin_ref, cot, n1_ref, qraw_ref, kraw_ref, q_ref, k_ref, v_ref, kt_ref, vt_ref, cg, send, recv, local):
    finish_half = half_gather(n, 0, cot, cg, send, recv, local, ring_places(n), lambda: None)
    x = x_ref[...].astype(F32)
    normed = (x * inverse_rms(x) * gain_ref[...]).astype(BF)
    n1_ref[...] = normed.T
    full = dot(normed, w_ref[...])
    qw, kw = q_ref.shape[1], k_ref.shape[1]
    cos, sin = cos_ref[...], sin_ref[...]

    def prep(head, gain):
        u = head * inverse_rms(head) * gain
        return u * cos + pltpu.roll(u, 64, 1) * sin

    qraw_ref[...] = full[:, :qw]
    kraw_ref[...] = full[:, qw : qw + kw]
    v = full[:, qw + kw :]
    v_ref[...] = v.astype(BF)
    vt_ref[...] = v.T.astype(BF)
    for h in range(qw // 128):
        q_ref[:, h * 128 : h * 128 + 128] = prep(
            full[:, h * 128 : h * 128 + 128], gq_ref[...]
        ).astype(BF)
    for h in range(kw // 128):
        turned = prep(full[:, qw + h * 128 : qw + h * 128 + 128], gk_ref[...])
        k_ref[:, h * 128 : h * 128 + 128] = turned.astype(BF)
        kt_ref[h * 128 : h * 128 + 128, :] = turned.T.astype(BF)

    @pl.when(pl.program_id(0) == pl.num_programs(0) - 1)
    def _():
        finish_half()


def bias_of(low_ref, high_ref, keys):
    key = lax.broadcasted_iota(jnp.int32, (keys, low_ref.shape[1]), 0)
    fine = (key >= low_ref[0:1, :]) & (key <= high_ref[0:1, :])
    return jnp.where(fine, 0.0, masked_score)


def attend(n, q_ref, k_ref, vt_ref, wo_ref, low_ref, high_ref, cot, cg_half, wd, attn_ref, lse_ref, part_ref, cg, dn, bias, send, recv, local, wsend, wrecv, wlocal):
    copies = start_columns(n, [(wd, dn, 0)], wsend, wrecv, wlocal, False)

    def beside():
        for copy in copies:
            copy.start()

    finish_half = half_gather(
        n, cot.shape[0] // 2, cot, cg, send, recv, local, others("seq", n), beside
    )
    keys = k_ref.shape[0]
    bias[...] = bias_of(low_ref, high_ref, keys)
    heads = q_ref.shape[1] // 128
    ratio = heads // (k_ref.shape[1] // 128)
    factor = 128 ** (-0.5) * log2e
    for h in range(heads):
        kv = h // ratio
        scores = dot_nt(
            k_ref[:, kv * 128 : kv * 128 + 128], q_ref[:, h * 128 : h * 128 + 128]
        )
        scores = scores * factor + bias[...]
        top = jnp.max(scores, axis=0, keepdims=True)
        probs = jnp.exp2(scores - top)
        total = jnp.sum(probs, axis=0, keepdims=True)
        mixed = dot(vt_ref[kv * 128 : kv * 128 + 128, :], probs.astype(BF))
        lse_ref[h : h + 1, :] = top + jnp.log2(total)
        attn_ref[:, h * 128 : h * 128 + 128] = (mixed / total).T.astype(BF)
    part_ref[...] = dot(attn_ref[...], wo_ref[...]).astype(BF)

    @pl.when(pl.program_id(0) == pl.num_programs(0) - 1)
    def _():
        finish_half()
        for copy in copies:
            copy.wait()


def middle_stage(n, part, x, gain, x2, n2, slots, stage, own, send, recv, asend, arecv, local):
    greet(ring_places(n))

    def finish(at, total):
        value = x[at].astype(F32) + total
        x2[at] = value
        own[at] = (value * inverse_rms(value) * gain[...]).astype(BF)

    start, relay, lower, upper = scatter_parts(n, part, slots, stage, send, recv, finish, True)
    send_on, pass_on, end = gather_parts(n, own, n2, asend, arecv, local)
    start()
    relay()
    lower()
    send_on(0)
    upper()
    send_on(1)
    pass_on()
    end()


def ffn_forward(cuts, n2_ref, wg_ref, wu_ref, gate_ref, up_ref, hidden_ref, turned_ref):
    count = n2_ref.shape[1] // cuts
    step = pl.program_id(0)

    @pl.when(step < cuts)
    def _():
        turned_ref[...] = n2_ref[:, pl.ds(pl.multiple_of(step * count, 128), count)].T

    gate = dot(n2_ref[...], wg_ref[...])
    up = dot(n2_ref[...], wu_ref[...])
    s = jax.nn.sigmoid(gate)
    silu = gate * s
    gate_ref[...] = up * (s * (1.0 + gate * (1.0 - s)))
    up_ref[...] = silu
    hidden_ref[...] = (silu * up).astype(BF)


def ffn_back(cot_ref, wd_ref, gate_ref, up_ref, dgate_ref, dup_ref):
    dh = dot(cot_ref[...], wd_ref[...])
    dgate_ref[...] = (dh * gate_ref[...]).astype(BF)
    dup_ref[...] = (dh * up_ref[...]).astype(BF)


def spread_rows(row, out):
    for i in range(out.shape[0]):
        out[i : i + 1, :] = row[:, i * 128 : i * 128 + 128]


def back_stage(n, dgate_far, dup_far, gu_far, x2, cot, gain, hidden_far, dn_far, dx2, dz, dgain, part_y, part, slots, stage, own, send, recv, asend, arecv, local, row, hidden, dn, load, dgate, dup, gu, rload, wload):
    greet(ring_places(n))
    me = lax.axis_index("seq")
    rows, width = x2.shape
    units = dup.shape[1]
    step = 512

    def row_loads(to):
        at = pl.ds(pl.multiple_of(to * rows, rows), rows)
        return [
            pltpu.make_async_copy(dgate_far.at[at], dgate.at[at], rload.at[0, to]),
            pltpu.make_async_copy(dup_far.at[at], dup.at[at], rload.at[1, to]),
        ]

    def weight_load(number):
        at = pl.ds(pl.multiple_of(number * step, step), step)
        return pltpu.make_async_copy(gu_far.at[at], gu.at[at], wload.at[number])

    order = [lax.rem(me + j, n) for j in range(1, n)] + [me]
    if n == 4:
        across, along, corner = square(me)
        order = [corner, across, along, me]
    for copy in row_loads(order[0]):
        copy.start()
    for number in range(width // step):
        weight_load(number).start()
    for copy in row_loads(order[1]):
        copy.start()
    loads = [
        pltpu.make_async_copy(hidden_far, hidden, load.at[0]),
        pltpu.make_async_copy(dn_far, dn, load.at[1]),
    ]

    def others_loads():
        for to in order[2:]:
            for copy in row_loads(to):
                copy.start()
        for copy in loads:
            copy.start()

    row[...] = jnp.zeros_like(row)

    def block(to, first=False):
        at = pl.ds(pl.multiple_of(to * rows, rows), rows)
        for copy in row_loads(to):
            copy.wait()

        def columns(number, carry):
            if first:
                weight_load(number).wait()
            span = pl.ds(pl.multiple_of(number * step, step), step)
            value = dot_nt(dgate[at, :], gu[span, pl.ds(0, units)])
            value += dot_nt(dup[at, :], gu[span, pl.ds(units, units)])
            part[to, :, span] = value.astype(BF)
            return carry

        lax.fori_loop(0, width // step, columns, 0)

    def forward(to, carry):
        at = pl.ds(pl.multiple_of(to * rows, rows), rows)

        def columns(number, carry):
            span = pl.ds(pl.multiple_of(number * step, step), step)
            part_y[to, :, span] = dot_nt(hidden[at, :], dn[span, :]).astype(BF)
            return carry

        return lax.fori_loop(0, width // step, columns, carry)

    def finish(at, total):
        back, dg = norm_back(x2[at], gain[...], total)
        value = cot[at].astype(F32) + back
        dx2[at] = value
        own[at] = value.astype(BF)
        row[...] += dg

    start, relay, lower, upper = scatter_parts(n, part, slots, stage, send, recv, finish, True)
    send_on, pass_on, end = gather_parts(n, own, dz, asend, arecv, local)
    if n == 4:
        block(corner, True)
        start(0, 1)
        others_loads()
        block(across)
        block(along)
        start(3)
        relay()
        block(me)
    else:
        block(order[0], True)
        others_loads()
        for to in order[1:]:
            block(to)
        start()
    for copy in loads:
        copy.wait()
    lax.fori_loop(0, n // 4, forward, 0)
    lower()
    send_on(0)
    upper()
    send_on(1)
    spread_rows(row[...], dgain)
    pass_on()
    lax.fori_loop(n // 4, n, forward, 0)
    end()


def attend_back(n, q_ref, qraw_ref, k_ref, kt_ref, v_ref, kraw_ref, dz_ref, wo_ref, lse_ref, low_ref, high_ref, cq_ref, sq_ref, ck_ref, sk_ref, gq_ref, gk_ref, attn_ref, part, x2, dq_ref, dk_ref, dv_ref, dgq_ref, dgk_ref, out, grads, dk_sum, dv_sum, slots, stage, send, recv, wo_sum, both, got, done, tsend, trecv, put):
    kv, block = pl.program_id(0), pl.program_id(1)
    keys = k_ref.shape[0]
    ratio = q_ref.shape[1] // 128
    scale = 128 ** (-0.5)

    def finish(at, total):
        out[at] = (x2[at] + total).astype(BF)

    start, relay, lower, upper = scatter_parts(n, part, slots, stage, send, recv, finish)
    core = lax.rem(lax.axis_index("fsdp"), 2)
    twin = lax.axis_index("fsdp") + 1 - 2 * core
    kheads, pieces, depth = both.shape[0], both.shape[1], both.shape[3]

    def move(number):
        return remote(
            both.at[number, :, 1 - core], got.at[number], tsend.at[number], trecv.at[number], "fsdp", twin
        )

    steps = pl.num_programs(0) * pl.num_programs(1)
    step = kv * pl.num_programs(1) + block

    @pl.when(step == 0)
    def _():
        greet(ring_places(n) + [("fsdp", twin)])
        start()
        dgq_ref[...] = jnp.zeros_like(dgq_ref)
        dgk_ref[...] = jnp.zeros_like(dgk_ref)

    @pl.when(step == steps * 3 // 8)
    def _():
        relay()

    @pl.when(block == 0)
    def _():
        dk_sum[...] = jnp.zeros_like(dk_sum)
        dv_sum[...] = jnp.zeros_like(dv_sum)
        wo_sum[...] = jnp.zeros_like(wo_sum)

    bias = bias_of(low_ref, high_ref, keys)
    dattn = dot_nt(dz_ref[...], wo_ref[...]).astype(BF)

    def prep_back(grad, raw, gain, cos, sin):
        du = grad * cos - pltpu.roll(grad, 64, 1) * sin
        return norm_back(raw, gain, du)

    for r in range(ratio):
        span = slice(r * 128, r * 128 + 128)
        qh, dah = q_ref[:, span], dattn[:, span]
        lse = lse_ref[pl.ds(kv * ratio + r, 1), :]
        scores = dot_nt(k_ref[...], qh) * (scale * log2e) + bias
        probs = jnp.exp2(scores - lse)
        dprobs = dot_nt(v_ref[...], dah)
        delta = jnp.sum(probs * dprobs, axis=0, keepdims=True)
        ds = (probs * (dprobs - delta)).astype(BF)
        dv_sum[...] += dot(probs.astype(BF), dah)
        dk_sum[...] += dot(ds, qh)
        dqr = dot(kt_ref[...], ds).T * scale
        back, dg = prep_back(dqr, qraw_ref[:, span], gq_ref[...], cq_ref[...], sq_ref[...])
        dq_ref[:, span] = back.astype(BF)
        dgq_ref[0:1] += dg

    wo_sum[...] += dot_tn(attn_ref[...], dz_ref[...])

    @pl.when(block == pl.num_programs(1) - 1)
    def _():
        both[kv] = wo_sum[...].astype(BF).reshape(both.shape[1:])
        move(kv).start()
        dv_ref[...] = dv_sum[...].astype(BF)
        back, dg = prep_back(
            dk_sum[...] * scale, kraw_ref[...], gk_ref[...], ck_ref[...], sk_ref[...]
        )
        dk_ref[...] = back.astype(BF)
        dgk_ref[0:1] += dg

    @pl.when(step == steps - 1)
    def _():
        cw = grads.shape[2]
        writes = []
        for number in range(kheads):
            move(number).wait_recv()
            value = both[number, :, core].astype(F32) + got[number].astype(F32)
            done[number] = value.astype(BF).reshape(done.shape[1:])
            for i in range(done.shape[2] // cw):
                rows = pl.ds(number * pieces * depth, pieces * depth)
                writes.append(
                    pltpu.make_async_copy(
                        done.at[number, :, pl.ds(i * cw, cw)],
                        grads.at[n + i, rows],
                        put.at[number, i],
                    )
                )
        for copy in writes:
            copy.start()
        lower()
        upper()
        for copy in writes:
            copy.wait()
        for number in range(kheads):
            move(number).wait_send()


def gradient(n, counts, kept, flipped, beside, *refs):
    a_ref, bs = refs[0], refs[1 : 1 + len(counts)]
    refs = refs[1 + len(counts) + kept :]
    if beside:
        given, out_ref, taken, both, got, send, recv, esend, erecv, local = refs[:10]
        refs = refs[10:]
    else:
        out_ref, both, got, send, recv = refs[:5]
        refs = refs[5:]
    turned = a_ref if flipped else refs[0]
    step = pl.program_id(0)
    tiles = sum(counts)
    core = lax.rem(lax.axis_index("fsdp"), 2)
    twin = lax.axis_index("fsdp") + 1 - 2 * core
    blocks, depth, tile = both.shape[1], both.shape[3], both.shape[4]
    piece = min(1024, turned.shape[0])
    part = piece // (2 * depth)

    def move(number):
        slot = lax.rem(number, 2)
        return remote(
            both.at[slot, :, 1 - core], got.at[number], send.at[number], recv.at[number], "fsdp", twin
        )

    @pl.when(step == 0)
    def _():
        greet([("fsdp", twin)] + (others("seq", n) if beside else []))
        if beside:
            for copy in exchange_copies(n, [given], [taken], esend, erecv, local):
                copy.start()
        if not flipped:
            turned[...] = a_ref[...].T

    begin = 0
    for b_ref, count in zip(bs, counts):

        @pl.when((step >= begin) & (step < begin + count))
        def _(b_ref=b_ref):
            slot = lax.rem(step, 2)

            @pl.when(step >= 2)
            def _():
                move(step - 2).wait_send()

            for i in range(turned.shape[0] // piece):
                rows = dot(turned[i * piece : i * piece + piece, :], b_ref[...]).astype(BF)
                both[slot, i * part : i * part + part] = rows.reshape(part, 2, depth, tile)
            move(step).start()

        begin += count

    @pl.when(step >= 1)
    def _():
        last = step - 1
        move(last).wait_recv()
        lead = out_ref.shape[0]
        inner = blocks // lead
        for i in range(lead):
            own = both[lax.rem(last, 2), i * inner : i * inner + inner, core]
            other = got[last, i * inner : i * inner + inner]
            total = (own.astype(F32) + other.astype(F32)).astype(BF)
            out_ref[i] = total.reshape(inner * depth, tile)

    @pl.when(step == tiles)
    def _():
        if tiles >= 2:
            move(tiles - 2).wait_send()
        move(tiles - 1).wait_send()
        if beside:
            for copy in exchange_copies(n, [given], [taken], esend, erecv, local):
                copy.wait()


def exchange_copies(n, ins, outs, send, recv, local):
    me = lax.axis_index("seq")
    copies = []
    for i, (source, out) in enumerate(zip(ins, outs)):
        for j in range(1, n):
            to = lax.rem(me + j, n)
            k = i * (n - 1) + j - 1
            copies.append(
                remote(source.at[to], out.at[me], send.at[k], recv.at[k], "seq", to)
            )
        copies.append(pltpu.make_async_copy(source.at[me], out.at[me], local.at[i]))
    return copies


def exchange(n, source, out, send, recv, local):
    greet(others("seq", n))
    copies = exchange_copies(n, [source], [out], send, recv, local)
    for copy in copies:
        copy.start()
    for copy in copies:
        copy.wait()


def write_out(nf, own_gain, own_head, y, dx, gains, att, o, gu, dn, out, dx_out, g_one, q_out, k_out, v_out, g_q, g_k, o_out, g_two, gate_out, up_out, down_out):
    out[...] = y[...]
    dx_out[...] = dx[...]
    qw, kw = q_out.shape[1], k_out.shape[1]
    q_out[...] = att[0, :, :qw].astype(F32)
    k_out[...] = att[0, :, qw : qw + kw].astype(F32)
    v_out[...] = att[0, :, qw + kw :].astype(F32)
    o_out[...] = o[0].astype(F32)
    units = gate_out.shape[1]
    gate_out[...] = gu[0, :, :units].astype(F32)
    up_out[...] = gu[0, :, units:].astype(F32)
    down_out[...] = dn[0].astype(F32)

    @pl.when(pl.program_id(0) == 0)
    def _():
        spot = lax.axis_index("fsdp")
        owner = lax.axis_index("seq") * nf + spot
        begin = lax.rem(spot, 128 // own_gain) * own_gain
        wide = pltpu.roll(gains[...], lax.rem(128 - begin, 128), 1)
        g_one[...] = wide[0:1, :own_gain]
        g_two[...] = wide[1:2, :own_gain]
        heads = pltpu.roll(gains[...], lax.rem(128 - owner * own_head, 128), 1)
        g_q[...] = heads[2:3, :own_head]
        g_k[...] = heads[3:4, :own_head]


def last_stage(n, nf, dq, dk, dv, w, x, dx2, gain, gu, two, gq, gk, out, gu_out, gains, part, slots, stage, send, recv, row, small, wide, mid, seen, esend, erecv, local, gsend, grecv):
    me, spot = lax.axis_index("seq"), lax.axis_index("fsdp")
    greet(others("seq", n) + others("fsdp", nf))
    row[...] = jnp.zeros_like(row)
    rows, width = x.shape
    qw, kw = dq.shape[1], dk.shape[1]
    step = 512

    def block(to):
        at = pl.ds(pl.multiple_of(to * rows, rows), rows)

        def columns(number, carry):
            span = pl.ds(pl.multiple_of(number * step, step), step)
            value = dot_nt(dq[at, :], w[span, pl.ds(0, qw)])
            value += dot_nt(dk[at, :], w[span, pl.ds(qw, kw)])
            value += dot_nt(dv[at, :], w[span, pl.ds(qw + kw, kw)])
            part[to, :, span] = value.astype(BF)
            return carry

        lax.fori_loop(0, width // step, columns, 0)

    def finish(at, total):
        back, dg = norm_back(x[at].astype(F32), gain[...], total)
        out[at] = (dx2[at] + back).astype(BF)
        row[...] += dg

    start, relay, lower, upper = scatter_parts(n, part, slots, stage, send, recv, finish)
    exchanges = exchange_copies(n, [gu], [gu_out], esend, erecv, local)
    if n == 4:
        across, along, corner = square(me)
        block(corner)
        start(0, 1)
        block(across)
        start(2)
        block(along)
        start(3)
        relay()
        for copy in exchanges:
            copy.start()
        block(me)
    else:
        for j in range(n):
            block(lax.rem(me + j, n))
        start()
        for copy in exchanges:
            copy.start()
    lower()
    upper()
    small[...] = jnp.zeros_like(small)
    per = 128 * n * nf // width
    one = row[...]
    for f in range(nf):
        for seq in range(n):
            line = (seq * nf + f) // per
            small[f, seq, 0:1] = one[:, line * 128 : line * 128 + 128]
            small[f, seq, 1:2] = two[line : line + 1]
            small[f, seq, 2:3] = gq[0:1]
            small[f, seq, 3:4] = gk[0:1]
    far = []
    for j in range(1, nf):
        to = lax.rem(spot + j, nf)
        far.append(
            remote(small.at[to], wide.at[j - 1], gsend.at[j - 1], grecv.at[j - 1], "fsdp", to)
        )
    for copy in far:
        copy.start()
    for copy in far:
        copy.wait_recv()
    total = small[spot]
    for j in range(nf - 1):
        total += wide[j]
    mid[...] = total
    near = []
    for j in range(1, n):
        to = lax.rem(me + j, n)
        k = nf + j - 2
        near.append(remote(mid.at[to], seen.at[j - 1], gsend.at[k], grecv.at[k], "seq", to))
    for copy in near:
        copy.start()
    for copy in near:
        copy.wait_recv()
    result = mid[me]
    for j in range(n - 1):
        result += seen[j]
    gains[...] = result
    for copy in far + near:
        copy.wait_send()
    for copy in exchanges:
        copy.wait()


def after(value, done):
    return lax.optimization_barrier((value, done))[0]


def dma(count):
    return pltpu.SemaphoreType.DMA((count,))


def shards(
    n,
    nf,
    tokens,
    seq_lengths,
    pic_starts,
    pic_lengths,
    norm1_gain,
    w_query,
    w_key,
    w_value,
    q_gain,
    k_gain,
    w_out,
    norm2_gain,
    w_gate,
    w_up,
    w_down,
    cotangent,
):
    rows, width = tokens.shape
    group = rows * n
    depth = w_query.shape[0]
    head = q_gain.shape[0] * n * nf
    qw, kw = w_query.shape[1] // n, w_key.shape[1] // n
    cw = qw + 2 * kw
    fw = w_gate.shape[1] // n
    qheads, kheads = qw // head, kw // head
    ratio = qheads // kheads
    own_gain = norm1_gain.shape[0]
    own_head = q_gain.shape[0]

    entries = []
    for gain in (norm1_gain, norm2_gain, q_gain, k_gain):
        entries += [gain, jnp.zeros((128 - gain.shape[0],), BF)]
    packed = jnp.concatenate(entries)[None, :]

    gather_sems = [dma(gather_copies(n)), dma(gather_copies(n)), pltpu.SemaphoreType.DMA]
    line = nf == 8
    half = head // 2
    powers = -(np.arange(half, dtype=np.float32) * np.float32(2.0) / np.float32(head))
    freq = np.tile((np.float32(theta) ** powers).astype(np.float32), 2)[None, :]
    small = pl.BlockSpec(memory_space=pltpu.SMEM)
    held = nf if line else 1
    w_att, gu, xg, wo, gain_one, gain_two, gain_q, gain_k, cos, sin, low, high = pl.pallas_call(
        functools.partial(entry_stage, n, nf, line, own_gain, own_head),
        out_shape=(
            shape((n, held, depth, cw), BF),
            shape((n, depth, 2 * fw), BF),
            shape((n, rows, width), BF),
            shape((held, depth, width), BF),
            shape((1, width), F32),
            shape((1, width), F32),
            shape((1, head), F32),
            shape((1, head), F32),
            shape((group, head), F32),
            shape((group, head), F32),
            shape((8, group), jnp.int32),
            shape((8, group), jnp.int32),
        ),
        in_specs=[ANY] * 7 + [VMEM] + [small] * 3 + [VMEM],
        out_specs=(ANY,) * 4 + (VMEM,) * 8,
        scratch_shapes=[
            pltpu.VMEM((8, 128), F32),
            pltpu.VMEM((n, 8, 128), F32),
            pltpu.VMEM((nf, n, 8, 128), F32),
            dma(3 * (n - 1)),
            dma(3 * (n - 1)),
            dma(3),
            dma(2 * (n - 1)),
            dma(2 * (n - 1)),
            dma(2),
        ]
        + gather_sems
        + [
            dma(n + nf - 2),
            dma(n + nf - 2),
            dma(2),
            dma(10),
            dma(10),
            dma(10),
            dma(10),
            pltpu.SemaphoreType.DMA,
        ],
        compiler_params=comm_params(0),
    )(
        w_query, w_key, w_value, w_gate, w_up, tokens, w_out, packed,
        seq_lengths, pic_starts, pic_lengths, jnp.asarray(freq),
    )
    wo = wo.reshape(-1, width)
    w_att = w_att.reshape(n, -1, cw)
    if not line:
        wo = lax.all_gather(wo, "fsdp", axis=0, tiled=True)
        w_att = lax.all_gather(w_att, "fsdp", axis=1, tiled=True)
    w_att = w_att.reshape(width, cw)
    gu = lax.all_gather(gu, "fsdp", axis=1, tiled=True).reshape(width, 2 * fw)

    def whole(dims):
        return pl.BlockSpec(dims, lambda *ids: (0,) * len(dims))

    def by_rows(count, columns):
        return pl.BlockSpec((count, columns), lambda i: (i, 0))

    def by_cols(count, columns):
        return pl.BlockSpec((count, columns), lambda i: (0, i))

    blocks = group // 256
    n1, qraw, kraw, q, k, v, kt, vt, cg = pl.pallas_call(
        functools.partial(project, n),
        grid=(blocks,),
        out_shape=(
            shape((width, group), BF),
            shape((group, qw), F32),
            shape((group, kw), F32),
            shape((group, qw), BF),
            shape((group, kw), BF),
            shape((group, kw), BF),
            shape((kw, group), BF),
            shape((kw, group), BF),
            shape((n, rows, width), BF),
        ),
        in_specs=[
            by_rows(256, width),
            whole((1, width)),
            whole((width, cw)),
            whole((1, head)),
            whole((1, head)),
            by_rows(256, head),
            by_rows(256, head),
            ANY,
        ],
        out_specs=(
            by_cols(width, 256),
            by_rows(256, qw),
            by_rows(256, kw),
            by_rows(256, qw),
            by_rows(256, kw),
            by_rows(256, kw),
            by_cols(kw, 256),
            by_cols(kw, 256),
            ANY,
        ),
        scratch_shapes=gather_sems,
        compiler_params=comm_params(11),
    )(xg.reshape(group, width), gain_one, w_att, gain_q, gain_k, cos, sin, cotangent)

    attn, lse, part_out, cg, dn = pl.pallas_call(
        functools.partial(attend, n),
        grid=(blocks,),
        out_shape=(
            shape((group, qw), BF),
            shape((8, group), F32),
            shape((group, width), BF),
            shape((n, rows, width), BF),
            shape((n, depth, fw), BF),
        ),
        in_specs=[
            by_rows(256, qw),
            whole((group, kw)),
            whole((kw, group)),
            whole((qw, width)),
            by_cols(8, 256),
            by_cols(8, 256),
            ANY,
            ANY,
            ANY,
        ],
        out_specs=(by_rows(256, qw), by_cols(8, 256), by_rows(256, width), ANY, ANY),
        scratch_shapes=[pltpu.VMEM((group, 256), F32)]
        + gather_sems
        + [dma(n - 1), dma(n - 1), dma(1)],
        input_output_aliases={7: 3},
        compiler_params=comm_params(3),
    )(q, k, vt, wo, low, high, cotangent, cg, w_down.T)
    cg = cg.reshape(group, width)
    dn = lax.all_gather(dn, "fsdp", axis=1, tiled=True).reshape(width, fw)

    slots = [
        pltpu.VMEM((scatter_slots(n), rows, width), BF),
        pltpu.VMEM((rows, width), BF),
    ]
    sems = [dma(max(6, n - 1)), dma(max(6, n - 1))]

    x2, n2 = pl.pallas_call(
        functools.partial(middle_stage, n),
        out_shape=(shape((rows, width), F32), shape((n, rows, width), BF)),
        in_specs=[VMEM] * 3,
        out_specs=(VMEM, ANY),
        scratch_shapes=slots + [pltpu.VMEM((rows, width), BF)] + sems + gather_sems,
        compiler_params=comm_params(2),
    )(part_out.reshape(n, rows, width), tokens, gain_two)
    n2 = n2.reshape(group, width)

    tile = 256
    tiles = fw // tile
    cuts = 1
    while 2 * cuts <= tiles:
        cuts *= 2
    gate, up, hidden, n2_turned = pl.pallas_call(
        functools.partial(ffn_forward, cuts),
        grid=(tiles,),
        out_shape=(
            shape((group, fw), F32),
            shape((group, fw), F32),
            shape((group, fw), BF),
            shape((width, group), BF),
        ),
        in_specs=[
            whole((group, width)),
            by_cols(width, tile),
            pl.BlockSpec((width, tile), lambda i: (0, i + tiles)),
        ],
        out_specs=(by_cols(group, tile),) * 3
        + (pl.BlockSpec((width // cuts, group), lambda i: (jnp.minimum(i, cuts - 1), 0)),),
        compiler_params=plain_params(),
    )(n2, gu, gu)

    def product(number, a, *bs, into=None, flipped=False, given=None):
        tile = 512
        while any(b.shape[1] % tile for b in bs):
            tile //= 2
        counts = [b.shape[1] // tile for b in bs]
        begins = [sum(counts[:i]) for i in range(len(bs))]
        tiles = sum(counts)

        def spec(begin, count):
            return pl.BlockSpec(
                (group, tile), lambda i: (0, jnp.clip(i - begin, 0, count - 1))
            )

        dims = (n, width // n // 2, tiles * tile) if into is None else into.shape
        kept = [] if into is None else [into]
        side = [] if given is None else [given]
        blocks = width // (2 * depth)
        outs = [pl.BlockSpec((n, dims[1], tile), lambda i: (0, 0, jnp.maximum(i - 1, 0)))]
        extra = [dma(n - 1), dma(n - 1), dma(1)] if side else []
        result = pl.pallas_call(
            functools.partial(gradient, n, counts, len(kept), flipped, len(side)),
            grid=(tiles + 1,),
            out_shape=(shape(dims, BF),) + tuple(shape(g.shape, BF) for g in side),
            in_specs=[whole(a.shape)]
            + [spec(b, c) for b, c in zip(begins, counts)]
            + [ANY] * len(kept + side),
            out_specs=tuple(outs + [ANY] * len(side)),
            scratch_shapes=[
                pltpu.VMEM((2, blocks, 2, depth, tile), BF),
                pltpu.VMEM((tiles, blocks, depth, tile), BF),
                dma(tiles),
                dma(tiles),
            ]
            + extra
            + ([] if flipped else [pltpu.VMEM((width, group), BF)]),
            input_output_aliases={} if into is None else {1 + len(bs): 0},
            compiler_params=comm_params(number),
        )(a, *bs, *kept, *side)
        return result if side else result[0]

    same_core = [[core + 2 * i for i in range(nf // 2)] for core in range(2)]

    def reduce_rows(grad):
        return lax.psum_scatter(
            grad, "fsdp", scatter_dimension=1, tiled=True, axis_index_groups=same_core
        )

    dn_grad = product(12, cg, hidden)
    dn_share = reduce_rows(dn_grad)

    dgate, dup = pl.pallas_call(
        ffn_back,
        grid=(tiles,),
        out_shape=(shape((group, fw), BF), shape((group, fw), BF)),
        in_specs=[
            whole((group, width)),
            by_cols(width, tile),
            by_cols(group, tile),
            by_cols(group, tile),
        ],
        out_specs=(by_cols(group, tile),) * 2,
        compiler_params=plain_params(),
    )(cg, after(dn, dn_grad), gate, up)

    gu_grad = product(13, n2_turned, dgate, dup, flipped=True)
    gu_share = reduce_rows(gu_grad)

    dx2, dz, dgain_two, part_y = pl.pallas_call(
        functools.partial(back_stage, n),
        out_shape=(
            shape((rows, width), F32),
            shape((n, rows, width), BF),
            shape((width // 128, 128), F32),
            shape((n, rows, width), BF),
        ),
        in_specs=[ANY] * 3 + [VMEM] * 3 + [ANY] * 2,
        out_specs=(VMEM, ANY, VMEM, VMEM),
        scratch_shapes=[pltpu.VMEM((n, rows, width), BF)]
        + slots
        + [pltpu.VMEM((rows, width), BF)]
        + sems
        + gather_sems
        + [
            pltpu.VMEM((1, width), F32),
            pltpu.VMEM((group, fw), BF),
            pltpu.VMEM((width, fw), BF),
            dma(2),
            pltpu.VMEM((group, fw), BF),
            pltpu.VMEM((group, fw), BF),
            pltpu.VMEM((width, 2 * fw), BF),
            pltpu.SemaphoreType.DMA((2, n)),
            dma(width // 512),
        ],
        compiler_params=comm_params(4),
    )(
        after(dgate, gu_grad), dup, gu, x2, cotangent, gain_two, hidden, dn,
    )
    dz = dz.reshape(group, width)

    wide = ratio * head
    dq, dk, dv, dgain_q, dgain_k, branch, wo_grad = pl.pallas_call(
        functools.partial(attend_back, n),
        grid=(kheads, blocks),
        out_shape=(
            shape((group, qw), BF),
            shape((group, kw), BF),
            shape((group, kw), BF),
            shape((8, head), F32),
            shape((8, head), F32),
            shape((rows, width), BF),
            shape((n + width // cw, width // n // 2, cw), BF),
        ),
        in_specs=[
            pl.BlockSpec((256, wide), lambda h, b: (b, h)),
            pl.BlockSpec((256, wide), lambda h, b: (b, h)),
            pl.BlockSpec((group, head), lambda h, b: (0, h)),
            pl.BlockSpec((head, group), lambda h, b: (h, 0)),
            pl.BlockSpec((group, head), lambda h, b: (0, h)),
            pl.BlockSpec((group, head), lambda h, b: (0, h)),
            pl.BlockSpec((256, width), lambda h, b: (b, 0)),
            pl.BlockSpec((wide, width), lambda h, b: (h, 0)),
            pl.BlockSpec((8, 256), lambda h, b: (0, b)),
            pl.BlockSpec((8, 256), lambda h, b: (0, b)),
            pl.BlockSpec((8, 256), lambda h, b: (0, b)),
            pl.BlockSpec((256, head), lambda h, b: (b, 0)),
            pl.BlockSpec((256, head), lambda h, b: (b, 0)),
            whole((group, head)),
            whole((group, head)),
            whole((1, head)),
            whole((1, head)),
            pl.BlockSpec((256, wide), lambda h, b: (b, h)),
            VMEM,
            VMEM,
        ],
        out_specs=(
            pl.BlockSpec((256, wide), lambda h, b: (b, h)),
            pl.BlockSpec((group, head), lambda h, b: (0, h)),
            pl.BlockSpec((group, head), lambda h, b: (0, h)),
            whole((8, head)),
            whole((8, head)),
            VMEM,
            ANY,
        ),
        scratch_shapes=[pltpu.VMEM((group, head), F32), pltpu.VMEM((group, head), F32)]
        + slots
        + sems
        + [
            pltpu.VMEM((wide, width), F32),
            pltpu.VMEM((kheads, wide // (2 * depth), 2, depth, width), BF),
            pltpu.VMEM((kheads, wide // (2 * depth), depth, width), BF),
            pltpu.VMEM((kheads, wide // 2, width), BF),
            dma(kheads),
            dma(kheads),
            pltpu.SemaphoreType.DMA((kheads, width // cw)),
        ],
        compiler_params=comm_params(5),
    )(
        q, qraw, k, kt, v, kraw, dz, wo, lse, low, high, cos, sin, cos, sin, gain_q, gain_k,
        attn, part_y, x2,
    )

    att_grad, dn_mine = product(
        15, n1, dq, dk, dv, into=wo_grad, flipped=True, given=dn_share
    )
    att_share = reduce_rows(after(att_grad, gu_share))

    input_raw, gu_mine, gains = pl.pallas_call(
        functools.partial(last_stage, n, nf),
        out_shape=(
            shape((rows, width), BF),
            shape(gu_share.shape, BF),
            shape((8, 128), F32),
        ),
        in_specs=[VMEM] * 7 + [ANY] + [VMEM] * 3,
        out_specs=(VMEM, ANY, VMEM),
        scratch_shapes=[pltpu.VMEM((n, rows, width), BF)]
        + slots
        + sems
        + [
            pltpu.VMEM((1, width), F32),
            pltpu.VMEM((nf, n, 8, 128), F32),
            pltpu.VMEM((nf - 1, n, 8, 128), F32),
            pltpu.VMEM((n, 8, 128), F32),
            pltpu.VMEM((n - 1, 8, 128), F32),
            dma(n - 1),
            dma(n - 1),
            dma(1),
            dma(n + nf - 2),
            dma(n + nf - 2),
        ],
        compiler_params=comm_params(7),
    )(
        after(dq, att_grad), dk, dv, w_att, tokens, dx2, gain_one, gu_share,
        dgain_two, dgain_q, dgain_k,
    )
    att_mine = pl.pallas_call(
        functools.partial(exchange, n),
        out_shape=shape((n, depth, cw), BF),
        in_specs=[ANY],
        out_specs=ANY,
        scratch_shapes=[dma(n - 1), dma(n - 1), dma(1)],
        compiler_params=comm_params(9),
    )(after(att_share, gains))

    def slab(count):
        return pl.BlockSpec((1, depth, count), lambda i: (i, 0, 0))

    each = width // n
    per = cw // each
    results = pl.pallas_call(
        functools.partial(write_out, nf, own_gain, own_head),
        grid=(n,),
        out_shape=(
            shape((rows, width), BF),
            shape((rows, width), BF),
            shape((1, own_gain), F32),
            shape(w_query.shape, F32),
            shape(w_key.shape, F32),
            shape(w_value.shape, F32),
            shape((1, own_head), F32),
            shape((1, own_head), F32),
            shape(w_out.shape, F32),
            shape((1, own_gain), F32),
            shape(w_gate.shape, F32),
            shape(w_up.shape, F32),
            shape(w_gate.shape, F32),
        ),
        in_specs=[
            by_rows(rows // n, width),
            by_rows(rows // n, width),
            whole((8, 128)),
            slab(cw),
            pl.BlockSpec(
                (1, depth, each), lambda i: (n + lax.div(i, per), 0, lax.rem(i, per))
            ),
            slab(2 * fw),
            slab(fw),
        ],
        out_specs=(
            by_rows(rows // n, width),
            by_rows(rows // n, width),
            whole((1, own_gain)),
            by_cols(depth, qw),
            by_cols(depth, kw),
            by_cols(depth, kw),
            whole((1, own_head)),
            whole((1, own_head)),
            by_cols(depth, each),
            whole((1, own_gain)),
            by_cols(depth, fw),
            by_cols(depth, fw),
            by_cols(depth, fw),
        ),
        compiler_params=plain_params(),
    )(branch, input_raw, gains, att_mine, att_share, gu_mine, dn_mine)
    flat = [r.reshape(-1) if i in (2, 6, 7, 9) else r for i, r in enumerate(results)]
    return tuple(flat[:-1]) + (flat[-1].T,)


def solution(mesh):
    return jax.shard_map(
        functools.partial(shards, mesh.shape["seq"], mesh.shape["fsdp"]),
        mesh=mesh,
        in_specs=(
            P(("fsdp", "seq"), None),
            P("fsdp", None),
            P("fsdp", None),
            P("fsdp", None),
            P(("seq", "fsdp")),
            P(("seq", "fsdp"), None),
            P(("seq", "fsdp"), None),
            P(("seq", "fsdp"), None),
            P(("seq", "fsdp")),
            P(("seq", "fsdp")),
            P(("seq", "fsdp"), None),
            P(("seq", "fsdp")),
            P(("seq", "fsdp"), None),
            P(("seq", "fsdp"), None),
            P(None, ("seq", "fsdp")),
            P(("fsdp", "seq"), None),
        ),
        out_specs=(
            P(("fsdp", "seq"), None),
            P(("fsdp", "seq"), None),
            P(("seq", "fsdp")),
            P(("seq", "fsdp"), None),
            P(("seq", "fsdp"), None),
            P(("seq", "fsdp"), None),
            P(("seq", "fsdp")),
            P(("seq", "fsdp")),
            P(("seq", "fsdp"), None),
            P(("seq", "fsdp")),
            P(("seq", "fsdp"), None),
            P(("seq", "fsdp"), None),
            P(None, ("seq", "fsdp")),
        ),
        check_vma=False,
    )
```
